32 devices in a mesh: dp: 8 (over z, core), mp: 4 (over y, x).
Axes of the slice: x: 2, y: 2, z: 4, core: 2. Of those that a mesh axis runs over, the one named last changes fastest.
Arguments:
- tokens: bfloat16 [4, 10240, 1024], P(None, ('dp', 'mp')), may hold values from -6 to 6
- cotangent: bfloat16 [4, 10240, 1024], P(None, ('dp', 'mp')), may hold values from -6 to 6
- qkv_weight: bfloat16 [1024, 3072], P(None, 'mp'), may hold values from -0.1875 to 0.1875
- out_weight: bfloat16 [1024, 1024], P('mp'), may hold values from -1.5 to 1.5
- up_weight: bfloat16 [1024, 4096], P(None, 'mp'), may hold values from -0.1875 to 0.1875
- down_weight: bfloat16 [4096, 1024], P('mp'), may hold values from -0.25 to 0.25
- ada_weight: bfloat16 [1024, 6144], P(None, 'mp'), may hold values from -0.1875 to 0.1875
- ada_bias: bfloat16 [6144], P('mp'), may hold values from -2 to 2
- rel_bias: float32 [16, 39], P('mp'), may hold values from -3 to 3
- class_table: float32 [101, 1024], replicated, may hold values from -5 to 5
- lengths: int32 [4, 32], P(None, 'dp'), may hold values from 2 to 5, as said below
- timesteps: int32 [4, 32], P(None, 'dp'), may hold values from 0 to 999
- classes: int32 [4, 32], P(None, 'dp'), may hold values from 0 to 100
Outputs:
- output: bfloat16 [4, 10240, 1024], P(None, ('dp', 'mp'))
- tokens_grad: bfloat16 [4, 10240, 1024], P(None, ('dp', 'mp'))
- qkv_grad: float32 [1024, 3072], P(None, 'mp')
- out_grad: float32 [1024, 1024], P('mp')
- up_grad: float32 [1024, 4096], P(None, 'mp')
- down_grad: float32 [4096, 1024], P('mp')
- ada_grad: float32 [1024, 6144], P(None, 'mp')
- ada_bias_grad: float32 [6144], P('mp')
- rel_grad: float32 [16, 39], P('mp')
- class_grad: float32 [101, 1024], replicated
The draws below stay inside these ranges and needn't reach their ends.
Inputs may be any that keep to these rules, and one draw needn't show every extreme that they name: `lengths`: keys in frames at or after a window's length are masked; each micro-batch has a window of all 5 frames.
All inputs are finite; a program needn't handle non-finite values.
Results may differ from the reference program's by a relative error of at most 0.022.
The reference program's roundings to bfloat16 on the way count: a program that leaves them out, or rounds other values in their place, can miss the bound.
Values may be sent and summed in bfloat16 or wider, within the bound.
No kernel may reach another device: no remote copies, remote signals or barrier semaphores. Data moves between devices by JAX's collectives and lax.ppermute only.
A program may use at most 384 MiB of HBM per device.

```python
import math
from functools import partial
import jax
import jax.numpy as jnp
from jax import lax

D = 1024
HEADS = 16
HD = 64
FF = 4096
CLASSES = 101
WT = 5
WH = 8
WW = 8
MB = 4
WIN_DEV = 4
WIN_TOK = 320
WINDOWS = 32
TOKENS = 10240
N_DP = 8


def draw_lengths(key, part):
    key = jax.random.fold_in(key, 11)
    frames_drawn = jax.random.randint(key, (MB, WINDOWS), 2, WT + 1)
    place_full = jax.random.randint(jax.random.fold_in(key, 1), (MB,), 0, WINDOWS)
    full_hit = jnp.arange(WINDOWS)[None, :] == place_full[:, None]
    return jnp.where(full_hit, WT, frames_drawn).astype(jnp.int32)


def touch_ends(values, rng, low, high):
    longest = values.shape.index(max(values.shape))
    spots = []
    for shift in (0, 1):
        where = [jax.random.randint(jax.random.fold_in(rng, axis), (), 0, length) for axis, length in enumerate(values.shape)]
        where[longest] = (where[longest] + shift) % values.shape[longest]
        spots.append(tuple(where))
    return values.at[spots[0]].set(low).at[spots[1]].set(high)


def spiked(array, stream_key, source, target, blocks, factor):
    owner, partner = [(jnp.arange(array.shape[position]) // (array.shape[position] // blocks)).reshape([-1 if axis == position else 1 for axis in range(array.ndim)]) for position in (source, target)]
    chosen = jax.random.permutation(stream_key, blocks)[partner]
    strong = (owner == chosen) | (owner == (partner + blocks // 2) % blocks)
    return jnp.where(strong, factor * array, array)


def levels(rng, extent, pieces, least, top_value):
    level = 1.0
    for dim, shards_of in pieces:
        heights = jax.random.uniform(jax.random.fold_in(jax.random.fold_in(rng, 6), dim), (shards_of,), jnp.float32, least / len(pieces), top_value / len(pieces))
        level = level * jnp.repeat(jnp.exp(heights), extent[dim] // shards_of).reshape((-1,) + (1,) * (len(extent) - 1 - dim))
    return level


def scatter_about(stream_key, dims, deviation, most, shards=(), kind=jnp.bfloat16):
    drawn = deviation * jax.random.normal(stream_key, dims, jnp.float32)
    if shards:
        drawn = drawn * levels(stream_key, dims, shards, -0.22, 0.18)
    return jnp.clip(drawn, -most, most).astype(kind)


def heavy_noise(key, extent, width, limit, cuts, heavy, held_as=jnp.bfloat16):
    drawn = width * jax.random.normal(key, extent, jnp.float32)
    if cuts:
        drawn = drawn * levels(key, extent, cuts, -0.22, 0.18)
    return jnp.clip(spiked(drawn, jax.random.fold_in(key, 3), *heavy), -limit, limit).astype(held_as)


def setup_inputs(seed: int = 0) -> dict:
    key_list = jax.random.split(jax.random.key(seed), 14)
    return {
        "tokens": scatter_about(key_list[0], (MB, TOKENS, D), 1.0, 6.0, ((1, 32),)),
        "cotangent": scatter_about(key_list[1], (MB, TOKENS, D), 1.0, 6.0, ((1, 32),)),
        "qkv_weight": scatter_about(key_list[2], (D, 3 * D), D ** -0.5, 0.1875, ((1, 4),)),
        "out_weight": scatter_about(key_list[3], (D, D), (D // 64) ** -0.5, 1.5, ((0, 4),)),
        "up_weight": scatter_about(key_list[4], (D, FF), D ** -0.5, 0.1875, ((1, 4),)),
        "down_weight": heavy_noise(key_list[5], (FF, D), (FF // 4) ** -0.5, 0.25, ((0, 4),), (0, 1, 4, 2.0)),
        "ada_weight": scatter_about(key_list[6], (D, 6 * D), D ** -0.5, 0.1875, ((1, 4),)),
        "ada_bias": scatter_about(key_list[7], (6 * D,), 0.3, 2.0, ((0, 4),)),
        "rel_bias": scatter_about(key_list[8], (HEADS, 2 * WT + 2 * WH + 2 * WW - 3), 0.5, 3.0, ((0, 4),), jnp.float32),
        "class_table": scatter_about(key_list[9], (CLASSES, D), 1.0, 5.0, (), jnp.float32),
        "lengths": draw_lengths(jax.random.fold_in(key_list[13], 71), 0),
        "timesteps": touch_ends(jax.random.randint(key_list[11], (MB, WINDOWS), 0, 1000), jax.random.fold_in(key_list[11], 1), 0, 999).astype(jnp.int32),
        "classes": touch_ends(jax.random.randint(key_list[12], (MB, WINDOWS), 0, CLASSES), jax.random.fold_in(key_list[12], 1), 0, CLASSES - 1).astype(jnp.int32),
    }


EPS = 1e-06
precise = lax.Precision.HIGHEST

@jax.custom_vjp
def low(v):
    return lax.optimization_barrier(v.astype(jnp.bfloat16)).astype(jnp.float32)

@jax.custom_vjp
def low_back(v):
    return v

def low_keep(v):
    return (low(v), None)

def low_pass(kept, grad):
    return (grad,)

def back_keep(v):
    return (v, None)

def back_low(kept, grad):
    return (low(grad),)
low.defvjp(low_keep, low_pass)
low_back.defvjp(back_keep, back_low)

def round_both(values):
    return low_back(low(values))

def layer_norm(values):
    center = values - lax.optimization_barrier(jnp.mean(values, axis=-1, keepdims=True))
    spread = lax.optimization_barrier(jnp.mean(center * center, axis=-1, keepdims=True))
    return center * lax.rsqrt(spread + EPS)

def modulate(values, shift, scale):
    return layer_norm(values) * (1.0 + scale) + shift

def gelu_tanh(values):
    return 0.5 * values * (1.0 + jnp.tanh(math.sqrt(2.0 / math.pi) * (values + 0.044715 * values * values * values)))

def silu_plain(values):
    return values / (1.0 + jnp.exp(-values))

def condition(timesteps, classes, class_table):
    half_width = class_table.shape[1] // 2
    frequency = jnp.exp(-math.log(10000.0) * jnp.arange(half_width).astype(class_table.dtype) / half_width)
    phase_angle = timesteps.astype(class_table.dtype)[..., None] * frequency
    sinusoid = jnp.concatenate([jnp.cos(phase_angle), jnp.sin(phase_angle)], axis=-1)
    onehot = (classes[..., None] == jnp.arange(class_table.shape[0])[None, None, :]).astype(class_table.dtype)
    lookup = jnp.einsum('mwc,cd->mwd', onehot, class_table, precision=precise)
    return silu_plain(sinusoid + lookup)

def axis_table(rel_part, window_span):
    places = jnp.arange(window_span)
    offsets = places[:, None] - places[None, :] + window_span - 1
    onehot = (offsets[:, :, None] == jnp.arange(2 * window_span - 1)[None, None, :]).astype(rel_part.dtype)
    return jnp.einsum('hr,abr->hab', rel_part, onehot, precision=precise)

def window_bias(rel_bias):
    frame_part = axis_table(rel_bias[:, :2 * WT - 1], WT)
    row_part = axis_table(rel_bias[:, 2 * WT - 1:2 * WT + 2 * WH - 2], WH)
    column_part = axis_table(rel_bias[:, 2 * WT + 2 * WH - 2:], WW)
    full_bias = frame_part[:, :, None, None, :, None, None] + row_part[:, None, :, None, None, :, None] + column_part[:, None, None, :, None, None, :]
    return full_bias.reshape(rel_bias.shape[0], WIN_TOK, WIN_TOK)

def attend(bias_full, block_in):
    packed, masks = block_in
    query_part = packed[:, :, :, 0]
    key_part = packed[:, :, :, 1]
    value_part = packed[:, :, :, 2]
    scores = low_back(jnp.einsum('wqhd,wkhd->whqk', query_part, key_part, precision=precise)) * HD ** (-0.5) + bias_full[None]
    scores = jnp.where(masks[:, None, None, :], scores, -1e+30)
    top_score = lax.optimization_barrier(jnp.max(scores, axis=-1, keepdims=True))
    expo = jnp.exp(scores - top_score)
    probs = expo / lax.optimization_barrier(jnp.sum(expo, axis=-1, keepdims=True))
    return jnp.einsum('whqk,wkhd->wqhd', low(probs), value_part, precision=precise)

def forward(tokens, qkv_weight, out_weight, up_weight, down_weight, ada_weight, ada_bias, rel_bias, class_table, lengths, timesteps, classes):
    bias_full = window_bias(rel_bias)
    frame_of = jnp.arange(WIN_TOK) // (WH * WW)
    cond_all = low(condition(timesteps, classes, class_table))
    results = []
    for micro_step in range(MB):
        modes = low_back(jnp.dot(cond_all[micro_step], ada_weight, precision=precise)) + ada_bias
        modes = jnp.repeat(modes, WIN_TOK, axis=0)
        shift_attn, scale_attn, gate_attn, shift_mlp, scale_mlp, gate_mlp = jnp.split(modes, 6, axis=1)
        inputs = tokens[micro_step]
        normed_one = low(modulate(inputs, shift_attn, scale_attn))
        packed = round_both(jnp.dot(normed_one, qkv_weight, precision=precise))
        packed = packed.reshape(N_DP, WIN_DEV, WIN_TOK, HEADS, 3, HD)
        masks = (frame_of[None, :] < lengths[micro_step][:, None]).reshape(N_DP, WIN_DEV, WIN_TOK)
        mixed = lax.map(jax.checkpoint(partial(attend, bias_full)), (packed, masks))
        heads_out = round_both(mixed.reshape(TOKENS, D))
        attn_out = low_back(jnp.dot(heads_out, out_weight, precision=precise))
        middle = inputs + gate_attn * attn_out
        normed_two = low(modulate(middle, shift_mlp, scale_mlp))
        hidden_pre = low_back(jnp.dot(normed_two, up_weight, precision=precise))
        hidden = low(gelu_tanh(hidden_pre))
        mlp_out = low_back(jnp.dot(hidden, down_weight, precision=precise))
        results.append(middle + gate_mlp * mlp_out)
    return jnp.stack(results)

def reference(tokens, cotangent, qkv_weight, out_weight, up_weight, down_weight, ada_weight, ada_bias, rel_bias, class_table, lengths, timesteps, classes):
    floats = [array_in.astype(jnp.float32) for array_in in (tokens, qkv_weight, out_weight, up_weight, down_weight, ada_weight, ada_bias, rel_bias, class_table)]

    def apply_layer(*params):
        return forward(*params, lengths, timesteps, classes)
    result, pull_back = jax.vjp(apply_layer, *floats)
    grads = pull_back(cotangent.astype(jnp.float32))
    return (result.astype(jnp.bfloat16), grads[0].astype(jnp.bfloat16), grads[1], grads[2], grads[3], grads[4], grads[5], grads[6], grads[7], grads[8])
```

```python
from functools import partial
import math

import jax
import jax.numpy as jnp
import numpy as np
from jax import lax
from jax.experimental import pallas as pl
from jax.experimental.pallas import tpu as pltpu
from jax.sharding import PartitionSpec as P

HD = 64
WT = 5
WH = 8
WW = 8
WIN = 320
D = 1024
EPS = 1e-06
NOFF = WT + WH + WW
C0 = math.sqrt(2.0 / math.pi)
C1 = 0.044715
precise = lax.Precision.HIGHEST
f32 = jnp.float32
bf16 = jnp.bfloat16
NN = (((1,), (0,)), ((), ()))
NT = (((1,), (1,)), ((), ()))
TN = (((0,), (0,)), ((), ()))
HALF = 512
QKV = 384


def mm(a, b, dims=NN):
    return lax.dot_general(a, b, dims, preferred_element_type=f32)


def whole(*dims):
    return pl.BlockSpec(dims, lambda i, *_: (0,) * len(dims))


def part(index, *dims):
    return pl.BlockSpec(dims, lambda i, *_: index)


def rows_of(width):
    return pl.BlockSpec((WIN, width), lambda i, *_: (i, 0))


def window_of(*dims):
    return pl.BlockSpec((None,) + dims, lambda i, *_: (i,) + (0,) * len(dims))


def shape(dims, dtype):
    return jax.ShapeDtypeStruct(dims, dtype)


def run(kernel, name, grid, ins, outs, scratch=(), after=(), scalars=(), flops=0, moved=0):
    first = len(scalars) + len(ins)

    def body(*refs):
        kernel(*refs[:first], *refs[first + len(after) :])

    hbm = pl.BlockSpec(memory_space=pl.ANY)
    return pl.pallas_call(
        body,
        grid_spec=pltpu.PrefetchScalarGridSpec(
            num_scalar_prefetch=len(scalars),
            grid=(grid,),
            in_specs=[spec for _, spec in ins] + [hbm] * len(after),
            out_specs=[spec for _, spec in outs],
            scratch_shapes=list(scratch),
        ),
        out_shape=[what for what, _ in outs],
        compiler_params=pltpu.CompilerParams(vmem_limit_bytes=56 * 2**20),
        cost_estimate=pl.CostEstimate(flops=int(flops), bytes_accessed=int(moved), transcendentals=0),
        name=name,
    )(*scalars, *[array for array, _ in ins], *after)


def ln_parts(values):
    center = values - jnp.mean(values, axis=-1, keepdims=True)
    rstd = lax.rsqrt(jnp.mean(center * center, axis=-1, keepdims=True) + EPS)
    return center * rstd, rstd


def ln_back(grad, scale, hat, rstd):
    inner = grad * (1.0 + scale)
    mean_one = jnp.mean(inner, axis=-1, keepdims=True)
    mean_two = jnp.mean(inner * hat, axis=-1, keepdims=True)
    return rstd * (inner - mean_one - hat * mean_two)


def attend_kernel(len_ref, x_ref, mode_ref, wa_ref, wb_ref, tbl_ref, e_ref, *rest):
    n1_ref, packed_ref, heads_ref, probs_ref, w_all, kb_all = rest if len(rest) == 6 else (None, *rest)
    w = pl.program_id(0)

    @pl.when(w == 0)
    def _():
        w_all[:QKV] = wa_ref[...]
        w_all[QKV:] = wb_ref[...]
        for p in range(2):
            kb_all[p] = mm(e_ref[...], tbl_ref[p]).astype(bf16)

    if n1_ref is None:
        x = x_ref[...]
    else:
        hat, _ = ln_parts(x_ref[...].astype(f32))
        x = (hat * (1.0 + mode_ref[1:2]) + mode_ref[0:1]).astype(bf16)
        n1_ref[...] = x
    pk = mm(x, w_all[...], NT).astype(bf16)
    packed_ref[...] = pk
    lane = lax.broadcasted_iota(jnp.int32, (WIN, 128), 1)
    low = lane < 64
    frame = lax.broadcasted_iota(jnp.int32, (WIN, 128), 0) // (WH * WW)
    mask_lane = (lane & 63) == 2 * NOFF
    hide = jnp.where(frame < len_ref[w], 0.0, -1e30).astype(bf16)
    for p in range(2):
        q = pk[:, p * QKV : p * QKV + 128]
        k = pk[:, p * QKV + 128 : p * QKV + 256]
        v = pk[:, p * QKV + 256 : p * QKV + 384]
        kb = jnp.where(mask_lane, hide, kb_all[p])
        outs = []
        for i in range(2):
            mine = low if i == 0 else ~low
            s = mm(jnp.where(mine, q, e_ref[...]), jnp.where(mine, k, kb), NT)
            ex = jnp.exp(s - jnp.max(s, axis=1, keepdims=True))
            pr = (ex * (1.0 / jnp.sum(ex, axis=1, keepdims=True))).astype(bf16)
            probs_ref[2 * p + i] = pr
            outs.append(mm(pr, v))
        heads_ref[:, p * 128 : (p + 1) * 128] = jnp.where(low, outs[0], outs[1]).astype(bf16)


def attend(lengths, source, modes, weight, table, query_hot, after=()):
    count = lengths.shape[0]
    rows = count * WIN
    first = source.ndim == 3
    outs = [
        (shape((rows, 2 * QKV), bf16), rows_of(2 * QKV)),
        (shape((rows, 256), bf16), rows_of(256)),
        (shape((count * 4, WIN, WIN), bf16), pl.BlockSpec((4, WIN, WIN), lambda i, l: (i, 0, 0))),
    ]
    if first:
        outs = [(shape((rows, D), bf16), rows_of(D))] + outs
    return run(
        attend_kernel,
        "attend",
        count,
        [
            (source, window_of(WIN, D) if first else rows_of(D)),
            (modes, window_of(6, D)),
            (weight[0], part((0, 0), QKV, D)),
            (weight[1], part((0, 0), QKV, D)),
            (table, whole(2, 128, 128)),
            (query_hot, whole(WIN, 128)),
        ],
        outs,
        [pltpu.VMEM((2 * QKV, D), bf16), pltpu.VMEM((2, WIN, 128), bf16)],
        after,
        [lengths],
        9e9,
        12e6,
    )


def middle_kernel(h0, h1, h2, h3, w0, w1, w2, w3, w4, w5, w6, w7, tok, cot, mode, attn_ref, mid_ref, n2_ref, di_ref, w_all):
    @pl.when(pl.program_id(0) == 0)
    def _():
        for i, ref in enumerate((w0, w1, w2, w3, w4, w5, w6, w7)):
            w_all[i * 128 : (i + 1) * 128] = ref[...]

    heads = jnp.concatenate([h0[...], h1[...], h2[...], h3[...]], axis=1)
    attn = mm(heads, w_all[...])
    attn_ref[...] = attn.astype(bf16)
    middle = tok[...].astype(f32) + mode[2:3] * attn
    mid_ref[...] = middle
    hat, _ = ln_parts(middle)
    n2_ref[...] = (hat * (1.0 + mode[4:5]) + mode[3:4]).astype(bf16)
    di_ref[...] = (mode[5:6] * cot[...].astype(f32)).astype(bf16)


def middle_step(heads, weights, tokens, cotangent, modes, after=()):
    count = tokens.shape[0]
    rows = count * WIN
    return run(
        middle_kernel,
        "middle",
        count,
        [(h, rows_of(256)) for h in heads]
        + [(half, part((3, 0), 128, D)) for pair in weights for half in pair]
        + [(tokens, window_of(WIN, D)), (cotangent, window_of(WIN, D)), (modes, window_of(6, D))],
        [(shape((rows, D), kind), rows_of(D)) for kind in (bf16, f32, bf16, bf16)],
        [pltpu.VMEM((D, D), bf16)],
        after,
        flops=2.7e9,
        moved=22e6,
    )


def feed_kernel(n2_ref, di_ref, up0, dn0, up1, dn1, hid_ref, pre_ref, g0_ref, g1_ref):
    def half_step(up_ref, dn_ref, g_ref):
        up = up_ref[...]
        dn = dn_ref[...]
        v = mm(n2_ref[...], up, NT)
        hg = mm(di_ref[...], dn, NT)
        v2 = v * v
        t = jnp.tanh(v * (C0 + (C0 * C1) * v2))
        share = 0.5 + 0.5 * t
        hid = (v * share).astype(bf16)
        slope = share + (0.5 * v) * (1.0 - t * t) * (C0 + (3.0 * C0 * C1) * v2)
        pre = (slope * hg).astype(bf16)
        hid_ref[...] = hid
        pre_ref[...] = pre
        g_ref[1] = mm(hid, di_ref[...], TN).astype(bf16)
        g_ref[0] = mm(pre, n2_ref[...], TN).astype(bf16)

    j = pl.program_id(0)

    @pl.when(j == 0)
    def _():
        half_step(up1, dn1, g1_ref)

    @pl.when(j == 1)
    def _():
        half_step(up0, dn0, g0_ref)


def feed(normed, down_in, weight, after=()):
    rows = normed.shape[0]
    ins = [(normed, whole(rows, D)), (down_in, whole(rows, D))]
    for up, down in weight:
        for array, place in (up, down):
            ins.append((array, pl.BlockSpec((None, HALF, D), lambda i, place=place: (place, 0, 0))))
    columns = pl.BlockSpec((rows, HALF), lambda j: (0, 1 - j))
    return run(
        feed_kernel,
        "feed",
        2,
        ins,
        [(shape((rows, 2 * HALF), bf16), columns)] * 2 + [(shape((2, HALF, D), bf16), whole(2, HALF, D))] * 2,
        (),
        after,
        flops=8 * rows * D * 2 * HALF,
        moved=20e6,
    )


def turn_kernel(p0, p1, p2, p3, w0, w1, w2, w3, w4, w5, w6, w7, mid_ref, attn_ref, cot_ref, mode_ref, mg_ref, oi_ref, sum_ref):
    ng = None
    for src, pair in ((p0, (w0, w1)), (p1, (w2, w3)), (p2, (w4, w5)), (p3, (w6, w7))):
        for h in range(2):
            term = mm(src[:, h * HALF : (h + 1) * HALF], pair[h][...])
            ng = term if ng is None else ng + term
    hat, rstd = ln_parts(mid_ref[...])
    mg = cot_ref[...].astype(f32) + ln_back(ng, mode_ref[4:5], hat, rstd)
    mg_ref[...] = mg
    oi_ref[...] = (mode_ref[2:3] * mg).astype(bf16)
    sum_ref[0:1] = jnp.sum(mg * attn_ref[...].astype(f32), axis=0, keepdims=True)
    sum_ref[1:2] = jnp.sum(ng, axis=0, keepdims=True)
    sum_ref[2:3] = jnp.sum(ng * hat, axis=0, keepdims=True)


def out_kernel(p0, p1, p2, p3, w0, w1, w2, w3, w4, w5, w6, w7, mid_ref, cot_ref, mode_ref, out_ref, sum_ref):
    mlp = None
    for src, pair in ((p0, (w0, w1)), (p1, (w2, w3)), (p2, (w4, w5)), (p3, (w6, w7))):
        for h in range(2):
            term = mm(src[:, h * HALF : (h + 1) * HALF], pair[h][...])
            mlp = term if mlp is None else mlp + term
    out_ref[...] = (mid_ref[...] + mode_ref[5:6] * mlp).astype(bf16)
    sum_ref[...] = jnp.sum(cot_ref[...].astype(f32) * mlp, axis=0, keepdims=True)


def of_units(arrays, weights, which):
    ins = [(array, rows_of(2 * HALF)) for array in arrays]
    for pair in weights:
        for half in pair:
            array, place = half[which]
            ins.append((array, pl.BlockSpec((None, HALF, D), lambda i, place=place: (place, 0, 0))))
    return ins


def turn_step(pre, weights, middle, attn_out, cotangent, modes, after=()):
    count = cotangent.shape[0]
    rows = count * WIN
    return run(
        turn_kernel,
        "turn",
        count,
        of_units(pre, weights, 0)
        + [(middle, rows_of(D)), (attn_out, rows_of(D)), (cotangent, window_of(WIN, D)), (modes, window_of(6, D))],
        [
            (shape((rows, D), f32), rows_of(D)),
            (shape((rows, D), bf16), rows_of(D)),
            (shape((count, 3, D), f32), window_of(3, D)),
        ],
        (),
        after,
        flops=10.7e9,
        moved=35e6,
    )


def out_step(hid, weights, middle, cotangent, modes, after=()):
    count = cotangent.shape[0]
    return run(
        out_kernel,
        "output",
        count,
        of_units(hid, weights, 1) + [(middle, rows_of(D)), (cotangent, window_of(WIN, D)), (modes, window_of(6, D))],
        [(shape((count, WIN, D), bf16), window_of(WIN, D)), (shape((count, 1, D), f32), window_of(1, D))],
        (),
        after,
        flops=10.7e9,
        moved=30e6,
    )


def attend_back_kernel(
    oi_ref, o0_ref, o1_ref, pk_ref, pr_ref, e_ref, n1_ref, oi_all, ho_ref, pg_ref, g0_ref, g1_ref, rel_ref, pg_all, t_all, ow
):
    w = pl.program_id(0)

    @pl.when(w == 0)
    def _():
        t_all[...] = jnp.zeros_like(t_all)
        ow[:128] = o0_ref[...]
        ow[128:] = o1_ref[...]

    hg = mm(oi_ref[...], ow[...], NT).astype(bf16)
    pk = pk_ref[...]
    low = lax.broadcasted_iota(jnp.int32, (WIN, 128), 1) < 64
    for p in range(2):
        q = pk[:, p * QKV : p * QKV + 128]
        k = pk[:, p * QKV + 128 : p * QKV + 256]
        v = pk[:, p * QKV + 256 : p * QKV + 384]
        do = hg[:, p * 128 : (p + 1) * 128]
        dv, dq, dk = [], [], []
        for i in range(2):
            mine = low if i == 0 else ~low
            qa = jnp.where(mine, q, e_ref[...])
            dp = mm(jnp.where(mine, do, jnp.zeros_like(do)), v, NT)
            prl = pr_ref[2 * p + i]
            pr = prl.astype(f32)
            t = pr * dp
            ds = (t - pr * jnp.sum(t, axis=1, keepdims=True)).astype(bf16)
            dv.append(mm(prl, do, TN))
            dq.append(mm(ds, k))
            dk.append(mm(ds, qa, TN))
        block = jnp.concatenate(
            [jnp.where(low, dq[0], dq[1]), jnp.where(low, dk[0], dk[1]), jnp.where(low, dv[0], dv[1])], axis=1
        ).astype(bf16)
        pg_ref[:, p * QKV : (p + 1) * QKV] = block
        pg_all[pl.ds(pl.multiple_of(w * WIN, WIN), WIN), p * QKV : (p + 1) * QKV] = block
        t_all[p] += jnp.where(low, dk[1], dk[0])

    @pl.when(w == pl.num_programs(0) - 1)
    def _():
        go = mm(ho_ref[...], oi_all[...], TN).astype(bf16)
        gq = mm(pg_all[...], n1_ref[...], TN).astype(bf16)
        for p, g_ref in enumerate((g0_ref, g1_ref)):
            g_ref[:QKV] = gq[p * QKV : (p + 1) * QKV]
            g_ref[QKV:] = go[p * 128 : (p + 1) * 128]
        hot = e_ref[...].astype(f32)
        for p in range(2):
            sums = lax.dot_general(hot, t_all[p], TN, precision=precise, preferred_element_type=f32)
            rel_ref[p] = sums[:32]


def attend_back(out_in, weight, packed, probs, query_hot, normed, heads, after=()):
    rows = normed.shape[0]
    return run(
        attend_back_kernel,
        "attend_back",
        rows // WIN,
        [
            (out_in, rows_of(D)),
            (weight[0], part((3, 0), 128, D)),
            (weight[1], part((3, 0), 128, D)),
            (packed, rows_of(2 * QKV)),
            (probs, pl.BlockSpec((4, WIN, WIN), lambda i: (i, 0, 0))),
            (query_hot, whole(WIN, 128)),
            (normed, whole(rows, D)),
            (out_in, whole(rows, D)),
            (heads, whole(rows, 256)),
        ],
        [
            (shape((rows, 2 * QKV), bf16), rows_of(2 * QKV)),
            (shape((HALF, D), bf16), whole(HALF, D)),
            (shape((HALF, D), bf16), whole(HALF, D)),
            (shape((2, 32, 128), f32), whole(2, 32, 128)),
        ],
        [pltpu.VMEM((rows, 2 * QKV), bf16), pltpu.VMEM((2, WIN, 128), f32), pltpu.VMEM((256, D), bf16)],
        after,
        flops=13e9,
        moved=20e6,
    )


def last_kernel(p0, p1, p2, p3, w0, w1, w2, w3, w4, w5, w6, w7, tok_ref, mode_ref, mg_ref, out_ref, sum_ref, w_all):
    @pl.when(pl.program_id(0) == 0)
    def _():
        for i, ref in enumerate((w0, w1, w2, w3, w4, w5, w6, w7)):
            w_all[i * QKV : (i + 1) * QKV] = ref[...]

    ng = None
    for i, src in enumerate((p0, p1, p2, p3)):
        term = mm(src[...], w_all[i * 2 * QKV : (i + 1) * 2 * QKV])
        ng = term if ng is None else ng + term
    hat, rstd = ln_parts(tok_ref[...].astype(f32))
    out_ref[...] = (mg_ref[...] + ln_back(ng, mode_ref[1:2], hat, rstd)).astype(bf16)
    sum_ref[0:1] = jnp.sum(ng, axis=0, keepdims=True)
    sum_ref[1:2] = jnp.sum(ng * hat, axis=0, keepdims=True)


def last_step(packed_grads, weights, tokens, modes, middle_grad, after=()):
    count = tokens.shape[0]
    return run(
        last_kernel,
        "last",
        count,
        [(array, rows_of(2 * QKV)) for array in packed_grads]
        + [(half, part((0, 0), QKV, D)) for pair in weights for half in pair]
        + [(tokens, window_of(WIN, D)), (modes, window_of(6, D)), (middle_grad, rows_of(D))],
        [(shape((count, WIN, D), bf16), window_of(WIN, D)), (shape((count, 2, D), f32), window_of(2, D))],
        [pltpu.VMEM((8 * QKV, D), bf16)],
        after,
        flops=8e9,
        moved=24e6,
    )


def silu_plain(values):
    return values / (1.0 + jnp.exp(-values))


def condition(timesteps, classes, class_table):
    half_width = class_table.shape[1] // 2
    frequency = jnp.exp(
        -math.log(10000.0) * jnp.arange(half_width).astype(class_table.dtype) / half_width
    )
    phase_angle = timesteps.astype(class_table.dtype)[..., None] * frequency
    sinusoid = jnp.concatenate([jnp.cos(phase_angle), jnp.sin(phase_angle)], axis=-1)
    onehot = (classes[..., None] == jnp.arange(class_table.shape[0])).astype(class_table.dtype)
    lookup = jnp.einsum("mwc,cd->mwd", onehot, class_table, precision=precise)
    return sinusoid + lookup


SPANS = ((0, 0, WT), (WT, 2 * WT - 1, WH), (WT + WH, 2 * WT + 2 * WH - 2, WW))


def place_hot():
    spot = np.arange(WIN)
    hot = np.zeros((WIN, NOFF), np.float32)
    for (start, _, _), where in zip(SPANS, (spot // (WH * WW), (spot // WW) % WH, spot % WW)):
        hot[spot, start + where] = 1.0
    return hot


def query_side():
    half = np.zeros((WIN, 64), np.float32)
    half[:, :NOFF] = place_hot()
    half[:, NOFF : 2 * NOFF] = place_hot()
    half[:, 2 * NOFF] = 1.0
    return np.concatenate([half, half], axis=1)


def offset_hot(rows, copies):
    hot = np.zeros((2 * NOFF - 3, rows, 64), np.float32)
    for start, begin, length in SPANS:
        for key in range(length):
            for query in range(length):
                for copy in range(copies):
                    hot[begin + query - key + length - 1, start + key, copy * NOFF + start + query] = 1.0
    return hot


def key_tables(rel, core):
    value = jnp.einsum("hr,rkq->hkq", rel.reshape(16, -1), offset_hot(64, 2), precision=precise)
    top = lax.reduce_precision(value, 8, 7)
    value = jnp.where(jnp.arange(64) < NOFF, top, value - top).astype(bf16)
    value = value.reshape(4, 2, 2, 64, 64)
    value = jnp.where(core == 0, value, value[:, ::-1])
    value = jnp.concatenate([value[:, :, 1], value[:, :, 0]], axis=-1)
    return jnp.pad(value, ((0, 0), (0, 0), (0, 64), (0, 0)))


def rel_sums(grids, core):
    grids = jnp.where(core == 0, grids, grids[:, ::-1])
    grids = grids.reshape(4, 2, 32, 2, 64)
    grids = jnp.stack([grids[:, :, :, 1], grids[:, :, :, 0]], axis=2).reshape(16, 32, 64)
    return jnp.einsum("hkq,rkq->hr", grids, offset_hot(32, 1), precision=precise).reshape(4, 4, -1)


def local_windows(
    sizes,
    tokens,
    cotangent,
    qkv_weight,
    out_weight,
    up_weight,
    down_weight,
    ada_weight,
    ada_bias,
    rel_bias,
    class_table,
    lengths,
    timesteps,
    classes,
):
    n_dp, n_mp = sizes
    micro = tokens.shape[0]
    mp = lax.axis_index("mp")
    dp = lax.axis_index("dp")
    core = dp & 1
    z_bits = [1 << b for b in range(1, n_dp.bit_length() - 1)]

    def swap_mp(bit):
        return lambda v: lax.ppermute(v, "mp", [(i, i ^ bit) for i in range(n_mp)])

    def swap_dp(bit):
        return lambda v: lax.ppermute(v, "dp", [(i, i ^ bit) for i in range(n_dp)])

    px, py, pd = swap_mp(1), swap_mp(2), swap_mp(3)
    pc = swap_dp(1)
    by_rel = [lambda v: v, px, py, pd]

    def total(*values):
        return sum(v.astype(f32) for v in values).astype(bf16)

    def cat(a, b, axis=0):
        return jnp.concatenate([a, b], axis=axis)

    def ordered(flag, a, b, axis=0):
        return cat(jnp.where(flag, a, b), jnp.where(flag, b, a), axis)

    def dp_gather(v):
        for bit in (1, *z_bits):
            v = ordered((dp & bit) == 0, v, swap_dp(bit)(v))
        return v

    pre_cond = condition(timesteps, classes, class_table)
    cond_low = silu_plain(pre_cond).astype(bf16)
    mode_cols = jnp.einsum("mwd,de->mwe", cond_low, ada_weight, preferred_element_type=f32) + ada_bias.astype(f32)
    order = jnp.arange(4) ^ mp
    rel_modes = [
        by_rel[r](lax.dynamic_index_in_dim(mode_cols, mp ^ r, axis=1, keepdims=False)) for r in range(4)
    ]
    modes = jnp.take(jnp.stack(rel_modes), order, axis=0)
    modes = modes.transpose(1, 0, 2).reshape(micro, 6, D)
    own_lengths = lax.dynamic_index_in_dim(lengths, mp, axis=1, keepdims=False)

    row = np.arange(2 * QKV)
    src = 2 * ((row // QKV) ^ core) + (row % 128) // 64
    src = src * 192 + ((row % QKV) // 128) * 64 + row % 64
    scale = np.where((row % QKV) < 128, HD**-0.5, 1.0).astype(np.float32)
    qkv_hot = jnp.where(jnp.arange(2 * QKV)[:, None] == src[None, :], scale[None, :], 0.0).astype(bf16)
    unit = np.arange(2 * HALF)
    up_hot = (unit[:, None] == (unit ^ (core * HALF))[None, :]).astype(bf16)
    both = (((0,), (1,)), ((), ()))
    qkv_rows = lax.dot_general(qkv_hot, qkv_weight, both, preferred_element_type=f32).astype(bf16)
    up_rows = lax.dot_general(up_hot, up_weight, both, preferred_element_type=f32).astype(bf16)

    def half_of(v, h):
        size = v.shape[0] // 2
        return lax.dynamic_slice_in_dim(v, (core ^ h) * size, size, 0)

    attn_own = [cat(qkv_rows[h * QKV : (h + 1) * QKV], half_of(out_weight, h)) for h in range(2)]
    feed_own = [jnp.stack([up_rows[h * HALF : (h + 1) * HALF], half_of(down_weight, h)]) for h in range(2)]

    ax, ay = px(attn_own[0]), py(attn_own[0])
    ad = cat(py(ax[: HALF // 2]), px(ay[HALF // 2 :]))
    attn_w = [attn_own] + [[v, pc(v)] for v in (ax, ay, ad)]
    fx, fy = px(feed_own[0]), py(feed_own[0])
    fu, fd = py(fx[:1]), px(fy[1:])
    feed_w = [[((v, 0), (v, 1)) for v in feed_own]]
    feed_w += [[((v, 0), (v, 1)) for v in (u, pc(u))] for u in (fx, fy)]
    feed_w += [[((u, 0), (v, 0)) for u, v in ((fu, fd), (pc(fu), pc(fd)))]]

    rel_all = jnp.stack([by_rel[r](rel_bias) for r in range(4)])
    tables = key_tables(rel_all, core)
    query_hot = jnp.asarray(query_side(), bf16)

    packed, heads, probs = [None] * 4, [None] * 4, [None] * 4
    normed_one, packed[0], heads[0], probs[0] = attend(own_lengths, tokens, modes, attn_w[0], tables[0], query_hot)
    for r in (1, 2, 3):
        packed[r], heads[r], probs[r] = attend(
            own_lengths, normed_one, modes, attn_w[r], tables[r], query_hot, [ad] if r == 2 else []
        )
    attn_out, middle, normed_two, down_in = middle_step(heads, attn_w, tokens, cotangent, modes)

    hid, pre, mine, other = [None] * 4, [None] * 4, [None] * 4, [None] * 4

    def feed_step(r, after):
        hid[r], pre[r], mine[r], sent = feed(normed_two, down_in, feed_w[r], after)
        other[r] = pc(sent)

    feed_step(1, [fx, fy])
    feed_step(2, [])
    send_x = px(total(mine[1][0], other[1][0]))
    feed_step(3, [other[1]])
    send_y = py(total(mine[2][1], other[2][1]))
    feed_step(0, [other[2]])
    diag_x = px(total(mine[3][0], other[3][0]))
    diag_y = py(total(mine[3][1], other[3][1]))
    middle_grad, out_in, turn_sums = turn_step(
        pre, feed_w, middle, attn_out, cotangent, modes, [other[3], send_x]
    )
    last_x = px(total(mine[1][1], other[1][1], diag_y))
    last_y = py(total(mine[2][0], other[2][0], diag_x))
    feed_a = (mine[0][0], other[0][0], send_x, last_y)
    feed_b = (mine[0][1], other[0][1], last_x, send_y)

    class Steps:
        def __init__(self, a, b):
            low = (dp & z_bits[0]) == 0
            pick = lambda flag: [jnp.where(flag, u, v) for u, v in zip(a, b)]
            self.keep, self.sent = total(*pick(low)), total(*pick(~low))
            self.level, self.back, self.got = 0, [], None

        def down(self):
            self.got = swap_dp(z_bits[self.level])(self.sent)
            return self.got

        def cut(self):
            keep = total(self.keep, self.got)
            self.level += 1
            if self.level < len(z_bits):
                low = (dp & z_bits[self.level]) == 0
                size = keep.shape[0] // 2
                a, b = keep[:size], keep[size:]
                self.keep, self.sent = jnp.where(low, a, b), jnp.where(low, b, a)
            else:
                self.keep = keep

        def up(self):
            self.level -= 1
            self.got = swap_dp(z_bits[self.level])(self.keep)
            return self.got

        def join(self):
            low = (dp & z_bits[self.level]) == 0
            self.keep = ordered(low, self.keep, self.got)

        def rest(self):
            while self.level < len(z_bits):
                self.down()
                self.cut()
            while self.level > 0:
                self.up()
                self.join()
            return self.keep, pc(self.keep)

    packed_grad, rel_grid, a_mine, a_other = [None] * 4, [None] * 4, [None] * 4, [None] * 4

    def back_step(r, after):
        packed_grad[r], a_mine[r], sent, rel_grid[r] = attend_back(
            out_in, attn_w[r], packed[r], probs[r], query_hot, normed_one, heads[r], after
        )
        a_other[r] = pc(sent)

    cut = HALF // 2
    back_step(3, [send_y, other[0]])
    back_step(1, [diag_x, diag_y])
    a_diag_x = px(total(a_mine[3][:cut], a_other[3][:cut]))
    a_diag_y = py(total(a_mine[3][cut:], a_other[3][cut:]))
    back_step(2, [a_other[3]])
    a_send_x = px(total(a_mine[1][:cut], a_other[1][:cut]))
    back_step(0, [a_other[1], last_x, last_y, a_diag_x, a_diag_y])
    feed_steps = Steps(feed_a, feed_b)
    a_send_y = py(total(a_mine[2][cut:], a_other[2][cut:]))
    a_last_x = px(total(a_mine[1][cut:], a_other[1][cut:], a_diag_y))
    a_last_y = py(total(a_mine[2][:cut], a_other[2][:cut], a_diag_x))
    token_grads, last_sums = last_step(
        packed_grad, attn_w, tokens, modes, middle_grad, [a_other[2], a_send_x, feed_steps.down()]
    )
    feed_steps.cut()
    attn_steps = Steps(
        (a_mine[0][:cut], a_other[0][:cut], a_send_x, a_last_y), (a_mine[0][cut:], a_other[0][cut:], a_last_x, a_send_y)
    )
    output, out_sums = out_step(
        hid, feed_w, middle, cotangent, modes, [a_other[0], a_last_x, a_last_y, a_send_y, feed_steps.down()]
    )
    a, b = feed_steps.rest()
    up_back, down_back = cat(a[:HALF], b[:HALF]), ordered(core == 0, a[HALF:], b[HALF:])
    grad_up = lax.dot_general(up_back, up_hot, both, preferred_element_type=f32)
    grad_down = down_back.astype(f32)
    a, b = attn_steps.rest()
    grad_qkv = lax.dot_general(cat(a[:QKV], b[:QKV]), qkv_hot, both, preferred_element_type=f32)
    grad_out = ordered(core == 0, a[QKV:], b[QKV:]).astype(f32)

    rel_part = rel_sums(jnp.stack(rel_grid), core)
    for bit in (1, *z_bits):
        rel_part = rel_part + swap_dp(bit)(rel_part)
    grad_rel = rel_part[0] + px(rel_part[1]) + py(rel_part[2]) + pd(rel_part[3])

    mode_grad = jnp.concatenate([last_sums, turn_sums, out_sums], axis=1).reshape(micro, 4, -1)
    mode_grad_cols = jnp.stack(
        [by_rel[r](lax.dynamic_index_in_dim(mode_grad, mp ^ r, axis=1, keepdims=False)) for r in range(4)]
    )
    mode_low = mode_grad_cols.astype(bf16).reshape(4 * micro, -1)
    cond_rel = jnp.take(cond_low, order, axis=1).transpose(1, 0, 2).reshape(4 * micro, D)
    cond_all = dp_gather(cond_rel)
    mode_all = dp_gather(mode_low)
    grad_ada = mm(cond_all, mode_all, TN)
    grad_ada_bias = jnp.sum(mode_all.astype(f32), axis=0)
    cond_grad = mm(mode_low, ada_weight, NT).reshape(4, micro, D)
    cond_grad = jnp.take(cond_grad, order, axis=0)
    cond_grad = cond_grad + px(cond_grad)
    cond_grad = cond_grad + py(cond_grad)
    own_pre = pre_cond.transpose(1, 0, 2)
    share = 1.0 / (1.0 + jnp.exp(-own_pre))
    cond_grad = cond_grad * (share * (1.0 + own_pre * (1.0 - share)))
    class_all = dp_gather(classes.T.reshape(-1))
    class_hot = (jnp.arange(class_table.shape[0])[:, None] == class_all[None, :]).astype(f32)
    class_grad = jnp.dot(class_hot, dp_gather(cond_grad.reshape(4 * micro, D)), precision=precise)

    return (
        output,
        token_grads,
        grad_qkv,
        grad_out,
        grad_up,
        grad_down,
        grad_ada,
        grad_ada_bias,
        grad_rel,
        class_grad,
    )


def layer_norm(values):
    center = values - jnp.mean(values, axis=-1, keepdims=True)
    spread = jnp.mean(center * center, axis=-1, keepdims=True)
    return center * lax.rsqrt(spread + EPS)


def modulate(values, shift, scale):
    return layer_norm(values) * (1.0 + scale) + shift


def gelu_tanh(values):
    return (
        0.5
        * values
        * (
            1.0
            + jnp.tanh(math.sqrt(2.0 / math.pi) * (values + 0.044715 * values * values * values))
        )
    )


def condition_whole(timesteps, classes, class_table):
    half_width = class_table.shape[1] // 2
    frequency = jnp.exp(
        -math.log(10000.0) * jnp.arange(half_width).astype(class_table.dtype) / half_width
    )
    phase_angle = timesteps.astype(class_table.dtype)[..., None] * frequency
    sinusoid = jnp.concatenate([jnp.cos(phase_angle), jnp.sin(phase_angle)], axis=-1)
    onehot = (classes[..., None] == jnp.arange(class_table.shape[0])[None, None, :]).astype(
        class_table.dtype
    )
    lookup = jnp.einsum("mwc,cd->mwd", onehot, class_table, precision=precise)
    return silu_plain(sinusoid + lookup)


def axis_table(rel_part, window_span):
    places = jnp.arange(window_span)
    offsets = places[:, None] - places[None, :] + window_span - 1
    onehot = (offsets[:, :, None] == jnp.arange(2 * window_span - 1)[None, None, :]).astype(
        rel_part.dtype
    )
    return jnp.einsum("hr,abr->hab", rel_part, onehot, precision=precise)


def window_bias(rel_bias):
    frame_part = axis_table(rel_bias[:, : 2 * WT - 1], WT)
    row_part = axis_table(rel_bias[:, 2 * WT - 1 : 2 * WT + 2 * WH - 2], WH)
    column_part = axis_table(rel_bias[:, 2 * WT + 2 * WH - 2 :], WW)
    full_bias = (
        frame_part[:, :, None, None, :, None, None]
        + row_part[:, None, :, None, None, :, None]
        + column_part[:, None, None, :, None, None, :]
    )
    return full_bias.reshape(rel_bias.shape[0], WIN, WIN)


def attention_scores(query_part, key_part, bias_full, masks):
    scores = (
        jnp.einsum("wqhd,wkhd->whqk", query_part, key_part, preferred_element_type=jnp.float32)
        * HD ** (-0.5)
        + bias_full[None]
    )
    return jnp.where(masks[:, None, None, :], scores, -1e30)


def local_general(
    tokens,
    cotangent,
    qkv_weight,
    out_weight,
    up_weight,
    down_weight,
    ada_weight,
    ada_bias,
    rel_bias,
    class_table,
    lengths,
    timesteps,
    classes,
):
    micro_count = tokens.shape[0]
    row_count = tokens.shape[1]
    win_count = lengths.shape[1]
    heads_here = rel_bias.shape[0]
    head_scale = HD ** (-0.5)
    first_row = lax.axis_index("mp") * row_count
    row_window = (first_row + jnp.arange(row_count)) // WIN
    spread_rows = (row_window[:, None] == jnp.arange(win_count)[None, :]).astype(jnp.float32)
    cond_low = condition_whole(timesteps, classes, class_table).astype(jnp.bfloat16)
    mode_cols = jnp.einsum(
        "mwd,de->mwe", cond_low, ada_weight, preferred_element_type=jnp.float32
    ) + ada_bias.astype(jnp.float32)
    mode_all = lax.all_gather(mode_cols, "mp", axis=2, tiled=True)
    bias_full, bias_pull = jax.vjp(window_bias, rel_bias)
    frame_of = jnp.arange(WIN) // (WH * WW)
    grad_qkv = jnp.zeros(qkv_weight.shape, jnp.float32)
    grad_out = jnp.zeros(out_weight.shape, jnp.float32)
    grad_up = jnp.zeros(up_weight.shape, jnp.float32)
    grad_down = jnp.zeros(down_weight.shape, jnp.float32)
    grad_rel = jnp.zeros(rel_bias.shape, jnp.float32)
    mode_parts = []
    outputs = []
    token_grads = []
    for micro_step in range(micro_count):
        mode_rows = jnp.dot(spread_rows, mode_all[micro_step], precision=precise)
        shift_attn, scale_attn, gate_attn, shift_mlp, scale_mlp, gate_mlp = jnp.split(
            mode_rows, 6, axis=1
        )
        inputs = tokens[micro_step].astype(jnp.float32)
        normed_one, pull_one = jax.vjp(modulate, inputs, shift_attn, scale_attn)
        gathered_one = lax.all_gather(normed_one.astype(jnp.bfloat16), "mp", axis=0, tiled=True)
        packed = jnp.dot(gathered_one, qkv_weight, preferred_element_type=jnp.float32).astype(
            jnp.bfloat16
        )
        packed = packed.reshape(win_count, WIN, heads_here, 3, HD)
        query_part = packed[:, :, :, 0]
        key_part = packed[:, :, :, 1]
        value_part = packed[:, :, :, 2]
        masks = frame_of[None, :] < lengths[micro_step][:, None]
        scores = attention_scores(query_part, key_part, bias_full, masks)
        top_score = jnp.max(scores, axis=-1, keepdims=True)
        expo = jnp.exp(scores - top_score)
        total = jnp.sum(expo, axis=-1, keepdims=True)
        log_total = top_score + jnp.log(total)
        probs_low = (expo / total).astype(jnp.bfloat16)
        heads_out = jnp.einsum(
            "whqk,wkhd->wqhd", probs_low, value_part, preferred_element_type=jnp.float32
        ).astype(jnp.bfloat16)
        heads_out = heads_out.reshape(win_count * WIN, heads_here * HD)
        attn_out = lax.psum_scatter(
            jnp.dot(heads_out, out_weight, preferred_element_type=jnp.float32),
            "mp",
            scatter_dimension=0,
            tiled=True,
        )
        middle = inputs + gate_attn * attn_out
        normed_two, pull_two = jax.vjp(modulate, middle, shift_mlp, scale_mlp)
        grad_y = cotangent[micro_step].astype(jnp.float32)
        down_in = (gate_mlp * grad_y).astype(jnp.bfloat16)
        gathered_two = lax.all_gather(normed_two.astype(jnp.bfloat16), "mp", axis=0, tiled=True)
        hidden_pre = jnp.dot(gathered_two, up_weight, preferred_element_type=jnp.float32)
        hidden_low, gelu_pull = jax.vjp(gelu_tanh, hidden_pre)
        hidden_low = hidden_low.astype(jnp.bfloat16)
        mlp_out = lax.psum_scatter(
            jnp.dot(hidden_low, down_weight, preferred_element_type=jnp.float32),
            "mp",
            scatter_dimension=0,
            tiled=True,
        )
        down_all = lax.all_gather(down_in, "mp", axis=0, tiled=True)
        hidden_grad = jnp.einsum(
            "rd,fd->rf", down_all, down_weight, preferred_element_type=jnp.float32
        )
        micro_down = jnp.einsum(
            "rf,rd->fd", hidden_low, down_all, preferred_element_type=jnp.float32
        )
        pre_low = gelu_pull(hidden_grad)[0].astype(jnp.bfloat16)
        micro_up = jnp.einsum(
            "rd,rf->df", gathered_two, pre_low, preferred_element_type=jnp.float32
        )
        normed_two_grad = lax.psum_scatter(
            jnp.einsum("rf,df->rd", pre_low, up_weight, preferred_element_type=jnp.float32),
            "mp",
            scatter_dimension=0,
            tiled=True,
        )
        outputs.append(middle + gate_mlp * mlp_out)
        grad_gate_mlp = grad_y * mlp_out
        resid_grad, grad_shift_mlp, grad_scale_mlp = pull_two(normed_two_grad)
        middle_grad = grad_y + resid_grad
        grad_gate_attn = middle_grad * attn_out
        out_in = (gate_attn * middle_grad).astype(jnp.bfloat16)
        out_all = lax.all_gather(out_in, "mp", axis=0, tiled=True)
        micro_out = jnp.einsum("rc,rd->cd", heads_out, out_all, preferred_element_type=jnp.float32)
        heads_grad = jnp.einsum(
            "rd,cd->rc", out_all, out_weight, preferred_element_type=jnp.float32
        ).astype(jnp.bfloat16)
        heads_grad = heads_grad.reshape(win_count, WIN, heads_here, HD)
        probs = jnp.exp(attention_scores(query_part, key_part, bias_full, masks) - log_total)
        probs_low = probs.astype(jnp.bfloat16)
        value_grad = jnp.einsum(
            "whqk,wqhd->wkhd", probs_low, heads_grad, preferred_element_type=jnp.float32
        )
        probs_grad = jnp.einsum(
            "wqhd,wkhd->whqk", heads_grad, value_part, preferred_element_type=jnp.float32
        )
        score_grad = probs * (probs_grad - jnp.sum(probs * probs_grad, axis=-1, keepdims=True))
        micro_rel = bias_pull(jnp.sum(score_grad, axis=0))[0]
        score_low = (score_grad * head_scale).astype(jnp.bfloat16)
        query_grad = jnp.einsum(
            "whqk,wkhd->wqhd", score_low, key_part, preferred_element_type=jnp.float32
        )
        key_grad = jnp.einsum(
            "whqk,wqhd->wkhd", score_low, query_part, preferred_element_type=jnp.float32
        )
        packed_grad = jnp.stack([query_grad, key_grad, value_grad], axis=3).astype(jnp.bfloat16)
        packed_grad = packed_grad.reshape(win_count * WIN, heads_here * 3 * HD)
        micro_qkv = jnp.einsum(
            "rd,rc->dc", gathered_one, packed_grad, preferred_element_type=jnp.float32
        )
        normed_one_grad = lax.psum_scatter(
            jnp.einsum("rc,dc->rd", packed_grad, qkv_weight, preferred_element_type=jnp.float32),
            "mp",
            scatter_dimension=0,
            tiled=True,
        )
        input_grad, grad_shift_attn, grad_scale_attn = pull_one(normed_one_grad)
        token_grads.append(middle_grad + input_grad)
        row_modes = jnp.concatenate(
            [
                grad_shift_attn,
                grad_scale_attn,
                grad_gate_attn,
                grad_shift_mlp,
                grad_scale_mlp,
                grad_gate_mlp,
            ],
            axis=1,
        )
        mode_parts.append(jnp.einsum("rw,re->we", spread_rows, row_modes, precision=precise))
        local_grads = (micro_qkv, micro_out, micro_rel, micro_up, micro_down)
        grad_qkv = grad_qkv + local_grads[0]
        grad_out = grad_out + local_grads[1]
        grad_rel = grad_rel + local_grads[2]
        grad_up = grad_up + local_grads[3]
        grad_down = grad_down + local_grads[4]
    mode_grad_cols = lax.psum_scatter(jnp.stack(mode_parts), "mp", scatter_dimension=2, tiled=True)
    mode_low = mode_grad_cols.astype(jnp.bfloat16)
    grad_ada = jnp.einsum("mwd,mwe->de", cond_low, mode_low, preferred_element_type=jnp.float32)
    grad_ada_bias = jnp.sum(mode_grad_cols, axis=(0, 1))
    cond_grad = jnp.einsum("mwe,de->mwd", mode_low, ada_weight, preferred_element_type=jnp.float32)
    cond_value, cond_pull = jax.vjp(partial(condition_whole, timesteps, classes), class_table)
    class_total = lax.psum(cond_pull(cond_grad)[0], ("dp", "mp"))
    grad_qkv, grad_out, grad_up, grad_down, grad_rel, grad_ada, grad_ada_bias = lax.psum(
        (grad_qkv, grad_out, grad_up, grad_down, grad_rel, grad_ada, grad_ada_bias), "dp"
    )
    return (
        jnp.stack(outputs).astype(jnp.bfloat16),
        jnp.stack(token_grads).astype(jnp.bfloat16),
        grad_qkv,
        grad_out,
        grad_up,
        grad_down,
        grad_ada,
        grad_ada_bias,
        grad_rel,
        class_total,
    )


def local(sizes, *arrays):
    if arrays[0].shape[1] == WIN and sizes[1] == 4:
        return local_windows(sizes, *arrays)
    return local_general(*arrays)


def solution(mesh):
    in_specs = (
        P(None, ("dp", "mp"), None),
        P(None, ("dp", "mp"), None),
        P(None, "mp"),
        P("mp", None),
        P(None, "mp"),
        P("mp", None),
        P(None, "mp"),
        P("mp"),
        P("mp", None),
        P(),
        P(None, "dp"),
        P(None, "dp"),
        P(None, "dp"),
    )
    out_specs = (
        P(None, ("dp", "mp"), None),
        P(None, ("dp", "mp"), None),
        P(None, "mp"),
        P("mp", None),
        P(None, "mp"),
        P("mp", None),
        P(None, "mp"),
        P("mp"),
        P("mp", None),
        P(),
    )
    sizes = (mesh.shape["dp"], mesh.shape["mp"])
    return jax.shard_map(
        partial(local, sizes), mesh=mesh, in_specs=in_specs, out_specs=out_specs, check_vma=False
    )
```

```python
from functools import partial
import math

import jax
import jax.numpy as jnp
import numpy as np
from jax import lax
from jax.experimental import pallas as pl
from jax.experimental.pallas import tpu as pltpu
from jax.sharding import PartitionSpec as P

HD = 64
WT = 5
WH = 8
WW = 8
WIN = 320
D = 1024
EPS = 1e-06
NOFF = WT + WH + WW
C0 = math.sqrt(2.0 / math.pi)
C1 = 0.044715
precise = lax.Precision.HIGHEST
f32 = jnp.float32
bf16 = jnp.bfloat16
NN = (((1,), (0,)), ((), ()))
NT = (((1,), (1,)), ((), ()))
TN = (((0,), (0,)), ((), ()))
HALF = 512
QKV = 384


def mm(a, b, dims=NN):
    return lax.dot_general(a, b, dims, preferred_element_type=f32)


def whole(*dims):
    return pl.BlockSpec(dims, lambda i, *_: (0,) * len(dims))


def part(index, *dims):
    return pl.BlockSpec(dims, lambda i, *_: index)


def rows_of(width):
    return pl.BlockSpec((WIN, width), lambda i, *_: (i, 0))


def window_of(*dims):
    return pl.BlockSpec((None,) + dims, lambda i, *_: (i,) + (0,) * len(dims))


def shape(dims, dtype):
    return pltpu.HBM(dims, dtype)


def near(dims, dtype):
    return jax.ShapeDtypeStruct(dims, dtype)


HBM = pl.BlockSpec(memory_space=pltpu.HBM)
VMEM = pl.BlockSpec(memory_space=pltpu.VMEM)
ANY = pl.BlockSpec(memory_space=pl.ANY)


class Loads:
    def __init__(self, sems):
        self.sems, self.copies = sems, []

    def add(self, source, target):
        self.copies.append(pltpu.make_async_copy(source, target, self.sems.at[len(self.copies)]))
        return self.copies[-1]

    def start(self):
        for copy in self.copies:
            copy.start()

    def wait(self):
        for copy in self.copies:
            copy.wait()


def in_hbm(array):
    return pltpu.with_memory_space_constraint(array, pltpu.HBM)


def run(kernel, name, grid, ins, outs, scratch=(), after=(), scalars=(), flops=0, moved=0, vmem=24):
    first = len(scalars) + len(ins)

    def body(*refs):
        kernel(*refs[:first], *refs[first + len(after) :])

    return pl.pallas_call(
        body,
        grid_spec=pltpu.PrefetchScalarGridSpec(
            num_scalar_prefetch=len(scalars),
            grid=(grid,),
            in_specs=[spec for _, spec in ins] + [HBM] * len(after),
            out_specs=[spec for _, spec in outs],
            scratch_shapes=list(scratch),
        ),
        out_shape=[what for what, _ in outs],
        compiler_params=pltpu.CompilerParams(vmem_limit_bytes=vmem * 2**20),
        cost_estimate=pl.CostEstimate(flops=1000, bytes_accessed=1000, transcendentals=0),
        name=name,
    )(*scalars, *[array if spec is VMEM else in_hbm(array) for array, spec in ins], *map(in_hbm, after))


def hold(values, after=(), flops=1000):
    return pl.pallas_call(
        lambda *refs: None,
        in_specs=[HBM] * (len(values) + len(after)),
        out_specs=[HBM] * len(values),
        out_shape=[shape(v.shape, v.dtype) for v in values],
        input_output_aliases={i: i for i in range(len(values))},
        cost_estimate=pl.CostEstimate(flops=flops, bytes_accessed=1000, transcendentals=0),
        name="hold",
    )(*map(in_hbm, (*values, *after)))


def arrive(values, after):
    return hold(values, after, 30 * 10**9)


def ln_parts(values):
    center = values - jnp.mean(values, axis=-1, keepdims=True)
    rstd = lax.rsqrt(jnp.mean(center * center, axis=-1, keepdims=True) + EPS)
    return center * rstd, rstd


def ln_back(grad, scale, hat, rstd):
    inner = grad * (1.0 + scale)
    mean_one = jnp.mean(inner, axis=-1, keepdims=True)
    mean_two = jnp.mean(inner * hat, axis=-1, keepdims=True)
    return rstd * (inner - mean_one - hat * mean_two)


def hot_rows(count, source):
    row = lax.broadcasted_iota(jnp.int32, (count, count), 0)
    col = lax.broadcasted_iota(jnp.int32, (count, count), 1)
    return col == source(row), row


def qkv_source(core):
    def source(row):
        half = jnp.where(row >= QKV, 1, 0)
        inner = row - half * QKV
        head = 2 * (half ^ core) + ((inner & 127) >> 6)
        return head * 3 * HD + (inner >> 7) * HD + (inner & 63)

    return source


def attn_rows_kernel(core_ref, qkv_ref, out_ref, own0, own1):
    core = core_ref[0]
    hot, row = hot_rows(2 * QKV, qkv_source(core))
    inner = jnp.where(row >= QKV, row - QKV, row)
    hot = jnp.where(hot, jnp.where(inner < 128, HD**-0.5, 1.0), 0.0).astype(bf16)
    rows = mm(hot, qkv_ref[...], NT).astype(bf16)
    for h, own in enumerate((own0, own1)):
        own[:QKV] = rows[h * QKV : (h + 1) * QKV]
        own[QKV:] = out_ref[pl.ds(pl.multiple_of((core ^ h) * 128, 128), 128)]


def feed_rows_kernel(core_ref, up_ref, down_ref, own0, own1):
    core = core_ref[0]
    hot, _ = hot_rows(2 * HALF, lambda row: row ^ (core * HALF))
    rows = mm(jnp.where(hot, 1.0, 0.0).astype(bf16), up_ref[...], NT).astype(bf16)
    for h, own in enumerate((own0, own1)):
        own[0] = rows[h * HALF : (h + 1) * HALF]
        own[1] = down_ref[pl.ds(pl.multiple_of((core ^ h) * HALF, HALF), HALF)]


def attn_rows(core, qkv, out, after):
    half = (shape((HALF, D), bf16), whole(HALF, D))
    ins = [(qkv, whole(D, 2 * QKV)), (out, whole(256, D))]
    return run(attn_rows_kernel, "attn_rows", 1, ins, [half, half], (), after, [core], 1e9, 4e6)


def feed_rows(core, up, down, after):
    half = (shape((2, HALF, D), bf16), whole(2, HALF, D))
    ins = [(up, whole(D, 2 * HALF)), (down, whole(2 * HALF, D))]
    return run(feed_rows_kernel, "feed_rows", 1, ins, [half, half], (), after, [core], 2e9, 8e6)


def attend_kernel(len_ref, x_ref, mode_ref, wa_ref, wb_ref, tbl_ref, e_ref, *rest):
    n1_ref, packed_ref, heads_ref, probs_ref, w_all, kb_all, sems = rest if len(rest) == 7 else (None, *rest)
    w = pl.program_id(0)

    @pl.when(w == 0)
    def _():
        loads = Loads(sems)
        loads.add(wa_ref.at[:QKV], w_all.at[:QKV])
        loads.add(wb_ref.at[:QKV], w_all.at[QKV:])
        loads.start()
        for p in range(2):
            kb_all[p] = mm(e_ref[...], tbl_ref[p]).astype(bf16)
        loads.wait()

    if n1_ref is None:
        x = x_ref[...]
    else:
        hat, _ = ln_parts(x_ref[...].astype(f32))
        x = (hat * (1.0 + mode_ref[1:2]) + mode_ref[0:1]).astype(bf16)
        n1_ref[...] = x
    pk = mm(x, w_all[...], NT).astype(bf16)
    packed_ref[...] = pk
    lane = lax.broadcasted_iota(jnp.int32, (WIN, 128), 1)
    low = lane < 64
    frame = lax.broadcasted_iota(jnp.int32, (WIN, 128), 0) // (WH * WW)
    mask_lane = (lane & 63) == 2 * NOFF
    hide = jnp.where(frame < len_ref[w], 0.0, -1e30).astype(bf16)
    for p in range(2):
        q = pk[:, p * QKV : p * QKV + 128]
        k = pk[:, p * QKV + 128 : p * QKV + 256]
        v = pk[:, p * QKV + 256 : p * QKV + 384]
        kb = jnp.where(mask_lane, hide, kb_all[p])
        outs = []
        for i in range(2):
            mine = low if i == 0 else ~low
            s = mm(jnp.where(mine, q, e_ref[...]), jnp.where(mine, k, kb), NT)
            ex = jnp.exp(s - jnp.max(s, axis=1, keepdims=True))
            pr = (ex * (1.0 / jnp.sum(ex, axis=1, keepdims=True))).astype(bf16)
            probs_ref[2 * p + i] = pr
            outs.append(mm(pr, v))
        heads_ref[:, p * 128 : (p + 1) * 128] = jnp.where(low, outs[0], outs[1]).astype(bf16)


def attend(lengths, source, modes, weight, table, query_hot, after=()):
    count = lengths.shape[0]
    rows = count * WIN
    first = source.ndim == 3
    outs = [
        (shape((rows, 2 * QKV), bf16), rows_of(2 * QKV)),
        (shape((rows, 256), bf16), rows_of(256)),
        (shape((count * 4, WIN, WIN), bf16), pl.BlockSpec((4, WIN, WIN), lambda i, l: (i, 0, 0))),
    ]
    if first:
        outs = [(near((rows, D), bf16), rows_of(D))] + outs
    return run(
        attend_kernel,
        "attend",
        count,
        [
            (source, window_of(WIN, D) if first else rows_of(D)),
            (modes, window_of(6, D)),
            (weight[0], ANY),
            (weight[1], ANY),
            (table, whole(2, 128, 128)),
            (query_hot, whole(WIN, 128)),
        ],
        outs,
        [pltpu.VMEM((2 * QKV, D), bf16), pltpu.VMEM((2, WIN, 128), bf16), pltpu.SemaphoreType.DMA((2,))],
        after,
        [lengths],
        9e9,
        12e6,
    )


def middle_kernel(h0, h1, h2, h3, w0, w1, w2, w3, w4, w5, w6, w7, tok, cot, mode, attn_ref, mid_ref, n2_ref, di_ref, w_all, sems):
    @pl.when(pl.program_id(0) == 0)
    def _():
        loads = Loads(sems)
        for i, ref in enumerate((w0, w1, w2, w3, w4, w5, w6, w7)):
            loads.add(ref.at[QKV:], w_all.at[pl.ds(i * 128, 128)])
        loads.start()
        loads.wait()

    heads = jnp.concatenate([h0[...], h1[...], h2[...], h3[...]], axis=1)
    attn = mm(heads, w_all[...])
    attn_ref[...] = attn.astype(bf16)
    middle = tok[...].astype(f32) + mode[2:3] * attn
    mid_ref[...] = middle
    hat, _ = ln_parts(middle)
    n2_ref[...] = (hat * (1.0 + mode[4:5]) + mode[3:4]).astype(bf16)
    di_ref[...] = (mode[5:6] * cot[...].astype(f32)).astype(bf16)


def middle_step(heads, weights, tokens, cotangent, modes, after=()):
    count = tokens.shape[0]
    rows = count * WIN
    return run(
        middle_kernel,
        "middle",
        count,
        [(h, rows_of(256)) for h in heads]
        + [(half, ANY) for pair in weights for half in pair]
        + [(tokens, window_of(WIN, D)), (cotangent, window_of(WIN, D)), (modes, window_of(6, D))],
        [(shape((rows, D), kind), rows_of(D)) for kind in (bf16, f32)] + [(near((rows, D), bf16), rows_of(D))] * 2,
        [pltpu.VMEM((D, D), bf16), pltpu.SemaphoreType.DMA((8,))],
        after,
        flops=2.7e9,
        moved=22e6,
    )


CHUNK = 256


def feed_kernel(places, n2, di, up0, dn0, up1, dn1, hid_hbm, pre_hbm, g0_hbm, g1_hbm, weight, hid, pre, grad, in_sems, out_sems):
    loads, stores = Loads(in_sems), Loads(out_sems)
    for i, ref in enumerate((up0, dn0, up1, dn1)):
        loads.add(ref.at[places[i]], weight.at[i // 2, i % 2])
    for i in (2, 3, 0, 1):
        loads.copies[i].start()

    def store(from_ref, to_ref):
        stores.add(from_ref, to_ref).start()

    for h, g_hbm in ((1, g1_hbm), (0, g0_hbm)):
        units = pl.ds(h * HALF, HALF)
        loads.copies[2 * h].wait()
        loads.copies[2 * h + 1].wait()
        for i in range(n2.shape[0] // CHUNK):
            rows = pl.ds(i * CHUNK, CHUNK)
            v = mm(n2[rows], weight[h, 0], NT)
            hg = mm(di[rows], weight[h, 1], NT)
            v2 = v * v
            t = jnp.tanh(v * (C0 + (C0 * C1) * v2))
            share = 0.5 + 0.5 * t
            hid[h, rows] = (v * share).astype(bf16)
            slope = share + (0.5 * v) * (1.0 - t * t) * (C0 + (3.0 * C0 * C1) * v2)
            pre[h, rows] = (slope * hg).astype(bf16)
        store(hid.at[h], hid_hbm.at[:, units])
        store(pre.at[h], pre_hbm.at[:, units])
        grad[h, 1] = mm(hid[h], di[...], TN).astype(bf16)
        store(grad.at[h, 1], g_hbm.at[1])
        grad[h, 0] = mm(pre[h], n2[...], TN).astype(bf16)
        store(grad.at[h, 0], g_hbm.at[0])
    stores.wait()


def feed(normed, down_in, weight, after=()):
    rows = normed.shape[0]
    halves = [array for half in weight for array, _ in half]
    places = [place for half in weight for _, place in half]
    return run(
        partial(feed_kernel, places),
        "feed",
        1,
        [(normed, VMEM), (down_in, VMEM)] + [(array, HBM) for array in halves],
        [(shape((rows, 2 * HALF), bf16), HBM)] * 2 + [(shape((2, HALF, D), bf16), HBM)] * 2,
        [pltpu.VMEM((2, 2, HALF, D), bf16)]
        + [pltpu.VMEM((2, rows, HALF), bf16)] * 2
        + [pltpu.VMEM((2, 2, HALF, D), bf16), pltpu.SemaphoreType.DMA((4,)), pltpu.SemaphoreType.DMA((8,))],
        after,
        vmem=32,
    )


def unit_sums(sources, pieces, places, weight, acc, sems):
    w = pl.program_id(0)

    def span(i):
        return slice(i % 2 * HALF, (i % 2 + 1) * HALF)

    @pl.when(w == 0)
    def _():
        loads = Loads(sems)
        for i, piece in enumerate(pieces):
            loads.add(piece.at[places[i]], weight.at[pl.ds(i * HALF, HALF)])
        loads.start()
        for i, copy in enumerate(loads.copies):
            copy.wait()
            term = mm(sources[i // 2][:, span(i)], weight[i * HALF : (i + 1) * HALF])
            acc[...] = term if i == 0 else acc[...] + term

    @pl.when(w > 0)
    def _():
        source = jnp.concatenate([ref[...] for ref in sources], axis=1)
        acc[...] = mm(source, weight[...])


def turn_kernel(places, p0, p1, p2, p3, w0, w1, w2, w3, w4, w5, w6, w7, mid_ref, attn_ref, cot_ref, mode_ref, *rest):
    mg_ref, oi_ref, sum_ref, weight, acc, sems = rest
    unit_sums((p0, p1, p2, p3), (w0, w1, w2, w3, w4, w5, w6, w7), places, weight, acc, sems)
    ng = acc[...]
    hat, rstd = ln_parts(mid_ref[...])
    mg = cot_ref[...].astype(f32) + ln_back(ng, mode_ref[4:5], hat, rstd)
    mg_ref[...] = mg
    oi_ref[...] = (mode_ref[2:3] * mg).astype(bf16)
    sum_ref[0:1] = jnp.sum(mg * attn_ref[...].astype(f32), axis=0, keepdims=True)
    sum_ref[1:2] = jnp.sum(ng, axis=0, keepdims=True)
    sum_ref[2:3] = jnp.sum(ng * hat, axis=0, keepdims=True)


def out_kernel(places, p0, p1, p2, p3, w0, w1, w2, w3, w4, w5, w6, w7, mid_ref, cot_ref, mode_ref, *rest):
    out_ref, sum_ref, weight, acc, sems = rest
    unit_sums((p0, p1, p2, p3), (w0, w1, w2, w3, w4, w5, w6, w7), places, weight, acc, sems)
    mlp = acc[...]
    out_ref[...] = (mid_ref[...] + mode_ref[5:6] * mlp).astype(bf16)
    sum_ref[...] = jnp.sum(cot_ref[...].astype(f32) * mlp, axis=0, keepdims=True)


def of_units(arrays, weights, which):
    halves = [half[which] for pair in weights for half in pair]
    ins = [(array, rows_of(2 * HALF)) for array in arrays] + [(array, HBM) for array, _ in halves]
    scratch = [pltpu.VMEM((8 * HALF, D), bf16), pltpu.VMEM((WIN, D), f32), pltpu.SemaphoreType.DMA((8,))]
    return ins, scratch, [place for _, place in halves]


def turn_step(pre, weights, middle, attn_out, cotangent, modes, after=()):
    count = cotangent.shape[0]
    rows = count * WIN
    ins, scratch, places = of_units(pre, weights, 0)
    return run(
        partial(turn_kernel, places),
        "turn",
        count,
        ins
        + [(middle, rows_of(D)), (attn_out, rows_of(D)), (cotangent, window_of(WIN, D)), (modes, window_of(6, D))],
        [
            (shape((rows, D), f32), rows_of(D)),
            (near((rows, D), bf16), rows_of(D)),
            (shape((count, 3, D), f32), window_of(3, D)),
        ],
        scratch,
        after,
        vmem=36,
        flops=10.7e9,
        moved=35e6,
    )


def out_step(hid, weights, middle, cotangent, modes, after=()):
    count = cotangent.shape[0]
    ins, scratch, places = of_units(hid, weights, 1)
    return run(
        partial(out_kernel, places),
        "output",
        count,
        ins + [(middle, rows_of(D)), (cotangent, window_of(WIN, D)), (modes, window_of(6, D))],
        [(shape((count, WIN, D), bf16), window_of(WIN, D)), (shape((count, 1, D), f32), window_of(1, D))],
        scratch,
        after,
        vmem=36,
        flops=10.7e9,
        moved=30e6,
    )


def attend_back_kernel(
    oi_ref, o0, o1, pk_ref, pr_ref, e_ref, n1_ref, oi_all, ho_hbm, pg_ref, g0_ref, g1_ref, rel_ref, *scratch
):
    pg_all, t_all, ow, ho_ref, sems = scratch
    w = pl.program_id(0)
    loads = Loads(sems)
    weights = [loads.add(o.at[QKV:], ow.at[pl.ds(i * 128, 128)]) for i, o in enumerate((o0, o1))]
    heads = loads.add(ho_hbm, ho_ref)

    @pl.when(w == 0)
    def _():
        loads.start()
        t_all[...] = jnp.zeros_like(t_all)
        for copy in weights:
            copy.wait()

    hg = mm(oi_ref[...], ow[...], NT).astype(bf16)
    pk = pk_ref[...]
    low = lax.broadcasted_iota(jnp.int32, (WIN, 128), 1) < 64
    for p in range(2):
        q = pk[:, p * QKV : p * QKV + 128]
        k = pk[:, p * QKV + 128 : p * QKV + 256]
        v = pk[:, p * QKV + 256 : p * QKV + 384]
        do = hg[:, p * 128 : (p + 1) * 128]
        dv, dq, dk = [], [], []
        for i in range(2):
            mine = low if i == 0 else ~low
            qa = jnp.where(mine, q, e_ref[...])
            dp = mm(jnp.where(mine, do, jnp.zeros_like(do)), v, NT)
            prl = pr_ref[2 * p + i]
            pr = prl.astype(f32)
            t = pr * dp
            ds = (t - pr * jnp.sum(t, axis=1, keepdims=True)).astype(bf16)
            dv.append(mm(prl, do, TN))
            dq.append(mm(ds, k))
            dk.append(mm(ds, qa, TN))
        block = jnp.concatenate(
            [jnp.where(low, dq[0], dq[1]), jnp.where(low, dk[0], dk[1]), jnp.where(low, dv[0], dv[1])], axis=1
        ).astype(bf16)
        pg_ref[:, p * QKV : (p + 1) * QKV] = block
        pg_all[pl.ds(pl.multiple_of(w * WIN, WIN), WIN), p * QKV : (p + 1) * QKV] = block
        t_all[p] += jnp.where(low, dk[1], dk[0])

    @pl.when(w == pl.num_programs(0) - 1)
    def _():
        heads.wait()
        go = mm(ho_ref[...], oi_all[...], TN).astype(bf16)
        gq = mm(pg_all[...], n1_ref[...], TN).astype(bf16)
        for p, g_ref in enumerate((g0_ref, g1_ref)):
            g_ref[:QKV] = gq[p * QKV : (p + 1) * QKV]
            g_ref[QKV:] = go[p * 128 : (p + 1) * 128]
        hot = e_ref[...].astype(f32)
        for p in range(2):
            sums = lax.dot_general(hot, t_all[p], TN, precision=precise, preferred_element_type=f32)
            rel_ref[p] = sums[:32]


def attend_back(out_in, weight, packed, probs, query_hot, normed, heads, after=()):
    rows = normed.shape[0]
    return run(
        attend_back_kernel,
        "attend_back",
        rows // WIN,
        [
            (out_in, rows_of(D)),
            (weight[0], ANY),
            (weight[1], ANY),
            (packed, rows_of(2 * QKV)),
            (probs, pl.BlockSpec((4, WIN, WIN), lambda i: (i, 0, 0))),
            (query_hot, whole(WIN, 128)),
            (normed, VMEM),
            (out_in, VMEM),
            (heads, HBM),
        ],
        [
            (shape((rows, 2 * QKV), bf16), rows_of(2 * QKV)),
            (shape((HALF, D), bf16), whole(HALF, D)),
            (shape((HALF, D), bf16), whole(HALF, D)),
            (shape((2, 32, 128), f32), whole(2, 32, 128)),
        ],
        [pltpu.VMEM((rows, 2 * QKV), bf16), pltpu.VMEM((2, WIN, 128), f32), pltpu.VMEM((256, D), bf16)]
        + [pltpu.VMEM((rows, 256), bf16), pltpu.SemaphoreType.DMA((3,))],
        after,
        flops=13e9,
        moved=20e6,
    )


def last_kernel(p0, p1, p2, p3, w0, w1, w2, w3, w4, w5, w6, w7, tok_ref, mode_ref, mg_ref, out_ref, sum_ref, w_all, acc, sems):
    @pl.when(pl.program_id(0) == 0)
    def _():
        loads = Loads(sems)
        for i, ref in enumerate((w0, w1, w2, w3, w4, w5, w6, w7)):
            loads.add(ref.at[:QKV], w_all.at[pl.ds(i * QKV, QKV)])
        loads.start()
        for i, src in enumerate((p0, p1, p2, p3)):
            loads.copies[2 * i].wait()
            loads.copies[2 * i + 1].wait()
            term = mm(src[...], w_all[i * 2 * QKV : (i + 1) * 2 * QKV])
            acc[...] = term if i == 0 else acc[...] + term

    @pl.when(pl.program_id(0) > 0)
    def _():
        acc[...] = mm(jnp.concatenate([p0[...], p1[...], p2[...], p3[...]], axis=1), w_all[...])

    ng = acc[...]
    hat, rstd = ln_parts(tok_ref[...].astype(f32))
    out_ref[...] = (mg_ref[...] + ln_back(ng, mode_ref[1:2], hat, rstd)).astype(bf16)
    sum_ref[0:1] = jnp.sum(ng, axis=0, keepdims=True)
    sum_ref[1:2] = jnp.sum(ng * hat, axis=0, keepdims=True)


def last_step(packed_grads, weights, tokens, modes, middle_grad, after=()):
    count = tokens.shape[0]
    return run(
        last_kernel,
        "last",
        count,
        [(array, rows_of(2 * QKV)) for array in packed_grads]
        + [(half, ANY) for pair in weights for half in pair]
        + [(tokens, window_of(WIN, D)), (modes, window_of(6, D)), (middle_grad, rows_of(D))],
        [(shape((count, WIN, D), bf16), window_of(WIN, D)), (shape((count, 2, D), f32), window_of(2, D))],
        [pltpu.VMEM((8 * QKV, D), bf16), pltpu.VMEM((WIN, D), f32), pltpu.SemaphoreType.DMA((8,))],
        after,
        flops=8e9,
        moved=24e6,
    )


def merge_kernel(sums, count, *refs):
    i = pl.program_id(0)
    refs = list(refs)
    outs = refs[len(refs) - len(sums) :]
    for spans, out in zip(sums, outs):
        value = None
        for first, last in spans:
            term = refs.pop(0)[...].astype(f32)
            if (first, last) != (0, count):
                term = jnp.where((i >= first) & (i < last), term, 0.0)
            value = term if value is None else value + term
        out[...] = value.astype(bf16)


def merge(*sums, rows=HALF, after=()):
    block = 128
    ins, spans = [], []
    for terms in sums:
        spans.append([])
        for array, place, start, *limits in terms:
            first, last = [limit // block for limit in (limits or (0, rows))]
            start = start // block

            def at(i, start=start, first=first, last=last):
                return jnp.clip(i, first, last - 1) + start

            if place is None:
                spec = pl.BlockSpec((block, D), lambda i, at=at: (at(i), 0))
            else:
                spec = pl.BlockSpec((None, block, D), lambda i, p=place, at=at: (p, at(i), 0))
            ins.append((array, spec))
            spans[-1].append((first, last))
    out = (shape((rows, D), bf16), pl.BlockSpec((block, D), lambda i: (i, 0)))
    return run(partial(merge_kernel, spans, rows // block), "merge", rows // block, ins, [out] * len(sums), (), after)


def parts_kernel(count, only, z_ref, *refs):
    which_sum = pl.program_id(0) % (1 + max([0] + [w for w in only if w is not None]))
    terms = len(only)
    for k in range(count):
        value = None
        for ref, which in zip(refs[k * terms : (k + 1) * terms], only):
            term = ref[...].astype(f32)
            if which is not None:
                term = jnp.where(which_sum == which, term, 0.0)
            value = term if value is None else value + term
        refs[count * terms + k][...] = value.astype(bf16)


def merge_parts(terms, z, count, outputs):
    size = HALF // count
    sums = max(2 if isinstance(term, tuple) or term.ndim == 3 else 1 for term in terms)
    ins, only = [], []
    for j in range(outputs):
        for term in terms:
            array, which = term if isinstance(term, tuple) else (term, None)

            def at(i, zr, j=j):
                return zr[0] ^ (i // sums * outputs + j)

            if array.ndim == 3:
                spec = pl.BlockSpec((None, size, D), lambda i, zr, at=at: (i % sums, at(i, zr), 0))
            else:
                spec = pl.BlockSpec((size, D), lambda i, zr, at=at: (at(i, zr), 0))
            ins.append((array, spec))
            only.append(which)
    grid = sums * count // outputs
    outs = [(shape((grid * size, D), bf16), pl.BlockSpec((size, D), lambda i, zr: (i, 0)))] * outputs
    return run(partial(parts_kernel, outputs, only[: len(terms)]), "merge_parts", grid, ins, outs, (), (), [z])


def attn_final_kernel(place_ref, a_ref, b_ref, qkv_ref, out_ref, rows):
    core, z = place_ref[0], place_ref[1]
    size = HALF // 4
    for h, ref in enumerate((a_ref, b_ref)):
        for k in range(4):
            part_at = z ^ k
            block = ref[k * size : (k + 1) * size]

            @pl.when(part_at < 3)
            def _():
                rows[pl.ds(pl.multiple_of(h * QKV + part_at * size, size), size)] = block

            @pl.when(part_at == 3)
            def _():
                out_ref[pl.ds(pl.multiple_of((core ^ h) * size, size), size)] = block.astype(f32)

    hot, row = hot_rows(2 * QKV, qkv_source(core))
    inner = jnp.where(row >= QKV, row - QKV, row)
    hot = jnp.where(hot, jnp.where(inner < 128, HD**-0.5, 1.0), 0.0).astype(bf16)
    qkv_ref[...] = mm(rows[...], hot, TN)


def attn_final(place, a, b):
    ins = [(a, whole(HALF, D)), (b, whole(HALF, D))]
    outs = [(shape((D, 2 * QKV), f32), whole(D, 2 * QKV)), (shape((256, D), f32), whole(256, D))]
    return run(attn_final_kernel, "attn_final", 1, ins, outs, [pltpu.VMEM((2 * QKV, D), bf16)], (), [place])


def feed_final_kernel(place_ref, *refs):
    up_ref, down_ref, rows = refs[4:]
    core, z = place_ref[0], place_ref[1]
    size = HALF // 4
    for h in range(2):
        for k, (ref, first) in enumerate(((refs[2 * h], 0), (refs[2 * h + 1], 0), (refs[2 * h], 2), (refs[2 * h + 1], 2))):
            start = (z ^ k) * size
            rows[pl.ds(pl.multiple_of(h * HALF + start, size), size)] = ref[first * size : (first + 1) * size]
            block = ref[(first + 1) * size : (first + 2) * size].astype(f32)
            down_ref[pl.ds(pl.multiple_of((core ^ h) * HALF + start, size), size)] = block
    hot, _ = hot_rows(2 * HALF, lambda row: row ^ (core * HALF))
    up_ref[...] = mm(rows[...], jnp.where(hot, 1.0, 0.0).astype(bf16), TN)


def feed_final(place, even, odd, other_even, other_odd):
    ins = [(v, whole(HALF, D)) for v in (even, odd, other_even, other_odd)]
    outs = [(shape((D, 2 * HALF), f32), whole(D, 2 * HALF)), (shape((2 * HALF, D), f32), whole(2 * HALF, D))]
    return run(feed_final_kernel, "feed_final", 1, ins, outs, [pltpu.VMEM((2 * HALF, D), bf16)], (), [place])


def silu_plain(values):
    return values / (1.0 + jnp.exp(-values))


def condition(timesteps, classes, class_table):
    half_width = class_table.shape[1] // 2
    frequency = jnp.exp(
        -math.log(10000.0) * jnp.arange(half_width).astype(class_table.dtype) / half_width
    )
    phase_angle = timesteps.astype(class_table.dtype)[..., None] * frequency
    sinusoid = jnp.concatenate([jnp.cos(phase_angle), jnp.sin(phase_angle)], axis=-1)
    onehot = (classes[..., None] == jnp.arange(class_table.shape[0])).astype(class_table.dtype)
    lookup = jnp.einsum("mwc,cd->mwd", onehot, class_table, precision=precise)
    return sinusoid + lookup


SPANS = ((0, 0, WT), (WT, 2 * WT - 1, WH), (WT + WH, 2 * WT + 2 * WH - 2, WW))


def place_hot():
    spot = np.arange(WIN)
    hot = np.zeros((WIN, NOFF), np.float32)
    for (start, _, _), where in zip(SPANS, (spot // (WH * WW), (spot // WW) % WH, spot % WW)):
        hot[spot, start + where] = 1.0
    return hot


def query_side():
    half = np.zeros((WIN, 64), np.float32)
    half[:, :NOFF] = place_hot()
    half[:, NOFF : 2 * NOFF] = place_hot()
    half[:, 2 * NOFF] = 1.0
    return np.concatenate([half, half], axis=1)


def offset_hot(rows, copies):
    hot = np.zeros((2 * NOFF - 3, rows, 64), np.float32)
    for start, begin, length in SPANS:
        for key in range(length):
            for query in range(length):
                for copy in range(copies):
                    hot[begin + query - key + length - 1, start + key, copy * NOFF + start + query] = 1.0
    return hot


def key_tables(rel, core):
    value = jnp.einsum("hr,rkq->hkq", rel.reshape(16, -1), offset_hot(64, 2), precision=precise)
    top = lax.reduce_precision(value, 8, 7)
    value = jnp.where(jnp.arange(64) < NOFF, top, value - top).astype(bf16)
    value = value.reshape(4, 2, 2, 64, 64)
    value = jnp.where(core == 0, value, value[:, ::-1])
    value = jnp.concatenate([value[:, :, 1], value[:, :, 0]], axis=-1)
    return jnp.pad(value, ((0, 0), (0, 0), (0, 64), (0, 0)))


def rel_sums(grids, core):
    grids = jnp.where(core == 0, grids, grids[:, ::-1])
    grids = grids.reshape(4, 2, 32, 2, 64)
    grids = jnp.stack([grids[:, :, :, 1], grids[:, :, :, 0]], axis=2).reshape(16, 32, 64)
    return jnp.einsum("hkq,rkq->hr", grids, offset_hot(32, 1), precision=precise).reshape(4, 4, -1)


def local_windows(
    sizes,
    tokens,
    cotangent,
    qkv_weight,
    out_weight,
    up_weight,
    down_weight,
    ada_weight,
    ada_bias,
    rel_bias,
    class_table,
    lengths,
    timesteps,
    classes,
):
    n_z, n_mp = sizes
    n_dp = 2 * n_z
    micro = tokens.shape[0]
    mp = lax.axis_index("mp")
    z = lax.axis_index("z")
    core = lax.axis_index("core")

    def swap_mp(bit):
        return lambda v: lax.ppermute(v, "mp", [(i, i ^ bit) for i in range(n_mp)])

    def swap_dp(bit):
        return lambda v: lax.ppermute(v, ("z", "core"), [(i, i ^ bit) for i in range(n_dp)])

    px, py, pd = swap_mp(1), swap_mp(2), swap_mp(3)
    pc = swap_dp(1)
    by_rel = [lambda v: v, px, py, pd]

    def cat(a, b, axis=0):
        return jnp.concatenate([a, b], axis=axis)

    dp_steps = [(1, core == 0)] + [(2 << b, ((z >> b) & 1) == 0) for b in range(n_z.bit_length() - 1)]

    def join(low, v, got):
        return cat(jnp.where(low, v, got), jnp.where(low, got, v))

    pre_cond = condition(timesteps, classes, class_table)
    cond_low = silu_plain(pre_cond).astype(bf16)
    mode_cols = jnp.einsum("mwd,de->mwe", cond_low, ada_weight, preferred_element_type=f32) + ada_bias.astype(f32)
    order = jnp.arange(4) ^ mp
    rel_row = jnp.pad(rel_bias, ((0, 0), (0, 128 - rel_bias.shape[1])))
    messages = [
        by_rel[r](cat(lax.dynamic_index_in_dim(mode_cols, mp ^ r, axis=1, keepdims=False), rel_row, 1))
        for r in range(4)
    ]
    messages = jnp.stack(messages)
    columns = mode_cols.shape[-1]
    modes = jnp.take(messages[:, :, :columns], order, axis=0)
    modes = modes.transpose(1, 0, 2).reshape(micro, 6, D)
    tables = key_tables(messages[:, :, columns : columns + rel_bias.shape[1]], core)
    own_lengths = lax.dynamic_index_in_dim(lengths, mp, axis=1, keepdims=False)

    core_row = core.reshape(1)
    query_hot = jnp.asarray(query_side(), bf16)
    packed, heads, probs = [None] * 4, [None] * 4, [None] * 4

    attn_own = attn_rows(core_row, qkv_weight, out_weight, [messages])
    ax, ay = px(attn_own[0]), py(attn_own[0])
    normed_one, packed[0], heads[0], probs[0] = attend(own_lengths, tokens, modes, attn_own, tables[0], query_hot)
    feed_own = list(feed_rows(core_row, up_weight, down_weight, [heads[0]]))
    ax, ay = hold([ax, ay], [heads[0]])
    adx, ady = py(ax[: HALF // 2]), px(ay[HALF // 2 :])
    attn_w = [attn_own, [ax, pc(ax)], [ay, pc(ay)]]
    packed[1], heads[1], probs[1] = attend(
        own_lengths, normed_one, modes, attn_w[1], tables[1], query_hot, [feed_own[1]]
    )
    adx, ady = hold([adx, ady], [heads[1]])
    (feed_own[0],) = hold(feed_own[:1], [adx, ady])
    fx, fy = px(feed_own[0]), py(feed_own[0])
    ad = cat(adx, ady)
    attn_w.append([ad, pc(ad)])
    for r in (2, 3):
        packed[r], heads[r], probs[r] = attend(
            own_lengths, normed_one, modes, attn_w[r], tables[r], query_hot, [heads[r - 1]]
        )
    attn_out, middle, normed_two, down_in = middle_step(heads, attn_w, tokens, cotangent, modes)

    hid, pre, mine, other = [None] * 4, [None] * 4, [None] * 4, [None] * 4

    def feed_step(r, weight, after):
        hid[r], pre[r], mine[r], sent = feed(normed_two, down_in, weight, after)
        other[r] = pc(sent)

    def pair(r, which):
        return [(mine[r], which, 0), (other[r], which, 0)]

    feed_w = [[((v, 0), (v, 1)) for v in feed_own]]
    feed_step(0, feed_w[0], [])
    fx, fy = hold([fx, fy], [hid[0]])
    fu, fd = fx[:1], fy[1:]
    feed_w += [[((v, 0), (v, 1)) for v in (u, pc(u))] for u in (fx, fy)]
    feed_step(1, feed_w[1], [hid[0], fu, fd])
    fu, fd = py(fu), px(fd)
    feed_step(2, feed_w[2], [hid[1]])
    fu, fd = arrive([fu, fd], [hid[2]])
    feed_w += [[((u, 0), (v, 0)) for u, v in ((fu, fd), (pc(fu), pc(fd)))]]
    (send_x,) = merge(pair(1, 0), after=[fu])
    (send_y,) = merge(pair(2, 1), after=[send_x])
    feed_step(3, feed_w[3], [hid[2], send_y])
    send_x, send_y = arrive([px(send_x), py(send_y)], [hid[3]])
    diag_x, diag_y = merge(pair(3, 0), pair(3, 1), after=[send_x])
    middle_grad, out_in, turn_sums = turn_step(
        pre, feed_w, middle, attn_out, cotangent, modes, [diag_x, diag_y]
    )
    diag_x, diag_y = arrive([px(diag_x), py(diag_y)], [middle_grad])
    last_x, last_y = merge(pair(1, 1) + [(diag_y, None, 0)], pair(2, 0) + [(diag_x, None, 0)])
    output, out_sums = out_step(hid, feed_w, middle, cotangent, modes, [last_x, last_y])
    last_x, last_y = arrive([px(last_x), py(last_y)], [out_sums])
    z_row = z.reshape(1)
    terms = [mine[0], other[0], (send_x, 0), (last_y, 0), (last_x, 1), (send_y, 1)]
    feed_keep, feed_sent = merge_parts(terms, z_row, n_z, 2)
    z_one, z_two = swap_dp(2), swap_dp(4)

    packed_grad, rel_grid, a_mine, a_other = [None] * 4, [None] * 4, [None] * 4, [None] * 4

    def back_step(r, after):
        packed_grad[r], a_mine[r], sent, rel_grid[r] = attend_back(
            out_in, attn_w[r], packed[r], probs[r], query_hot, normed_one, heads[r], after
        )
        a_other[r] = pc(sent)

    cut = HALF // 2

    def a_pair(r, start):
        return [(a_mine[r], None, start), (a_other[r], None, start)]

    back_step(3, [feed_keep])
    (feed_got,) = arrive([z_one(feed_sent)], [packed_grad[3]])
    (feed_sent,) = merge([(feed_keep, None, cut), (feed_got, None, cut)], rows=cut)
    back_step(1, [packed_grad[3], feed_sent])
    (feed_two,) = arrive([z_two(feed_sent)], [packed_grad[1]])
    (feed_one,) = merge([(feed_keep, None, 0), (feed_got, None, 0), (feed_two, None, 0)], rows=cut)
    a_diag_x, a_diag_y = merge(a_pair(3, 0), a_pair(3, cut), rows=cut, after=[feed_one])
    back_step(2, [a_diag_x, a_diag_y])
    feed_two, a_diag_x, a_diag_y = arrive([z_two(feed_one), px(a_diag_x), py(a_diag_y)], [packed_grad[2]])
    feed_even = cat(feed_one, feed_two)
    (a_last_x,) = merge(a_pair(1, 0) + [(a_diag_y, None, -cut, cut, HALF)])
    (a_last_y,) = merge(a_pair(2, 0) + [(a_diag_x, None, 0, 0, cut)], after=[a_last_x])
    back_step(0, [packed_grad[2], a_last_y, feed_even])
    feed_odd, a_last_x, a_last_y = arrive([z_one(feed_even), px(a_last_x), py(a_last_y)], [packed_grad[0]])

    def exchange(parts):
        return [swap_dp(2 * k)(v) for k, v in enumerate(parts) if k]

    attn_parts = merge_parts([a_mine[0], a_other[0], a_last_x, a_last_y], z_row, n_z, n_z)
    token_grads, last_sums = last_step(packed_grad, attn_w, tokens, modes, middle_grad, attn_parts)
    attn_got = exchange(attn_parts)
    feed_other = [pc(feed_even), pc(feed_odd)]
    *attn_got, feed_other[0], feed_other[1] = arrive(attn_got + feed_other, [last_sums])
    (attn_own,) = merge([(v, None, 0) for v in (attn_parts[0], *attn_got)], rows=HALF // n_z)

    place = jnp.stack([core, z])
    mode_grad = jnp.concatenate([last_sums, turn_sums, out_sums], axis=1).reshape(micro, 4, -1).transpose(1, 0, 2)
    messages = [lax.dynamic_index_in_dim(mode_grad, mp ^ r, axis=0, keepdims=False) for r in range(4)]
    rel_grid = hold(rel_grid, [attn_own])
    rel_part = jnp.pad(rel_sums(jnp.stack(rel_grid), core), ((0, 0), (0, 4 * (micro - 1)), (0, 128 - rel_bias.shape[1])))
    *messages[1:], attn_far = arrive([by_rel[r](messages[r]) for r in (1, 2, 3)] + [swap_dp(6)(attn_own)], [attn_own])
    mode_low = jnp.stack(messages).astype(bf16).reshape(4 * micro, -1)
    cond_grad = mm(mode_low, ada_weight, NT).reshape(4, micro, D)
    cond_grad = jnp.take(cond_grad, order, axis=0).reshape(4 * micro, D)
    grad_up, grad_down = feed_final(place, feed_even, feed_odd, *feed_other)
    shares = [cat(cond_grad, rel_part[r], 1) for r in range(4)]
    *shares[1:], attn_two = arrive(
        [by_rel[r](shares[r]) for r in (1, 2, 3)] + [swap_dp(4)(attn_own)], [attn_far, grad_up]
    )
    shares = jnp.take(jnp.stack(shares), order, axis=0)
    cond_grad = shares[0] + shares[1] + shares[2] + shares[3]
    own_pre = pre_cond.transpose(1, 0, 2).reshape(4 * micro, D)
    share = 1.0 / (1.0 + jnp.exp(-own_pre))
    own_class = cond_grad[:, :D] * (share * (1.0 + own_pre * (1.0 - share)))
    grads = jnp.concatenate([mode_low, own_class.astype(bf16), cond_grad[:, D:].astype(bf16)], axis=1)
    got, attn_one = arrive([swap_dp(dp_steps[0][0])(grads), swap_dp(2)(attn_own)], [attn_two])
    grads = join(dp_steps[0][1], grads, got)
    attn_own = jnp.concatenate([attn_own, attn_one, attn_two, attn_far])
    got, attn_other = arrive([swap_dp(dp_steps[1][0])(grads), pc(attn_own)], [attn_one])
    grads = join(dp_steps[1][1], grads, got)
    grad_qkv, grad_out = attn_final(place, attn_own, attn_other)
    for step, low in dp_steps[2:]:
        (got,) = arrive([swap_dp(step)(grads)], [grad_qkv])
        grads = join(low, grads, got)
    mode_all, class_part, rel_part = grads[:, :columns], grads[:, columns : columns + D], grads[:, columns + D :]
    grad_rel = jnp.sum(rel_part.astype(f32).reshape(n_dp, 4 * micro, -1), axis=0)[:4, : rel_bias.shape[1]]

    class_col = jnp.pad(classes.T.reshape(-1, 1).astype(bf16), ((0, 0), (0, 127)))
    cond_rel = jnp.take(cond_low, order, axis=1).transpose(1, 0, 2).reshape(4 * micro, D)
    cond_all = cat(cond_rel, class_col, 1)
    for step, low in dp_steps:
        cond_all = join(low, cond_all, swap_dp(step)(cond_all))
    class_all = cond_all[:, D].astype(jnp.int32)
    grad_ada = mm(cond_all[:, :D], mode_all, TN)
    grad_ada_bias = jnp.sum(mode_all.astype(f32), axis=0)
    class_hot = (jnp.arange(class_table.shape[0])[:, None] == class_all[None, :]).astype(bf16)
    class_grad = jnp.dot(class_hot, class_part, preferred_element_type=f32)

    return (
        output,
        token_grads,
        grad_qkv,
        grad_out,
        grad_up,
        grad_down,
        grad_ada,
        grad_ada_bias,
        grad_rel,
        class_grad,
    )


def layer_norm(values):
    center = values - jnp.mean(values, axis=-1, keepdims=True)
    spread = jnp.mean(center * center, axis=-1, keepdims=True)
    return center * lax.rsqrt(spread + EPS)


def modulate(values, shift, scale):
    return layer_norm(values) * (1.0 + scale) + shift


def gelu_tanh(values):
    return (
        0.5
        * values
        * (
            1.0
            + jnp.tanh(math.sqrt(2.0 / math.pi) * (values + 0.044715 * values * values * values))
        )
    )


def condition_whole(timesteps, classes, class_table):
    half_width = class_table.shape[1] // 2
    frequency = jnp.exp(
        -math.log(10000.0) * jnp.arange(half_width).astype(class_table.dtype) / half_width
    )
    phase_angle = timesteps.astype(class_table.dtype)[..., None] * frequency
    sinusoid = jnp.concatenate([jnp.cos(phase_angle), jnp.sin(phase_angle)], axis=-1)
    onehot = (classes[..., None] == jnp.arange(class_table.shape[0])[None, None, :]).astype(
        class_table.dtype
    )
    lookup = jnp.einsum("mwc,cd->mwd", onehot, class_table, precision=precise)
    return silu_plain(sinusoid + lookup)


def axis_table(rel_part, window_span):
    places = jnp.arange(window_span)
    offsets = places[:, None] - places[None, :] + window_span - 1
    onehot = (offsets[:, :, None] == jnp.arange(2 * window_span - 1)[None, None, :]).astype(
        rel_part.dtype
    )
    return jnp.einsum("hr,abr->hab", rel_part, onehot, precision=precise)


def window_bias(rel_bias):
    frame_part = axis_table(rel_bias[:, : 2 * WT - 1], WT)
    row_part = axis_table(rel_bias[:, 2 * WT - 1 : 2 * WT + 2 * WH - 2], WH)
    column_part = axis_table(rel_bias[:, 2 * WT + 2 * WH - 2 :], WW)
    full_bias = (
        frame_part[:, :, None, None, :, None, None]
        + row_part[:, None, :, None, None, :, None]
        + column_part[:, None, None, :, None, None, :]
    )
    return full_bias.reshape(rel_bias.shape[0], WIN, WIN)


def attention_scores(query_part, key_part, bias_full, masks):
    scores = (
        jnp.einsum("wqhd,wkhd->whqk", query_part, key_part, preferred_element_type=jnp.float32)
        * HD ** (-0.5)
        + bias_full[None]
    )
    return jnp.where(masks[:, None, None, :], scores, -1e30)


def local_general(
    tokens,
    cotangent,
    qkv_weight,
    out_weight,
    up_weight,
    down_weight,
    ada_weight,
    ada_bias,
    rel_bias,
    class_table,
    lengths,
    timesteps,
    classes,
):
    micro_count = tokens.shape[0]
    row_count = tokens.shape[1]
    win_count = lengths.shape[1]
    heads_here = rel_bias.shape[0]
    head_scale = HD ** (-0.5)
    first_row = lax.axis_index("mp") * row_count
    row_window = (first_row + jnp.arange(row_count)) // WIN
    spread_rows = (row_window[:, None] == jnp.arange(win_count)[None, :]).astype(jnp.float32)
    cond_low = condition_whole(timesteps, classes, class_table).astype(jnp.bfloat16)
    mode_cols = jnp.einsum(
        "mwd,de->mwe", cond_low, ada_weight, preferred_element_type=jnp.float32
    ) + ada_bias.astype(jnp.float32)
    mode_all = lax.all_gather(mode_cols, "mp", axis=2, tiled=True)
    bias_full, bias_pull = jax.vjp(window_bias, rel_bias)
    frame_of = jnp.arange(WIN) // (WH * WW)
    grad_qkv = jnp.zeros(qkv_weight.shape, jnp.float32)
    grad_out = jnp.zeros(out_weight.shape, jnp.float32)
    grad_up = jnp.zeros(up_weight.shape, jnp.float32)
    grad_down = jnp.zeros(down_weight.shape, jnp.float32)
    grad_rel = jnp.zeros(rel_bias.shape, jnp.float32)
    mode_parts = []
    outputs = []
    token_grads = []
    for micro_step in range(micro_count):
        mode_rows = jnp.dot(spread_rows, mode_all[micro_step], precision=precise)
        shift_attn, scale_attn, gate_attn, shift_mlp, scale_mlp, gate_mlp = jnp.split(
            mode_rows, 6, axis=1
        )
        inputs = tokens[micro_step].astype(jnp.float32)
        normed_one, pull_one = jax.vjp(modulate, inputs, shift_attn, scale_attn)
        gathered_one = lax.all_gather(normed_one.astype(jnp.bfloat16), "mp", axis=0, tiled=True)
        packed = jnp.dot(gathered_one, qkv_weight, preferred_element_type=jnp.float32).astype(
            jnp.bfloat16
        )
        packed = packed.reshape(win_count, WIN, heads_here, 3, HD)
        query_part = packed[:, :, :, 0]
        key_part = packed[:, :, :, 1]
        value_part = packed[:, :, :, 2]
        masks = frame_of[None, :] < lengths[micro_step][:, None]
        scores = attention_scores(query_part, key_part, bias_full, masks)
        top_score = jnp.max(scores, axis=-1, keepdims=True)
        expo = jnp.exp(scores - top_score)
        total = jnp.sum(expo, axis=-1, keepdims=True)
        log_total = top_score + jnp.log(total)
        probs_low = (expo / total).astype(jnp.bfloat16)
        heads_out = jnp.einsum(
            "whqk,wkhd->wqhd", probs_low, value_part, preferred_element_type=jnp.float32
        ).astype(jnp.bfloat16)
        heads_out = heads_out.reshape(win_count * WIN, heads_here * HD)
        attn_out = lax.psum_scatter(
            jnp.dot(heads_out, out_weight, preferred_element_type=jnp.float32),
            "mp",
            scatter_dimension=0,
            tiled=True,
        )
        middle = inputs + gate_attn * attn_out
        normed_two, pull_two = jax.vjp(modulate, middle, shift_mlp, scale_mlp)
        grad_y = cotangent[micro_step].astype(jnp.float32)
        down_in = (gate_mlp * grad_y).astype(jnp.bfloat16)
        gathered_two = lax.all_gather(normed_two.astype(jnp.bfloat16), "mp", axis=0, tiled=True)
        hidden_pre = jnp.dot(gathered_two, up_weight, preferred_element_type=jnp.float32)
        hidden_low, gelu_pull = jax.vjp(gelu_tanh, hidden_pre)
        hidden_low = hidden_low.astype(jnp.bfloat16)
        mlp_out = lax.psum_scatter(
            jnp.dot(hidden_low, down_weight, preferred_element_type=jnp.float32),
            "mp",
            scatter_dimension=0,
            tiled=True,
        )
        down_all = lax.all_gather(down_in, "mp", axis=0, tiled=True)
        hidden_grad = jnp.einsum(
            "rd,fd->rf", down_all, down_weight, preferred_element_type=jnp.float32
        )
        micro_down = jnp.einsum(
            "rf,rd->fd", hidden_low, down_all, preferred_element_type=jnp.float32
        )
        pre_low = gelu_pull(hidden_grad)[0].astype(jnp.bfloat16)
        micro_up = jnp.einsum(
            "rd,rf->df", gathered_two, pre_low, preferred_element_type=jnp.float32
        )
        normed_two_grad = lax.psum_scatter(
            jnp.einsum("rf,df->rd", pre_low, up_weight, preferred_element_type=jnp.float32),
            "mp",
            scatter_dimension=0,
            tiled=True,
        )
        outputs.append(middle + gate_mlp * mlp_out)
        grad_gate_mlp = grad_y * mlp_out
        resid_grad, grad_shift_mlp, grad_scale_mlp = pull_two(normed_two_grad)
        middle_grad = grad_y + resid_grad
        grad_gate_attn = middle_grad * attn_out
        out_in = (gate_attn * middle_grad).astype(jnp.bfloat16)
        out_all = lax.all_gather(out_in, "mp", axis=0, tiled=True)
        micro_out = jnp.einsum("rc,rd->cd", heads_out, out_all, preferred_element_type=jnp.float32)
        heads_grad = jnp.einsum(
            "rd,cd->rc", out_all, out_weight, preferred_element_type=jnp.float32
        ).astype(jnp.bfloat16)
        heads_grad = heads_grad.reshape(win_count, WIN, heads_here, HD)
        probs = jnp.exp(attention_scores(query_part, key_part, bias_full, masks) - log_total)
        probs_low = probs.astype(jnp.bfloat16)
        value_grad = jnp.einsum(
            "whqk,wqhd->wkhd", probs_low, heads_grad, preferred_element_type=jnp.float32
        )
        probs_grad = jnp.einsum(
            "wqhd,wkhd->whqk", heads_grad, value_part, preferred_element_type=jnp.float32
        )
        score_grad = probs * (probs_grad - jnp.sum(probs * probs_grad, axis=-1, keepdims=True))
        micro_rel = bias_pull(jnp.sum(score_grad, axis=0))[0]
        score_low = (score_grad * head_scale).astype(jnp.bfloat16)
        query_grad = jnp.einsum(
            "whqk,wkhd->wqhd", score_low, key_part, preferred_element_type=jnp.float32
        )
        key_grad = jnp.einsum(
            "whqk,wqhd->wkhd", score_low, query_part, preferred_element_type=jnp.float32
        )
        packed_grad = jnp.stack([query_grad, key_grad, value_grad], axis=3).astype(jnp.bfloat16)
        packed_grad = packed_grad.reshape(win_count * WIN, heads_here * 3 * HD)
        micro_qkv = jnp.einsum(
            "rd,rc->dc", gathered_one, packed_grad, preferred_element_type=jnp.float32
        )
        normed_one_grad = lax.psum_scatter(
            jnp.einsum("rc,dc->rd", packed_grad, qkv_weight, preferred_element_type=jnp.float32),
            "mp",
            scatter_dimension=0,
            tiled=True,
        )
        input_grad, grad_shift_attn, grad_scale_attn = pull_one(normed_one_grad)
        token_grads.append(middle_grad + input_grad)
        row_modes = jnp.concatenate(
            [
                grad_shift_attn,
                grad_scale_attn,
                grad_gate_attn,
                grad_shift_mlp,
                grad_scale_mlp,
                grad_gate_mlp,
            ],
            axis=1,
        )
        mode_parts.append(jnp.einsum("rw,re->we", spread_rows, row_modes, precision=precise))
        local_grads = (micro_qkv, micro_out, micro_rel, micro_up, micro_down)
        grad_qkv = grad_qkv + local_grads[0]
        grad_out = grad_out + local_grads[1]
        grad_rel = grad_rel + local_grads[2]
        grad_up = grad_up + local_grads[3]
        grad_down = grad_down + local_grads[4]
    mode_grad_cols = lax.psum_scatter(jnp.stack(mode_parts), "mp", scatter_dimension=2, tiled=True)
    mode_low = mode_grad_cols.astype(jnp.bfloat16)
    grad_ada = jnp.einsum("mwd,mwe->de", cond_low, mode_low, preferred_element_type=jnp.float32)
    grad_ada_bias = jnp.sum(mode_grad_cols, axis=(0, 1))
    cond_grad = jnp.einsum("mwe,de->mwd", mode_low, ada_weight, preferred_element_type=jnp.float32)
    cond_value, cond_pull = jax.vjp(partial(condition_whole, timesteps, classes), class_table)
    class_total = lax.psum(cond_pull(cond_grad)[0], ("dp", "mp"))
    grad_qkv, grad_out, grad_up, grad_down, grad_rel, grad_ada, grad_ada_bias = lax.psum(
        (grad_qkv, grad_out, grad_up, grad_down, grad_rel, grad_ada, grad_ada_bias), "dp"
    )
    return (
        jnp.stack(outputs).astype(jnp.bfloat16),
        jnp.stack(token_grads).astype(jnp.bfloat16),
        grad_qkv,
        grad_out,
        grad_up,
        grad_down,
        grad_ada,
        grad_ada_bias,
        grad_rel,
        class_total,
    )


def solution(mesh):
    n_dp, n_mp = mesh.shape["dp"], mesh.shape["mp"]

    def specs(*dp):
        rows = P(None, (*dp, "mp"), None)
        weights = (P(None, "mp"), P("mp", None), P(None, "mp"), P("mp", None), P(None, "mp"), P("mp"), P("mp", None), P())
        return (rows, rows, *weights, *[P(None, dp)] * 3), (rows, rows, *weights)

    def program(tokens, *arrays):
        if n_mp == 4 and n_dp % 2 == 0 and tokens.shape[1] == n_dp * n_mp * WIN:
            devices = mesh.devices.reshape(n_dp // 2, 2, n_mp)
            split = jax.sharding.Mesh(devices, ("z", "core", "mp"))
            ins, outs = specs("z", "core")
            step = jax.shard_map(
                partial(local_windows, (n_dp // 2, n_mp)), mesh=split, in_specs=ins, out_specs=outs, check_vma=False
            )
        else:
            ins, outs = specs("dp")
            step = jax.shard_map(local_general, mesh=mesh, in_specs=ins, out_specs=outs, check_vma=False)
        return step(tokens, *arrays)

    return program
```

```python
from functools import partial
import math
from typing import NamedTuple

import jax
import jax.numpy as jnp
import numpy as np
from jax import lax
from jax.experimental import pallas as pl
from jax.experimental.pallas import tpu as pltpu
from jax.sharding import PartitionSpec as P

HD = 64
WT = 5
WH = 8
WW = 8
WIN = 320
D = 1024
EPS = 1e-06
NOFF = WT + WH + WW
C0 = math.sqrt(2.0 / math.pi)
C1 = 0.044715
precise = lax.Precision.HIGHEST
f32 = jnp.float32
bf16 = jnp.bfloat16
NN = (((1,), (0,)), ((), ()))
NT = (((1,), (1,)), ((), ()))
TN = (((0,), (0,)), ((), ()))
HALF = 512
QKV = 384


def mm(a, b, dims=NN):
    return lax.dot_general(a, b, dims, preferred_element_type=f32)


def whole(*dims):
    return pl.BlockSpec(dims, lambda i, *_: (0,) * len(dims))


def part(index, *dims):
    return pl.BlockSpec(dims, lambda i, *_: index)


def rows_of(width):
    return pl.BlockSpec((WIN, width), lambda i, *_: (i, 0))


def window_of(*dims):
    return pl.BlockSpec((None,) + dims, lambda i, *_: (i,) + (0,) * len(dims))


def shape(dims, dtype):
    return pltpu.HBM(dims, dtype)


def near(dims, dtype):
    return jax.ShapeDtypeStruct(dims, dtype)


HBM = pl.BlockSpec(memory_space=pltpu.HBM)
VMEM = pl.BlockSpec(memory_space=pltpu.VMEM)


class Loads:
    def __init__(self, sems):
        self.sems, self.copies = sems, []

    def add(self, source, target):
        self.copies.append(pltpu.make_async_copy(source, target, self.sems.at[len(self.copies)]))
        return self.copies[-1]

    def start(self):
        for copy in self.copies:
            copy.start()

    def wait(self):
        for copy in self.copies:
            copy.wait()


class Moved(NamedTuple):
    array: jax.Array


def in_hbm(array):
    return pltpu.with_memory_space_constraint(array, pltpu.HBM)


def operand(array, spec):
    if isinstance(array, Moved):
        return array.array, pl.BlockSpec(memory_space=pl.ANY) if spec is HBM else spec
    return array if spec is VMEM else in_hbm(array), spec


def run(kernel, name, grid, ins, outs, scratch=(), after=(), scalars=(), flops=0, moved=0, vmem=24):
    first = len(scalars) + len(ins)

    ins = [operand(array, spec) for array, spec in ins]

    def body(*refs):
        kernel(*refs[:first], *refs[first + len(after) :])

    return pl.pallas_call(
        body,
        grid_spec=pltpu.PrefetchScalarGridSpec(
            num_scalar_prefetch=len(scalars),
            grid=(grid,),
            in_specs=[spec for _, spec in ins] + [HBM] * len(after),
            out_specs=[spec for _, spec in outs],
            scratch_shapes=list(scratch),
        ),
        out_shape=[what for what, _ in outs],
        compiler_params=pltpu.CompilerParams(vmem_limit_bytes=vmem * 2**20),
        cost_estimate=pl.CostEstimate(flops=1000, bytes_accessed=1000, transcendentals=0),
        name=name,
    )(*scalars, *[array for array, _ in ins], *map(in_hbm, after))


def hold(values, after=(), flops=1000):
    anywhere = pl.BlockSpec(memory_space=pl.ANY)
    return pl.pallas_call(
        lambda *refs: None,
        in_specs=[anywhere] * len(values) + [HBM] * len(after),
        out_specs=[anywhere] * len(values),
        out_shape=[near(v.shape, v.dtype) for v in values],
        input_output_aliases={i: i for i in range(len(values))},
        cost_estimate=pl.CostEstimate(flops=flops, bytes_accessed=1000, transcendentals=0),
        name="hold",
    )(*values, *map(in_hbm, after))


def arrive(values, after):
    return hold(values, after, 30 * 10**9)


def ln_parts(values):
    center = values - jnp.mean(values, axis=-1, keepdims=True)
    rstd = lax.rsqrt(jnp.mean(center * center, axis=-1, keepdims=True) + EPS)
    return center * rstd, rstd


def ln_back(grad, scale, hat, rstd):
    inner = grad * (1.0 + scale)
    mean_one = jnp.mean(inner, axis=-1, keepdims=True)
    mean_two = jnp.mean(inner * hat, axis=-1, keepdims=True)
    return rstd * (inner - mean_one - hat * mean_two)


def hot_rows(count, source):
    row = lax.broadcasted_iota(jnp.int32, (count, count), 0)
    col = lax.broadcasted_iota(jnp.int32, (count, count), 1)
    return col == source(row), row


def qkv_source(core):
    def source(row):
        half = jnp.where(row >= QKV, 1, 0)
        inner = row - half * QKV
        head = 2 * (half ^ core) + ((inner & 127) >> 6)
        return head * 3 * HD + (inner >> 7) * HD + (inner & 63)

    return source


def attn_rows_kernel(core_ref, qkv_ref, out_ref, own0, own1):
    core = core_ref[0]
    hot, row = hot_rows(2 * QKV, qkv_source(core))
    inner = jnp.where(row >= QKV, row - QKV, row)
    hot = jnp.where(hot, jnp.where(inner < 128, HD**-0.5, 1.0), 0.0).astype(bf16)
    rows = mm(hot, qkv_ref[...], NT).astype(bf16)
    for h, own in enumerate((own0, own1)):
        own[:QKV] = rows[h * QKV : (h + 1) * QKV]
        own[QKV:] = out_ref[pl.ds(pl.multiple_of((core ^ h) * 128, 128), 128)]


def feed_rows_kernel(core_ref, up_ref, down_ref, own0, own1):
    core = core_ref[0]
    hot, _ = hot_rows(2 * HALF, lambda row: row ^ (core * HALF))
    rows = mm(jnp.where(hot, 1.0, 0.0).astype(bf16), up_ref[...], NT).astype(bf16)
    for h, own in enumerate((own0, own1)):
        own[0] = rows[h * HALF : (h + 1) * HALF]
        own[1] = down_ref[pl.ds(pl.multiple_of((core ^ h) * HALF, HALF), HALF)]


def attn_rows(core, qkv, out, after):
    half = (shape((HALF, D), bf16), whole(HALF, D))
    ins = [(qkv, whole(D, 2 * QKV)), (out, whole(256, D))]
    return run(attn_rows_kernel, "attn_rows", 1, ins, [half, half], (), after, [core], 1e9, 4e6)


def feed_rows(core, up, down, after):
    half = (shape((2, HALF, D), bf16), whole(2, HALF, D))
    ins = [(up, whole(D, 2 * HALF)), (down, whole(2 * HALF, D))]
    return run(feed_rows_kernel, "feed_rows", 1, ins, [half, half], (), after, [core], 2e9, 8e6)


def attend_kernel(len_ref, x_ref, mode_ref, wa_ref, wb_ref, tbl_ref, e_ref, *rest):
    n1_ref, packed_ref, heads_ref, probs_ref, w_all, kb_all, sems = rest if len(rest) == 7 else (None, *rest)
    w = pl.program_id(0)

    @pl.when(w == 0)
    def _():
        loads = Loads(sems)
        loads.add(wa_ref.at[:QKV], w_all.at[:QKV])
        loads.add(wb_ref.at[:QKV], w_all.at[QKV:])
        loads.start()
        for p in range(2):
            kb_all[p] = mm(e_ref[...], tbl_ref[p]).astype(bf16)
        loads.wait()

    if n1_ref is None:
        x = x_ref[...]
    else:
        hat, _ = ln_parts(x_ref[...].astype(f32))
        x = (hat * (1.0 + mode_ref[1:2]) + mode_ref[0:1]).astype(bf16)
        n1_ref[...] = x
    pk = mm(x, w_all[...], NT).astype(bf16)
    packed_ref[...] = pk
    lane = lax.broadcasted_iota(jnp.int32, (WIN, 128), 1)
    low = lane < 64
    frame = lax.broadcasted_iota(jnp.int32, (WIN, 128), 0) // (WH * WW)
    mask_lane = (lane & 63) == 2 * NOFF
    hide = jnp.where(frame < len_ref[w], 0.0, -1e30).astype(bf16)
    for p in range(2):
        q = pk[:, p * QKV : p * QKV + 128]
        k = pk[:, p * QKV + 128 : p * QKV + 256]
        v = pk[:, p * QKV + 256 : p * QKV + 384]
        kb = jnp.where(mask_lane, hide, kb_all[p])
        v_rows = v.T
        outs = []
        for i in range(2):
            mine = low if i == 0 else ~low
            s = mm(jnp.where(mine, k, kb), jnp.where(mine, q, e_ref[...]), NT)
            ex = jnp.exp(s - jnp.max(s, axis=0, keepdims=True))
            pr = (ex * (1.0 / jnp.sum(ex, axis=0, keepdims=True))).astype(bf16)
            probs_ref[2 * p + i] = pr
            outs.append(mm(v_rows, pr)[i * HD : (i + 1) * HD])
        heads_ref[:, p * 128 : (p + 1) * 128] = jnp.concatenate(outs, axis=0).T.astype(bf16)


def attend(lengths, source, modes, weight, table, query_hot, after=()):
    count = lengths.shape[0]
    rows = count * WIN
    first = source.ndim == 3
    outs = [
        (shape((rows, 2 * QKV), bf16), rows_of(2 * QKV)),
        (shape((rows, 256), bf16), rows_of(256)),
        (shape((count * 4, WIN, WIN), bf16), pl.BlockSpec((4, WIN, WIN), lambda i, l: (i, 0, 0))),
    ]
    if first:
        outs = [(near((rows, D), bf16), rows_of(D))] + outs
    return run(
        attend_kernel,
        "attend",
        count,
        [
            (source, window_of(WIN, D) if first else rows_of(D)),
            (modes, window_of(6, D)),
            (weight[0], HBM),
            (weight[1], HBM),
            (table, whole(2, 128, 128)),
            (query_hot, whole(WIN, 128)),
        ],
        outs,
        [pltpu.VMEM((2 * QKV, D), bf16), pltpu.VMEM((2, WIN, 128), bf16), pltpu.SemaphoreType.DMA((2,))],
        after,
        [lengths],
        9e9,
        12e6,
    )


def middle_kernel(h0, h1, h2, h3, w0, w1, w2, w3, w4, w5, w6, w7, tok, cot, mode, attn_ref, mid_ref, n2_ref, di_ref, w_all, sems):
    @pl.when(pl.program_id(0) == 0)
    def _():
        loads = Loads(sems)
        for i, ref in enumerate((w0, w1, w2, w3, w4, w5, w6, w7)):
            loads.add(ref.at[QKV:], w_all.at[pl.ds(i * 128, 128)])
        loads.start()
        loads.wait()

    heads = jnp.concatenate([h0[...], h1[...], h2[...], h3[...]], axis=1)
    attn = mm(heads, w_all[...])
    attn_ref[...] = attn.astype(bf16)
    middle = tok[...].astype(f32) + mode[2:3] * attn
    mid_ref[...] = middle
    hat, _ = ln_parts(middle)
    n2_ref[...] = (hat * (1.0 + mode[4:5]) + mode[3:4]).astype(bf16)
    di_ref[...] = (mode[5:6] * cot[...].astype(f32)).astype(bf16)


def middle_step(heads, weights, tokens, cotangent, modes, after=()):
    count = tokens.shape[0]
    rows = count * WIN
    return run(
        middle_kernel,
        "middle",
        count,
        [(h, rows_of(256)) for h in heads]
        + [(half, HBM) for pair in weights for half in pair]
        + [(tokens, window_of(WIN, D)), (cotangent, window_of(WIN, D)), (modes, window_of(6, D))],
        [(shape((rows, D), kind), rows_of(D)) for kind in (bf16, f32)] + [(near((rows, D), bf16), rows_of(D))] * 2,
        [pltpu.VMEM((D, D), bf16), pltpu.SemaphoreType.DMA((8,))],
        after,
        flops=2.7e9,
        moved=22e6,
    )


CHUNK = 256


def feed_kernel(places, n2, di, up0, dn0, up1, dn1, hid_hbm, pre_hbm, g0_hbm, g1_hbm, weight, hid, pre, grad, in_sems, out_sems):
    loads, stores = Loads(in_sems), Loads(out_sems)
    for i, ref in enumerate((up0, dn0, up1, dn1)):
        loads.add(ref.at[places[i]], weight.at[i // 2, i % 2])
    for i in (2, 3, 0, 1):
        loads.copies[i].start()

    def store(from_ref, to_ref):
        stores.add(from_ref, to_ref).start()

    for h, g_hbm in ((1, g1_hbm), (0, g0_hbm)):
        units = pl.ds(h * HALF, HALF)
        loads.copies[2 * h].wait()
        loads.copies[2 * h + 1].wait()
        for i in range(n2.shape[0] // CHUNK):
            rows = pl.ds(i * CHUNK, CHUNK)
            v = mm(n2[rows], weight[h, 0], NT)
            hg = mm(di[rows], weight[h, 1], NT)
            v2 = v * v
            t = jnp.tanh(v * (C0 + (C0 * C1) * v2))
            share = 0.5 + 0.5 * t
            hid[h, rows] = (v * share).astype(bf16)
            slope = share + (0.5 * v) * (1.0 - t * t) * (C0 + (3.0 * C0 * C1) * v2)
            pre[h, rows] = (slope * hg).astype(bf16)
        store(hid.at[h], hid_hbm.at[:, units])
        store(pre.at[h], pre_hbm.at[:, units])
        grad[h, 1] = mm(hid[h], di[...], TN).astype(bf16)
        store(grad.at[h, 1], g_hbm.at[1])
        grad[h, 0] = mm(pre[h], n2[...], TN).astype(bf16)
        store(grad.at[h, 0], g_hbm.at[0])
    stores.wait()


def feed(normed, down_in, weight, after=()):
    rows = normed.shape[0]
    halves = [array for half in weight for array, _ in half]
    places = [place for half in weight for _, place in half]
    return run(
        partial(feed_kernel, places),
        "feed",
        1,
        [(normed, VMEM), (down_in, VMEM)] + [(array, HBM) for array in halves],
        [(shape((rows, 2 * HALF), bf16), HBM)] * 2 + [(shape((2, HALF, D), bf16), HBM)] * 2,
        [pltpu.VMEM((2, 2, HALF, D), bf16)]
        + [pltpu.VMEM((2, rows, HALF), bf16)] * 2
        + [pltpu.VMEM((2, 2, HALF, D), bf16), pltpu.SemaphoreType.DMA((4,)), pltpu.SemaphoreType.DMA((8,))],
        after,
        vmem=32,
    )


def unit_sums(sources, pieces, places, weight, acc, sems):
    w = pl.program_id(0)

    def span(i):
        return slice(i % 2 * HALF, (i % 2 + 1) * HALF)

    @pl.when(w == 0)
    def _():
        loads = Loads(sems)
        for i, piece in enumerate(pieces):
            loads.add(piece.at[places[i]], weight.at[pl.ds(i * HALF, HALF)])
        loads.start()
        for i, copy in enumerate(loads.copies):
            copy.wait()
            term = mm(sources[i // 2][:, span(i)], weight[i * HALF : (i + 1) * HALF])
            acc[...] = term if i == 0 else acc[...] + term

    @pl.when(w > 0)
    def _():
        source = jnp.concatenate([ref[...] for ref in sources], axis=1)
        acc[...] = mm(source, weight[...])


def turn_kernel(places, p0, p1, p2, p3, w0, w1, w2, w3, w4, w5, w6, w7, mid_ref, attn_ref, cot_ref, mode_ref, *rest):
    mg_ref, oi_ref, sum_ref, weight, acc, sems = rest
    unit_sums((p0, p1, p2, p3), (w0, w1, w2, w3, w4, w5, w6, w7), places, weight, acc, sems)
    ng = acc[...]
    hat, rstd = ln_parts(mid_ref[...])
    mg = cot_ref[...].astype(f32) + ln_back(ng, mode_ref[4:5], hat, rstd)
    mg_ref[...] = mg
    oi_ref[...] = (mode_ref[2:3] * mg).astype(bf16)
    sum_ref[0:1] = jnp.sum(mg * attn_ref[...].astype(f32), axis=0, keepdims=True)
    sum_ref[1:2] = jnp.sum(ng, axis=0, keepdims=True)
    sum_ref[2:3] = jnp.sum(ng * hat, axis=0, keepdims=True)


def out_kernel(places, p0, p1, p2, p3, w0, w1, w2, w3, w4, w5, w6, w7, mid_ref, cot_ref, mode_ref, *rest):
    out_ref, sum_ref, weight, acc, sems = rest
    unit_sums((p0, p1, p2, p3), (w0, w1, w2, w3, w4, w5, w6, w7), places, weight, acc, sems)
    mlp = acc[...]
    out_ref[...] = (mid_ref[...] + mode_ref[5:6] * mlp).astype(bf16)
    sum_ref[...] = jnp.sum(cot_ref[...].astype(f32) * mlp, axis=0, keepdims=True)


def of_units(arrays, weights, which):
    halves = [half[which] for pair in weights for half in pair]
    ins = [(array, rows_of(2 * HALF)) for array in arrays] + [(array, HBM) for array, _ in halves]
    scratch = [pltpu.VMEM((8 * HALF, D), bf16), pltpu.VMEM((WIN, D), f32), pltpu.SemaphoreType.DMA((8,))]
    return ins, scratch, [place for _, place in halves]


def turn_step(pre, weights, middle, attn_out, cotangent, modes, after=()):
    count = cotangent.shape[0]
    rows = count * WIN
    ins, scratch, places = of_units(pre, weights, 0)
    return run(
        partial(turn_kernel, places),
        "turn",
        count,
        ins
        + [(middle, rows_of(D)), (attn_out, rows_of(D)), (cotangent, window_of(WIN, D)), (modes, window_of(6, D))],
        [
            (shape((rows, D), f32), rows_of(D)),
            (near((rows, D), bf16), rows_of(D)),
            (shape((count, 3, D), f32), window_of(3, D)),
        ],
        scratch,
        after,
        vmem=36,
        flops=10.7e9,
        moved=35e6,
    )


def out_step(hid, weights, middle, cotangent, modes, after=()):
    count = cotangent.shape[0]
    ins, scratch, places = of_units(hid, weights, 1)
    return run(
        partial(out_kernel, places),
        "output",
        count,
        ins + [(middle, rows_of(D)), (cotangent, window_of(WIN, D)), (modes, window_of(6, D))],
        [(shape((count, WIN, D), bf16), window_of(WIN, D)), (shape((count, 1, D), f32), window_of(1, D))],
        scratch,
        after,
        vmem=36,
        flops=10.7e9,
        moved=30e6,
    )


def attend_back_kernel(
    oi_ref, o0, o1, pk_ref, pr_ref, e_ref, n1_ref, oi_all, ho_hbm, pg_ref, g0_ref, g1_ref, rel_ref, *scratch
):
    pg_all, t_all, ow, ho_ref, sems = scratch
    w = pl.program_id(0)
    loads = Loads(sems)
    weights = [loads.add(o.at[QKV:], ow.at[pl.ds(i * 128, 128)]) for i, o in enumerate((o0, o1))]
    heads = loads.add(ho_hbm, ho_ref)

    @pl.when(w == 0)
    def _():
        loads.start()
        t_all[...] = jnp.zeros_like(t_all)
        for copy in weights:
            copy.wait()

    hg = mm(oi_ref[...], ow[...], NT).astype(bf16)
    pk = pk_ref[...]
    low = lax.broadcasted_iota(jnp.int32, (WIN, 128), 1) < 64
    for p in range(2):
        q = pk[:, p * QKV : p * QKV + 128]
        k = pk[:, p * QKV + 128 : p * QKV + 256]
        v = pk[:, p * QKV + 256 : p * QKV + 384]
        do = hg[:, p * 128 : (p + 1) * 128]
        k_rows = k.T
        dv, dq, dk = [], [], []
        for i in range(2):
            mine = low if i == 0 else ~low
            qa = jnp.where(mine, q, e_ref[...])
            dp = mm(jnp.where(mine, v, jnp.zeros_like(v)), do, NT)
            prl = pr_ref[2 * p + i]
            pr = prl.astype(f32)
            t = pr * dp
            ds = (t - pr * jnp.sum(t, axis=0, keepdims=True)).astype(bf16)
            dv.append(mm(prl, do))
            dq.append(mm(k_rows, ds)[i * HD : (i + 1) * HD])
            dk.append(mm(ds, qa))
        dq = jnp.concatenate(dq, axis=0).T
        block = jnp.concatenate(
            [dq, jnp.where(low, dk[0], dk[1]), jnp.where(low, dv[0], dv[1])], axis=1
        ).astype(bf16)
        pg_ref[:, p * QKV : (p + 1) * QKV] = block
        pg_all[pl.ds(pl.multiple_of(w * WIN, WIN), WIN), p * QKV : (p + 1) * QKV] = block
        t_all[p] += jnp.where(low, dk[1], dk[0])

    @pl.when(w == pl.num_programs(0) - 1)
    def _():
        heads.wait()
        go = mm(ho_ref[...], oi_all[...], TN).astype(bf16)
        gq = mm(pg_all[...], n1_ref[...], TN).astype(bf16)
        for p, g_ref in enumerate((g0_ref, g1_ref)):
            g_ref[:QKV] = gq[p * QKV : (p + 1) * QKV]
            g_ref[QKV:] = go[p * 128 : (p + 1) * 128]
        hot = e_ref[...].astype(f32)
        for p in range(2):
            sums = lax.dot_general(hot, t_all[p], TN, precision=precise, preferred_element_type=f32)
            rel_ref[p] = sums[:32]


def attend_back(out_in, weight, packed, probs, query_hot, normed, heads, after=()):
    rows = normed.shape[0]
    return run(
        attend_back_kernel,
        "attend_back",
        rows // WIN,
        [
            (out_in, rows_of(D)),
            (weight[0], HBM),
            (weight[1], HBM),
            (packed, rows_of(2 * QKV)),
            (probs, pl.BlockSpec((4, WIN, WIN), lambda i: (i, 0, 0))),
            (query_hot, whole(WIN, 128)),
            (normed, VMEM),
            (out_in, VMEM),
            (heads, HBM),
        ],
        [
            (shape((rows, 2 * QKV), bf16), rows_of(2 * QKV)),
            (shape((HALF, D), bf16), whole(HALF, D)),
            (shape((HALF, D), bf16), whole(HALF, D)),
            (shape((2, 32, 128), f32), whole(2, 32, 128)),
        ],
        [pltpu.VMEM((rows, 2 * QKV), bf16), pltpu.VMEM((2, WIN, 128), f32), pltpu.VMEM((256, D), bf16)]
        + [pltpu.VMEM((rows, 256), bf16), pltpu.SemaphoreType.DMA((3,))],
        after,
        flops=13e9,
        moved=20e6,
    )


def last_kernel(p0, p1, p2, p3, w0, w1, w2, w3, w4, w5, w6, w7, tok_ref, mode_ref, mg_ref, out_ref, sum_ref, w_all, acc, sems):
    @pl.when(pl.program_id(0) == 0)
    def _():
        loads = Loads(sems)
        for i, ref in enumerate((w0, w1, w2, w3, w4, w5, w6, w7)):
            loads.add(ref.at[:QKV], w_all.at[pl.ds(i * QKV, QKV)])
        loads.start()
        for i, src in enumerate((p0, p1, p2, p3)):
            loads.copies[2 * i].wait()
            loads.copies[2 * i + 1].wait()
            term = mm(src[...], w_all[i * 2 * QKV : (i + 1) * 2 * QKV])
            acc[...] = term if i == 0 else acc[...] + term

    @pl.when(pl.program_id(0) > 0)
    def _():
        acc[...] = mm(jnp.concatenate([p0[...], p1[...], p2[...], p3[...]], axis=1), w_all[...])

    ng = acc[...]
    hat, rstd = ln_parts(tok_ref[...].astype(f32))
    out_ref[...] = (mg_ref[...] + ln_back(ng, mode_ref[1:2], hat, rstd)).astype(bf16)
    sum_ref[0:1] = jnp.sum(ng, axis=0, keepdims=True)
    sum_ref[1:2] = jnp.sum(ng * hat, axis=0, keepdims=True)


def last_step(packed_grads, weights, tokens, modes, middle_grad, after=()):
    count = tokens.shape[0]
    return run(
        last_kernel,
        "last",
        count,
        [(array, rows_of(2 * QKV)) for array in packed_grads]
        + [(half, HBM) for pair in weights for half in pair]
        + [(tokens, window_of(WIN, D)), (modes, window_of(6, D)), (middle_grad, rows_of(D))],
        [(shape((count, WIN, D), bf16), window_of(WIN, D)), (shape((count, 2, D), f32), window_of(2, D))],
        [pltpu.VMEM((8 * QKV, D), bf16), pltpu.VMEM((WIN, D), f32), pltpu.SemaphoreType.DMA((8,))],
        after,
        flops=8e9,
        moved=24e6,
    )


def merge_kernel(sums, count, *refs):
    i = pl.program_id(0)
    refs = list(refs)
    outs = refs[len(refs) - len(sums) :]
    for spans, out in zip(sums, outs):
        value = None
        for first, last in spans:
            term = refs.pop(0)[...].astype(f32)
            if (first, last) != (0, count):
                term = jnp.where((i >= first) & (i < last), term, 0.0)
            value = term if value is None else value + term
        out[...] = value.astype(bf16)


def merge(*sums, rows=HALF, after=()):
    block = min(256, rows)
    ins, spans = [], []
    for terms in sums:
        spans.append([])
        for array, place, start, *limits in terms:
            first, last = [limit // block for limit in (limits or (0, rows))]
            start = start // block

            def at(i, start=start, first=first, last=last):
                return jnp.clip(i, first, last - 1) + start

            if place is None:
                spec = pl.BlockSpec((block, D), lambda i, at=at: (at(i), 0))
            else:
                spec = pl.BlockSpec((None, block, D), lambda i, p=place, at=at: (p, at(i), 0))
            ins.append((array, spec))
            spans[-1].append((first, last))
    out = (shape((rows, D), bf16), pl.BlockSpec((block, D), lambda i: (i, 0)))
    return run(partial(merge_kernel, spans, rows // block), "merge", rows // block, ins, [out] * len(sums), (), after)


def parts_kernel(count, only, z_ref, *refs):
    which_sum = pl.program_id(0) % (1 + max([0] + [w for w in only if w is not None]))
    terms = len(only)
    for k in range(count):
        value = None
        for ref, which in zip(refs[k * terms : (k + 1) * terms], only):
            term = ref[...].astype(f32)
            if which is not None:
                term = jnp.where(which_sum == which, term, 0.0)
            value = term if value is None else value + term
        refs[count * terms + k][...] = value.astype(bf16)


def merge_parts(terms, z, count, outputs):
    size = HALF // count
    sums = 2 if any(type(term) is tuple for term in terms) else 1
    ins, only = [], []
    for j in range(outputs):
        for term in terms:
            array, which = term if type(term) is tuple else (term, None)
            dims = array.array.ndim if isinstance(array, Moved) else array.ndim

            def at(i, zr, j=j):
                return zr[0] ^ (i // sums * outputs + j)

            if dims == 3:
                spec = pl.BlockSpec((None, size, D), lambda i, zr, at=at: (i % sums, at(i, zr), 0))
            else:
                spec = pl.BlockSpec((size, D), lambda i, zr, at=at: (at(i, zr), 0))
            ins.append((array, spec))
            only.append(which)
    grid = sums * count // outputs
    outs = [(shape((grid * size, D), bf16), pl.BlockSpec((size, D), lambda i, zr: (i, 0)))] * outputs
    return run(partial(parts_kernel, outputs, only[: len(terms)]), "merge_parts", grid, ins, outs, (), (), [z])


def attn_final_kernel(place_ref, a_ref, b_ref, qkv_ref, out_ref, rows, hot):
    core, z = place_ref[0], place_ref[1]
    size = HALF // 4

    @pl.when(pl.program_id(0) == 0)
    def _():
        match, row = hot_rows(2 * QKV, qkv_source(core))
        inner = jnp.where(row >= QKV, row - QKV, row)
        hot[...] = jnp.where(match, jnp.where(inner < 128, HD**-0.5, 1.0), 0.0).astype(bf16)

    for h, ref in enumerate((a_ref, b_ref)):
        for k in range(4):
            part_at = z ^ k
            block = ref[k * size : (k + 1) * size]

            @pl.when(part_at < 3)
            def _():
                rows[pl.ds(pl.multiple_of(h * QKV + part_at * size, size), size)] = block

            @pl.when(part_at == 3)
            def _():
                out_ref[pl.ds(pl.multiple_of((core ^ h) * size, size), size)] = block.astype(f32)

    qkv_ref[...] = mm(rows[...], hot[...], TN)


def columns_of(rows):
    return pl.BlockSpec((rows, 256), lambda i, *_: (0, i))


def attn_final(place, a, b):
    ins = [(a, columns_of(HALF)), (b, columns_of(HALF))]
    outs = [
        (shape((D, 2 * QKV), f32), pl.BlockSpec((256, 2 * QKV), lambda i, *_: (i, 0))),
        (shape((256, D), f32), columns_of(256)),
    ]
    scratch = [pltpu.VMEM((2 * QKV, 256), bf16), pltpu.VMEM((2 * QKV, 2 * QKV), bf16)]
    return run(attn_final_kernel, "attn_final", D // 256, ins, outs, scratch, (), [place])


def feed_final_kernel(place_ref, *refs):
    up_ref, down_ref, rows, hot = refs[4:]
    core, z = place_ref[0], place_ref[1]
    size = HALF // 4

    @pl.when(pl.program_id(0) == 0)
    def _():
        hot[...] = jnp.where(hot_rows(2 * HALF, lambda row: row ^ (core * HALF))[0], 1.0, 0.0).astype(bf16)

    for h in range(2):
        for k, (ref, first) in enumerate(((refs[2 * h], 0), (refs[2 * h + 1], 0), (refs[2 * h], 2), (refs[2 * h + 1], 2))):
            start = (z ^ k) * size
            rows[pl.ds(pl.multiple_of(h * HALF + start, size), size)] = ref[first * size : (first + 1) * size]
            block = ref[(first + 1) * size : (first + 2) * size].astype(f32)
            down_ref[pl.ds(pl.multiple_of((core ^ h) * HALF + start, size), size)] = block
    up_ref[...] = mm(rows[...], hot[...], TN)


def feed_final(place, even, odd, other_even, other_odd):
    ins = [(v, columns_of(HALF)) for v in (even, odd, other_even, other_odd)]
    outs = [
        (shape((D, 2 * HALF), f32), pl.BlockSpec((256, 2 * HALF), lambda i, *_: (i, 0))),
        (shape((2 * HALF, D), f32), columns_of(2 * HALF)),
    ]
    scratch = [pltpu.VMEM((2 * HALF, 256), bf16), pltpu.VMEM((2 * HALF, 2 * HALF), bf16)]
    return run(feed_final_kernel, "feed_final", D // 256, ins, outs, scratch, (), [place])


def mode_shares_kernel(m0, m1, m2, m3, rel_ref, ada_ref, low_ref, s0, s1, s2, s3, rows):
    count = m0.shape[0]
    for r, ref in enumerate((m0, m1, m2, m3)):
        rows[r * count : (r + 1) * count] = ref[...]
    low = rows[...].astype(bf16)
    low_ref[...] = low
    cond = mm(low, ada_ref[...], NT)
    for r, ref in enumerate((s0, s1, s2, s3)):
        ref[:, :D] = cond
        ref[:, D:] = rel_ref[r]


def mode_shares(messages, rel_part, ada_weight):
    count, columns = messages[0].shape
    rows = 4 * count
    ins = [(v, whole(count, columns)) for v in messages]
    ins += [(rel_part, whole(4, rows, 128)), (ada_weight, whole(D, columns))]
    outs = [(shape((rows, columns), bf16), whole(rows, columns))] + [(shape((rows, D + 128), f32), whole(rows, D + 128))] * 4
    return run(mode_shares_kernel, "mode_shares", 1, ins, outs, [pltpu.VMEM((rows, columns), f32)])


def mode_rows_kernel(mp_ref, low_ref, s0, s1, s2, s3, slope_ref, cond_ref, out_ref):
    rows, columns = low_ref.shape
    count = rows // 4
    mp = mp_ref[0]
    moved = [s0[:, :D]]
    for k, ref in ((1, s1), (2, s2), (3, s3)):
        blocks = [ref[(r ^ k) * count : ((r ^ k) + 1) * count, :D] for r in range(4)]
        moved.append(jnp.concatenate(blocks, axis=0))
    cond = (moved[0] + moved[1]) + (moved[2] + moved[3])
    value = (cond * slope_ref[...]).astype(bf16)
    row = lax.broadcasted_iota(jnp.int32, (rows, rows), 0)
    col = lax.broadcasted_iota(jnp.int32, (rows, rows), 1)
    hot = jnp.where(col == row ^ (mp * count), 1.0, 0.0).astype(bf16)
    out_ref[:, :columns] = low_ref[...]
    out_ref[:, columns : columns + D] = mm(hot, value).astype(bf16)
    out_ref[:, columns + D : columns + D + 128] = (s0[:, D:] + s1[:, D:] + s2[:, D:] + s3[:, D:]).astype(bf16)
    out_ref[:, columns + D + 128 :] = cond_ref[...]


def mode_rows(mp, low, shares, slope, cond):
    rows, columns = low.shape
    width = columns + 2 * (D + 128)
    ins = [(low, whole(rows, columns))] + [(v, whole(rows, D + 128)) for v in shares]
    ins += [(slope, whole(rows, D)), (cond, whole(rows, D + 128))]
    outs = [(shape((rows, width), bf16), whole(rows, width))]
    return run(mode_rows_kernel, "mode_rows", 1, ins, outs, (), (), [mp])[0]


def mode_final_kernel(dp_ref, *refs):
    *parts, ada_ref, bias_ref, class_ref, rel_ref, rows = refs
    size = parts[0].shape[0]
    columns = ada_ref.shape[1]
    marks = [0, columns, columns + D, columns + D + 128, columns + 2 * D + 128, columns + 2 * D + 256]
    for k, ref in enumerate(parts):
        rows[pl.ds(pl.multiple_of((dp_ref[0] ^ k) * size, size), size)] = ref[...]
    modes, classes, rel, cond, index = [rows[:, i:j] for i, j in zip(marks, marks[1:])]
    ada_ref[...] = mm(cond, modes, TN)
    bias_ref[...] = jnp.sum(modes.astype(f32), axis=0, keepdims=True)
    lane = lax.broadcasted_iota(jnp.int32, index.shape, 1).astype(f32)
    hot = jnp.where(lane == index[:, :1].astype(f32), 1.0, 0.0).astype(bf16)
    class_ref[...] = mm(hot, classes, TN)[: class_ref.shape[0]]
    total = rel[:size].astype(f32)
    for i in range(1, len(parts)):
        total = total + rel[i * size : (i + 1) * size].astype(f32)
    rel_ref[...] = total


def mode_final(dp, parts, columns, class_count):
    size, width = parts[0].shape
    ins = [(v, whole(size, width)) for v in parts]
    outs = [(shape(dims, f32), whole(*dims)) for dims in ((D, columns), (1, columns), (class_count, D), (size, 128))]
    scratch = [pltpu.VMEM((len(parts) * size, width), bf16)]
    return run(mode_final_kernel, "mode_final", 1, ins, outs, scratch, (), [dp], vmem=32)


def silu_plain(values):
    return values / (1.0 + jnp.exp(-values))


def condition(timesteps, classes, class_table):
    half_width = class_table.shape[1] // 2
    frequency = jnp.exp(
        -math.log(10000.0) * jnp.arange(half_width).astype(class_table.dtype) / half_width
    )
    phase_angle = timesteps.astype(class_table.dtype)[..., None] * frequency
    sinusoid = jnp.concatenate([jnp.cos(phase_angle), jnp.sin(phase_angle)], axis=-1)
    onehot = (classes[..., None] == jnp.arange(class_table.shape[0])).astype(class_table.dtype)
    lookup = jnp.einsum("mwc,cd->mwd", onehot, class_table, precision=precise)
    return sinusoid + lookup


SPANS = ((0, 0, WT), (WT, 2 * WT - 1, WH), (WT + WH, 2 * WT + 2 * WH - 2, WW))


def place_hot():
    spot = np.arange(WIN)
    hot = np.zeros((WIN, NOFF), np.float32)
    for (start, _, _), where in zip(SPANS, (spot // (WH * WW), (spot // WW) % WH, spot % WW)):
        hot[spot, start + where] = 1.0
    return hot


def query_side():
    half = np.zeros((WIN, 64), np.float32)
    half[:, :NOFF] = place_hot()
    half[:, NOFF : 2 * NOFF] = place_hot()
    half[:, 2 * NOFF] = 1.0
    return np.concatenate([half, half], axis=1)


def offset_hot(rows, copies):
    hot = np.zeros((2 * NOFF - 3, rows, 64), np.float32)
    for start, begin, length in SPANS:
        for key in range(length):
            for query in range(length):
                for copy in range(copies):
                    hot[begin + query - key + length - 1, start + key, copy * NOFF + start + query] = 1.0
    return hot


def key_tables(rel, core):
    value = jnp.einsum("hr,rkq->hkq", rel.reshape(16, -1), offset_hot(64, 2), precision=precise)
    top = lax.reduce_precision(value, 8, 7)
    value = jnp.where(jnp.arange(64) < NOFF, top, value - top).astype(bf16)
    value = value.reshape(4, 2, 2, 64, 64)
    value = jnp.where(core == 0, value, value[:, ::-1])
    value = jnp.concatenate([value[:, :, 1], value[:, :, 0]], axis=-1)
    return jnp.pad(value, ((0, 0), (0, 0), (0, 64), (0, 0)))


def rel_sums(grids, core):
    grids = jnp.where(core == 0, grids, grids[:, ::-1])
    grids = grids.reshape(4, 2, 32, 2, 64)
    grids = jnp.stack([grids[:, :, :, 1], grids[:, :, :, 0]], axis=2).reshape(16, 32, 64)
    return jnp.einsum("hkq,rkq->hr", grids, offset_hot(32, 1), precision=precise).reshape(4, 4, -1)


def local_windows(
    sizes,
    tokens,
    cotangent,
    qkv_weight,
    out_weight,
    up_weight,
    down_weight,
    ada_weight,
    ada_bias,
    rel_bias,
    class_table,
    lengths,
    timesteps,
    classes,
):
    n_z, n_mp = sizes
    n_dp = 2 * n_z
    micro = tokens.shape[0]
    mp = lax.axis_index("mp")
    z = lax.axis_index("z")
    core = lax.axis_index("core")

    def swap_mp(bit):
        return lambda v: lax.ppermute(v, "mp", [(i, i ^ bit) for i in range(n_mp)])

    def swap_dp(bit):
        return lambda v: lax.ppermute(v, ("z", "core"), [(i, i ^ bit) for i in range(n_dp)])

    px, py, pd = swap_mp(1), swap_mp(2), swap_mp(3)
    pc = swap_dp(1)
    by_rel = [lambda v: v, px, py, pd]

    def cat(a, b, axis=0):
        return jnp.concatenate([a, b], axis=axis)

    pre_cond = condition(timesteps, classes, class_table)
    cond_low = silu_plain(pre_cond).astype(bf16)
    mode_cols = jnp.einsum("mwd,de->mwe", cond_low, ada_weight, preferred_element_type=f32) + ada_bias.astype(f32)
    order = jnp.arange(4) ^ mp
    rel_row = jnp.pad(rel_bias, ((0, 0), (0, 128 - rel_bias.shape[1])))
    messages = [
        by_rel[r](cat(lax.dynamic_index_in_dim(mode_cols, mp ^ r, axis=1, keepdims=False), rel_row, 1))
        for r in range(4)
    ]
    messages = jnp.stack(messages)
    columns = mode_cols.shape[-1]
    modes = jnp.take(messages[:, :, :columns], order, axis=0)
    modes = modes.transpose(1, 0, 2).reshape(micro, 6, D)
    tables = key_tables(messages[:, :, columns : columns + rel_bias.shape[1]], core)
    own_lengths = lax.dynamic_index_in_dim(lengths, mp, axis=1, keepdims=False)

    core_row = core.reshape(1)
    query_hot = jnp.asarray(query_side(), bf16)
    packed, heads, probs = [None] * 4, [None] * 4, [None] * 4

    attn_own = list(attn_rows(core_row, qkv_weight, out_weight, [mode_cols]))
    (attn_own[0],) = hold(attn_own[:1], [messages])
    ax, ay = px(attn_own[0]), py(attn_own[0])
    normed_one, packed[0], heads[0], probs[0] = attend(own_lengths, tokens, modes, attn_own, tables[0], query_hot)
    feed_own = list(feed_rows(core_row, up_weight, down_weight, [heads[0]]))
    ax, ay = hold([ax, ay], [feed_own[1]])
    adx, ady = py(ax[: HALF // 2]), px(ay[HALF // 2 :])
    attn_w = [attn_own] + [[Moved(v), Moved(pc(v))] for v in (ax, ay)]
    packed[1], heads[1], probs[1] = attend(
        own_lengths, normed_one, modes, attn_w[1], tables[1], query_hot, [feed_own[1]]
    )
    adx, ady = hold([adx, ady], [heads[1]])
    (feed_own[0],) = hold(feed_own[:1], [adx, ady])
    fx, fy = px(feed_own[0]), py(feed_own[0])
    ad = cat(adx, ady)
    attn_w.append([ad, Moved(pc(ad))])
    for r in (2, 3):
        packed[r], heads[r], probs[r] = attend(
            own_lengths, normed_one, modes, attn_w[r], tables[r], query_hot, [heads[r - 1]]
        )
    attn_out, middle, normed_two, down_in = middle_step(heads, attn_w, tokens, cotangent, modes)

    hid, pre, mine, other = [None] * 4, [None] * 4, [None] * 4, [None] * 4

    def feed_step(r, weight, after):
        hid[r], pre[r], mine[r], sent = feed(normed_two, down_in, weight, after)
        other[r] = pc(sent)

    def pair(r, which):
        return [(mine[r], which, 0), (Moved(other[r]), which, 0)]

    feed_w = [[((v, 0), (v, 1)) for v in feed_own]]
    feed_step(0, feed_w[0], [])
    fx, fy = hold([fx, fy], [hid[0]])
    fu, fd = fx[:1], fy[1:]
    feed_w += [[((Moved(v), 0), (Moved(v), 1)) for v in (u, pc(u))] for u in (fx, fy)]
    feed_step(1, feed_w[1], [hid[0], fu, fd])
    fu, fd = py(fu), px(fd)
    feed_step(2, feed_w[2], [hid[1]])
    fu, fd = arrive([fu, fd], [hid[2]])
    feed_w += [[((Moved(u), 0), (Moved(v), 0)) for u, v in ((fu, fd), (pc(fu), pc(fd)))]]
    (send_x,) = merge(pair(1, 0), after=[fu])
    (send_y,) = merge(pair(2, 1), after=[send_x])
    feed_step(3, feed_w[3], [hid[2], send_y])
    send_x, send_y = arrive([px(send_x), py(send_y)], [hid[3]])
    diag_x, diag_y = merge(pair(3, 0), pair(3, 1), after=[send_x])
    middle_grad, out_in, turn_sums = turn_step(
        pre, feed_w, middle, attn_out, cotangent, modes, [diag_x, diag_y]
    )
    diag_x, diag_y = arrive([px(diag_x), py(diag_y)], [middle_grad])
    last_x, last_y = merge(pair(1, 1) + [(Moved(diag_y), None, 0)], pair(2, 0) + [(Moved(diag_x), None, 0)])
    still = [[[(v.array if isinstance(v, Moved) else v, at) for v, at in half] for half in halves] for halves in feed_w]
    output, out_sums = out_step(hid, still, middle, cotangent, modes, [last_x, last_y])
    last_x, last_y = arrive([px(last_x), py(last_y)], [out_sums])
    z_row = z.reshape(1)
    terms = [mine[0], Moved(other[0])]
    terms += [(Moved(send_x), 0), (Moved(last_y), 0), (Moved(last_x), 1), (Moved(send_y), 1)]
    feed_keep, feed_sent = merge_parts(terms, z_row, n_z, 2)
    z_one, z_two = swap_dp(2), swap_dp(4)

    own_pre = jnp.take(pre_cond.transpose(1, 0, 2), order, axis=0).reshape(4 * micro, D)
    share = 1.0 / (1.0 + jnp.exp(-own_pre))
    class_col = jnp.pad(classes.T.reshape(-1, 1).astype(bf16), ((0, 0), (0, 127)))
    cond_rel = jnp.take(cond_low, order, axis=1).transpose(1, 0, 2).reshape(4 * micro, D)
    slope, cond_rel = hold([share * (1.0 + own_pre * (1.0 - share)), cat(cond_rel, class_col, 1)])

    attn_w = [[v.array if isinstance(v, Moved) else v for v in halves] for halves in attn_w]
    packed_grad, rel_grid, a_mine, a_other = [None] * 4, [None] * 4, [None] * 4, [None] * 4

    def back_step(r, after):
        packed_grad[r], a_mine[r], sent, rel_grid[r] = attend_back(
            out_in, attn_w[r], packed[r], probs[r], query_hot, normed_one, heads[r], after
        )
        a_other[r] = pc(sent)

    cut = HALF // 2

    def a_pair(r, start):
        return [(a_mine[r], None, start), (Moved(a_other[r]), None, start)]

    back_step(3, [feed_keep])
    (feed_got,) = arrive([z_one(feed_sent)], [packed_grad[3]])
    (feed_sent,) = merge([(feed_keep, None, cut), (Moved(feed_got), None, cut)], rows=cut)
    back_step(1, [packed_grad[3], feed_sent])
    (feed_two,) = arrive([z_two(feed_sent)], [packed_grad[1]])
    (feed_one,) = merge([(feed_keep, None, 0), (Moved(feed_got), None, 0), (Moved(feed_two), None, 0)], rows=cut)
    a_diag_x, a_diag_y = merge(a_pair(3, 0), a_pair(3, cut), rows=cut, after=[feed_one])
    back_step(2, [a_diag_x, a_diag_y, slope, cond_rel])
    feed_two, a_diag_x, a_diag_y = arrive([z_two(feed_one), px(a_diag_x), py(a_diag_y)], [packed_grad[2]])
    feed_even = cat(feed_one, feed_two)
    (a_last_x,) = merge(a_pair(1, 0) + [(Moved(a_diag_y), None, -cut, cut, HALF)])
    (a_last_y,) = merge(a_pair(2, 0) + [(Moved(a_diag_x), None, 0, 0, cut)], after=[a_last_x])
    back_step(0, [packed_grad[2], a_last_y, feed_even])
    feed_odd, a_last_x, a_last_y = arrive([z_one(feed_even), px(a_last_x), py(a_last_y)], [packed_grad[0]])

    def exchange(parts):
        return [swap_dp(2 * k)(v) for k, v in enumerate(parts) if k]

    attn_parts = merge_parts([a_mine[0], *map(Moved, (a_other[0], a_last_x, a_last_y))], z_row, n_z, n_z)
    token_grads, last_sums = last_step(packed_grad, attn_w, tokens, modes, middle_grad, attn_parts)
    attn_got = exchange(attn_parts)
    feed_other = [pc(feed_even), pc(feed_odd)]
    *attn_got, feed_other[0], feed_other[1] = arrive(attn_got + feed_other, [last_sums])
    (attn_own,) = merge([(v, None, 0) for v in (attn_parts[0], *attn_got)], rows=HALF // n_z)

    place = jnp.stack([core, z])
    mode_grad = jnp.concatenate([last_sums, turn_sums, out_sums], axis=1).reshape(micro, 4, -1).transpose(1, 0, 2)
    messages = [lax.dynamic_index_in_dim(mode_grad, mp ^ r, axis=0, keepdims=False) for r in range(4)]
    rel_grid = hold(rel_grid, [attn_own])
    rel_part = jnp.pad(rel_sums(jnp.stack(rel_grid), core), ((0, 0), (0, 4 * (micro - 1)), (0, 128 - rel_bias.shape[1])))
    grad_up, grad_down = feed_final(place, feed_even, Moved(feed_odd), *map(Moved, feed_other))
    *messages[1:], attn_far = arrive(
        [by_rel[r](messages[r]) for r in (1, 2, 3)] + [swap_dp(6)(attn_own)], [attn_own, grad_up]
    )
    mode_low, *shares = mode_shares(messages, rel_part, ada_weight)
    *shares[1:], attn_two, attn_one = arrive(
        [by_rel[r](shares[r]) for r in (1, 2, 3)] + [swap_dp(4)(attn_own), swap_dp(2)(attn_own)], [attn_far]
    )
    grads = mode_rows(mp.reshape(1), mode_low, shares, slope, cond_rel)
    attn_own = jnp.concatenate([attn_own, attn_one, attn_two, attn_far])
    got = [swap_dp(k)(grads) for k in range(1, n_dp)]
    (attn_other,) = hold([pc(attn_own)], [grads])
    grad_qkv, grad_out = attn_final(place, attn_own, Moved(attn_other))
    got = arrive(got, [grad_qkv])
    grad_ada, grad_ada_bias, class_grad, grad_rel = mode_final(
        (2 * z + core).reshape(1), [grads, *got], columns, class_table.shape[0]
    )
    grad_ada_bias = grad_ada_bias.reshape(-1)
    grad_rel = grad_rel[:4, : rel_bias.shape[1]]

    return (
        output,
        token_grads,
        grad_qkv,
        grad_out,
        grad_up,
        grad_down,
        grad_ada,
        grad_ada_bias,
        grad_rel,
        class_grad,
    )


def layer_norm(values):
    center = values - jnp.mean(values, axis=-1, keepdims=True)
    spread = jnp.mean(center * center, axis=-1, keepdims=True)
    return center * lax.rsqrt(spread + EPS)


def modulate(values, shift, scale):
    return layer_norm(values) * (1.0 + scale) + shift


def gelu_tanh(values):
    return (
        0.5
        * values
        * (
            1.0
            + jnp.tanh(math.sqrt(2.0 / math.pi) * (values + 0.044715 * values * values * values))
        )
    )


def condition_whole(timesteps, classes, class_table):
    half_width = class_table.shape[1] // 2
    frequency = jnp.exp(
        -math.log(10000.0) * jnp.arange(half_width).astype(class_table.dtype) / half_width
    )
    phase_angle = timesteps.astype(class_table.dtype)[..., None] * frequency
    sinusoid = jnp.concatenate([jnp.cos(phase_angle), jnp.sin(phase_angle)], axis=-1)
    onehot = (classes[..., None] == jnp.arange(class_table.shape[0])[None, None, :]).astype(
        class_table.dtype
    )
    lookup = jnp.einsum("mwc,cd->mwd", onehot, class_table, precision=precise)
    return silu_plain(sinusoid + lookup)


def axis_table(rel_part, window_span):
    places = jnp.arange(window_span)
    offsets = places[:, None] - places[None, :] + window_span - 1
    onehot = (offsets[:, :, None] == jnp.arange(2 * window_span - 1)[None, None, :]).astype(
        rel_part.dtype
    )
    return jnp.einsum("hr,abr->hab", rel_part, onehot, precision=precise)


def window_bias(rel_bias):
    frame_part = axis_table(rel_bias[:, : 2 * WT - 1], WT)
    row_part = axis_table(rel_bias[:, 2 * WT - 1 : 2 * WT + 2 * WH - 2], WH)
    column_part = axis_table(rel_bias[:, 2 * WT + 2 * WH - 2 :], WW)
    full_bias = (
        frame_part[:, :, None, None, :, None, None]
        + row_part[:, None, :, None, None, :, None]
        + column_part[:, None, None, :, None, None, :]
    )
    return full_bias.reshape(rel_bias.shape[0], WIN, WIN)


def attention_scores(query_part, key_part, bias_full, masks):
    scores = (
        jnp.einsum("wqhd,wkhd->whqk", query_part, key_part, preferred_element_type=jnp.float32)
        * HD ** (-0.5)
        + bias_full[None]
    )
    return jnp.where(masks[:, None, None, :], scores, -1e30)


def local_general(
    tokens,
    cotangent,
    qkv_weight,
    out_weight,
    up_weight,
    down_weight,
    ada_weight,
    ada_bias,
    rel_bias,
    class_table,
    lengths,
    timesteps,
    classes,
):
    micro_count = tokens.shape[0]
    row_count = tokens.shape[1]
    win_count = lengths.shape[1]
    heads_here = rel_bias.shape[0]
    head_scale = HD ** (-0.5)
    first_row = lax.axis_index("mp") * row_count
    row_window = (first_row + jnp.arange(row_count)) // WIN
    spread_rows = (row_window[:, None] == jnp.arange(win_count)[None, :]).astype(jnp.float32)
    cond_low = condition_whole(timesteps, classes, class_table).astype(jnp.bfloat16)
    mode_cols = jnp.einsum(
        "mwd,de->mwe", cond_low, ada_weight, preferred_element_type=jnp.float32
    ) + ada_bias.astype(jnp.float32)
    mode_all = lax.all_gather(mode_cols, "mp", axis=2, tiled=True)
    bias_full, bias_pull = jax.vjp(window_bias, rel_bias)
    frame_of = jnp.arange(WIN) // (WH * WW)
    grad_qkv = jnp.zeros(qkv_weight.shape, jnp.float32)
    grad_out = jnp.zeros(out_weight.shape, jnp.float32)
    grad_up = jnp.zeros(up_weight.shape, jnp.float32)
    grad_down = jnp.zeros(down_weight.shape, jnp.float32)
    grad_rel = jnp.zeros(rel_bias.shape, jnp.float32)
    mode_parts = []
    outputs = []
    token_grads = []
    for micro_step in range(micro_count):
        mode_rows = jnp.dot(spread_rows, mode_all[micro_step], precision=precise)
        shift_attn, scale_attn, gate_attn, shift_mlp, scale_mlp, gate_mlp = jnp.split(
            mode_rows, 6, axis=1
        )
        inputs = tokens[micro_step].astype(jnp.float32)
        normed_one, pull_one = jax.vjp(modulate, inputs, shift_attn, scale_attn)
        gathered_one = lax.all_gather(normed_one.astype(jnp.bfloat16), "mp", axis=0, tiled=True)
        packed = jnp.dot(gathered_one, qkv_weight, preferred_element_type=jnp.float32).astype(
            jnp.bfloat16
        )
        packed = packed.reshape(win_count, WIN, heads_here, 3, HD)
        query_part = packed[:, :, :, 0]
        key_part = packed[:, :, :, 1]
        value_part = packed[:, :, :, 2]
        masks = frame_of[None, :] < lengths[micro_step][:, None]
        scores = attention_scores(query_part, key_part, bias_full, masks)
        top_score = jnp.max(scores, axis=-1, keepdims=True)
        expo = jnp.exp(scores - top_score)
        total = jnp.sum(expo, axis=-1, keepdims=True)
        log_total = top_score + jnp.log(total)
        probs_low = (expo / total).astype(jnp.bfloat16)
        heads_out = jnp.einsum(
            "whqk,wkhd->wqhd", probs_low, value_part, preferred_element_type=jnp.float32
        ).astype(jnp.bfloat16)
        heads_out = heads_out.reshape(win_count * WIN, heads_here * HD)
        attn_out = lax.psum_scatter(
            jnp.dot(heads_out, out_weight, preferred_element_type=jnp.float32),
            "mp",
            scatter_dimension=0,
            tiled=True,
        )
        middle = inputs + gate_attn * attn_out
        normed_two, pull_two = jax.vjp(modulate, middle, shift_mlp, scale_mlp)
        grad_y = cotangent[micro_step].astype(jnp.float32)
        down_in = (gate_mlp * grad_y).astype(jnp.bfloat16)
        gathered_two = lax.all_gather(normed_two.astype(jnp.bfloat16), "mp", axis=0, tiled=True)
        hidden_pre = jnp.dot(gathered_two, up_weight, preferred_element_type=jnp.float32)
        hidden_low, gelu_pull = jax.vjp(gelu_tanh, hidden_pre)
        hidden_low = hidden_low.astype(jnp.bfloat16)
        mlp_out = lax.psum_scatter(
            jnp.dot(hidden_low, down_weight, preferred_element_type=jnp.float32),
            "mp",
            scatter_dimension=0,
            tiled=True,
        )
        down_all = lax.all_gather(down_in, "mp", axis=0, tiled=True)
        hidden_grad = jnp.einsum(
            "rd,fd->rf", down_all, down_weight, preferred_element_type=jnp.float32
        )
        micro_down = jnp.einsum(
            "rf,rd->fd", hidden_low, down_all, preferred_element_type=jnp.float32
        )
        pre_low = gelu_pull(hidden_grad)[0].astype(jnp.bfloat16)
        micro_up = jnp.einsum(
            "rd,rf->df", gathered_two, pre_low, preferred_element_type=jnp.float32
        )
        normed_two_grad = lax.psum_scatter(
            jnp.einsum("rf,df->rd", pre_low, up_weight, preferred_element_type=jnp.float32),
            "mp",
            scatter_dimension=0,
            tiled=True,
        )
        outputs.append(middle + gate_mlp * mlp_out)
        grad_gate_mlp = grad_y * mlp_out
        resid_grad, grad_shift_mlp, grad_scale_mlp = pull_two(normed_two_grad)
        middle_grad = grad_y + resid_grad
        grad_gate_attn = middle_grad * attn_out
        out_in = (gate_attn * middle_grad).astype(jnp.bfloat16)
        out_all = lax.all_gather(out_in, "mp", axis=0, tiled=True)
        micro_out = jnp.einsum("rc,rd->cd", heads_out, out_all, preferred_element_type=jnp.float32)
        heads_grad = jnp.einsum(
            "rd,cd->rc", out_all, out_weight, preferred_element_type=jnp.float32
        ).astype(jnp.bfloat16)
        heads_grad = heads_grad.reshape(win_count, WIN, heads_here, HD)
        probs = jnp.exp(attention_scores(query_part, key_part, bias_full, masks) - log_total)
        probs_low = probs.astype(jnp.bfloat16)
        value_grad = jnp.einsum(
            "whqk,wqhd->wkhd", probs_low, heads_grad, preferred_element_type=jnp.float32
        )
        probs_grad = jnp.einsum(
            "wqhd,wkhd->whqk", heads_grad, value_part, preferred_element_type=jnp.float32
        )
        score_grad = probs * (probs_grad - jnp.sum(probs * probs_grad, axis=-1, keepdims=True))
        micro_rel = bias_pull(jnp.sum(score_grad, axis=0))[0]
        score_low = (score_grad * head_scale).astype(jnp.bfloat16)
        query_grad = jnp.einsum(
            "whqk,wkhd->wqhd", score_low, key_part, preferred_element_type=jnp.float32
        )
        key_grad = jnp.einsum(
            "whqk,wqhd->wkhd", score_low, query_part, preferred_element_type=jnp.float32
        )
        packed_grad = jnp.stack([query_grad, key_grad, value_grad], axis=3).astype(jnp.bfloat16)
        packed_grad = packed_grad.reshape(win_count * WIN, heads_here * 3 * HD)
        micro_qkv = jnp.einsum(
            "rd,rc->dc", gathered_one, packed_grad, preferred_element_type=jnp.float32
        )
        normed_one_grad = lax.psum_scatter(
            jnp.einsum("rc,dc->rd", packed_grad, qkv_weight, preferred_element_type=jnp.float32),
            "mp",
            scatter_dimension=0,
            tiled=True,
        )
        input_grad, grad_shift_attn, grad_scale_attn = pull_one(normed_one_grad)
        token_grads.append(middle_grad + input_grad)
        row_modes = jnp.concatenate(
            [
                grad_shift_attn,
                grad_scale_attn,
                grad_gate_attn,
                grad_shift_mlp,
                grad_scale_mlp,
                grad_gate_mlp,
            ],
            axis=1,
        )
        mode_parts.append(jnp.einsum("rw,re->we", spread_rows, row_modes, precision=precise))
        local_grads = (micro_qkv, micro_out, micro_rel, micro_up, micro_down)
        grad_qkv = grad_qkv + local_grads[0]
        grad_out = grad_out + local_grads[1]
        grad_rel = grad_rel + local_grads[2]
        grad_up = grad_up + local_grads[3]
        grad_down = grad_down + local_grads[4]
    mode_grad_cols = lax.psum_scatter(jnp.stack(mode_parts), "mp", scatter_dimension=2, tiled=True)
    mode_low = mode_grad_cols.astype(jnp.bfloat16)
    grad_ada = jnp.einsum("mwd,mwe->de", cond_low, mode_low, preferred_element_type=jnp.float32)
    grad_ada_bias = jnp.sum(mode_grad_cols, axis=(0, 1))
    cond_grad = jnp.einsum("mwe,de->mwd", mode_low, ada_weight, preferred_element_type=jnp.float32)
    cond_value, cond_pull = jax.vjp(partial(condition_whole, timesteps, classes), class_table)
    class_total = lax.psum(cond_pull(cond_grad)[0], ("dp", "mp"))
    grad_qkv, grad_out, grad_up, grad_down, grad_rel, grad_ada, grad_ada_bias = lax.psum(
        (grad_qkv, grad_out, grad_up, grad_down, grad_rel, grad_ada, grad_ada_bias), "dp"
    )
    return (
        jnp.stack(outputs).astype(jnp.bfloat16),
        jnp.stack(token_grads).astype(jnp.bfloat16),
        grad_qkv,
        grad_out,
        grad_up,
        grad_down,
        grad_ada,
        grad_ada_bias,
        grad_rel,
        class_total,
    )


def solution(mesh):
    n_dp, n_mp = mesh.shape["dp"], mesh.shape["mp"]

    def specs(*dp):
        rows = P(None, (*dp, "mp"), None)
        weights = (P(None, "mp"), P("mp", None), P(None, "mp"), P("mp", None), P(None, "mp"), P("mp"), P("mp", None), P())
        return (rows, rows, *weights, *[P(None, dp)] * 3), (rows, rows, *weights)

    def program(tokens, *arrays):
        if n_mp == 4 and n_dp % 2 == 0 and tokens.shape[1] == n_dp * n_mp * WIN:
            devices = mesh.devices.reshape(n_dp // 2, 2, n_mp)
            split = jax.sharding.Mesh(devices, ("z", "core", "mp"))
            ins, outs = specs("z", "core")
            step = jax.shard_map(
                partial(local_windows, (n_dp // 2, n_mp)), mesh=split, in_specs=ins, out_specs=outs, check_vma=False
            )
        else:
            ins, outs = specs("dp")
            step = jax.shard_map(local_general, mesh=mesh, in_specs=ins, out_specs=outs, check_vma=False)
        return step(tokens, *arrays)

    return program
```

```python
from functools import partial
import math
from typing import NamedTuple

import jax
import jax.numpy as jnp
import numpy as np
from jax import lax
from jax.experimental import pallas as pl
from jax.experimental.pallas import tpu as pltpu
from jax.sharding import PartitionSpec as P

HD = 64
WT = 5
WH = 8
WW = 8
WIN = 320
D = 1024
EPS = 1e-06
NOFF = WT + WH + WW
C0 = math.sqrt(2.0 / math.pi)
C1 = 0.044715
precise = lax.Precision.HIGHEST
f32 = jnp.float32
bf16 = jnp.bfloat16
NN = (((1,), (0,)), ((), ()))
NT = (((1,), (1,)), ((), ()))
TN = (((0,), (0,)), ((), ()))
HALF = 512
QKV = 384


def mm(a, b, dims=NN):
    return lax.dot_general(a, b, dims, preferred_element_type=f32)


def whole(*dims):
    return pl.BlockSpec(dims, lambda i, *_: (0,) * len(dims))


def part(index, *dims):
    return pl.BlockSpec(dims, lambda i, *_: index)


def rows_of(width):
    return pl.BlockSpec((WIN, width), lambda i, *_: (i, 0))


def window_of(*dims):
    return pl.BlockSpec((None,) + dims, lambda i, *_: (i,) + (0,) * len(dims))


def shape(dims, dtype):
    return pltpu.HBM(dims, dtype)


def near(dims, dtype):
    return jax.ShapeDtypeStruct(dims, dtype)


HBM = pl.BlockSpec(memory_space=pltpu.HBM)
VMEM = pl.BlockSpec(memory_space=pltpu.VMEM)


class Loads:
    def __init__(self, sems):
        self.sems, self.copies = sems, []

    def add(self, source, target):
        self.copies.append(pltpu.make_async_copy(source, target, self.sems.at[len(self.copies)]))
        return self.copies[-1]

    def start(self):
        for copy in self.copies:
            copy.start()

    def wait(self):
        for copy in self.copies:
            copy.wait()


class Moved(NamedTuple):
    array: jax.Array


def in_hbm(array):
    return pltpu.with_memory_space_constraint(array, pltpu.HBM)


def operand(array, spec):
    if isinstance(array, Moved):
        return array.array, pl.BlockSpec(memory_space=pl.ANY) if spec is HBM else spec
    return array if spec is VMEM else in_hbm(array), spec


def run(kernel, name, grid, ins, outs, scratch=(), after=(), scalars=(), flops=0, moved=0, vmem=24):
    first = len(scalars) + len(ins)

    ins = [operand(array, spec) for array, spec in ins]

    def body(*refs):
        kernel(*refs[:first], *refs[first + len(after) :])

    return pl.pallas_call(
        body,
        grid_spec=pltpu.PrefetchScalarGridSpec(
            num_scalar_prefetch=len(scalars),
            grid=(grid,),
            in_specs=[spec for _, spec in ins] + [HBM] * len(after),
            out_specs=[spec for _, spec in outs],
            scratch_shapes=list(scratch),
        ),
        out_shape=[what for what, _ in outs],
        compiler_params=pltpu.CompilerParams(vmem_limit_bytes=vmem * 2**20),
        cost_estimate=pl.CostEstimate(flops=1000, bytes_accessed=1000, transcendentals=0),
        name=name,
    )(*scalars, *[array for array, _ in ins], *map(in_hbm, after))


def hold(values, after=(), flops=1000):
    anywhere = pl.BlockSpec(memory_space=pl.ANY)
    return pl.pallas_call(
        lambda *refs: None,
        in_specs=[anywhere] * len(values) + [HBM] * len(after),
        out_specs=[anywhere] * len(values),
        out_shape=[near(v.shape, v.dtype) for v in values],
        input_output_aliases={i: i for i in range(len(values))},
        cost_estimate=pl.CostEstimate(flops=flops, bytes_accessed=1000, transcendentals=0),
        name="hold",
    )(*values, *map(in_hbm, after))


def arrive(values, after):
    return hold(values, after, 30 * 10**9)


def ln_parts(values):
    center = values - jnp.mean(values, axis=-1, keepdims=True)
    rstd = lax.rsqrt(jnp.mean(center * center, axis=-1, keepdims=True) + EPS)
    return center * rstd, rstd


def ln_back(grad, scale, hat, rstd):
    inner = grad * (1.0 + scale)
    mean_one = jnp.mean(inner, axis=-1, keepdims=True)
    mean_two = jnp.mean(inner * hat, axis=-1, keepdims=True)
    return rstd * (inner - mean_one - hat * mean_two)


def hot_rows(count, source):
    row = lax.broadcasted_iota(jnp.int32, (count, count), 0)
    col = lax.broadcasted_iota(jnp.int32, (count, count), 1)
    return col == source(row), row


def qkv_source(core):
    def source(row):
        half = jnp.where(row >= QKV, 1, 0)
        inner = row - half * QKV
        head = 2 * (half ^ core) + ((inner & 127) >> 6)
        return head * 3 * HD + (inner >> 7) * HD + (inner & 63)

    return source


def attn_rows_kernel(core_ref, qkv_ref, out_ref, own0, own1):
    core = core_ref[0]
    hot, row = hot_rows(2 * QKV, qkv_source(core))
    inner = jnp.where(row >= QKV, row - QKV, row)
    hot = jnp.where(hot, jnp.where(inner < 128, HD**-0.5, 1.0), 0.0).astype(bf16)
    rows = mm(hot, qkv_ref[...], NT).astype(bf16)
    for h, own in enumerate((own0, own1)):
        own[:QKV] = rows[h * QKV : (h + 1) * QKV]
        own[QKV:] = out_ref[pl.ds(pl.multiple_of((core ^ h) * 128, 128), 128)]


def feed_rows_kernel(core_ref, up_ref, down_ref, up0, down0, up1, down1):
    core = core_ref[0]
    hot, _ = hot_rows(2 * HALF, lambda row: row ^ (core * HALF))
    rows = mm(jnp.where(hot, 1.0, 0.0).astype(bf16), up_ref[...], NT).astype(bf16)
    for h, (up, down) in enumerate(((up0, down0), (up1, down1))):
        up[0] = rows[h * HALF : (h + 1) * HALF]
        down[0] = down_ref[pl.ds(pl.multiple_of((core ^ h) * HALF, HALF), HALF)]


def attn_rows(core, qkv, out, after):
    half = (shape((HALF, D), bf16), whole(HALF, D))
    ins = [(qkv, whole(D, 2 * QKV)), (out, whole(256, D))]
    return run(attn_rows_kernel, "attn_rows", 1, ins, [half, half], (), after, [core], 1e9, 4e6)


def feed_rows(core, up, down, after):
    half = (shape((1, HALF, D), bf16), whole(1, HALF, D))
    ins = [(up, whole(D, 2 * HALF)), (down, whole(2 * HALF, D))]
    return run(feed_rows_kernel, "feed_rows", 1, ins, [half] * 4, (), after, [core], 2e9, 8e6)


def attend_kernel(len_ref, x_ref, mode_ref, wa_ref, wb_ref, tbl_ref, e_ref, *rest):
    n1_ref, packed_ref, heads_ref, probs_ref, w_all, kb_all, sems = rest if len(rest) == 7 else (None, *rest)
    w = pl.program_id(0)

    @pl.when(w == 0)
    def _():
        loads = Loads(sems)
        loads.add(wa_ref.at[:QKV], w_all.at[:QKV])
        loads.add(wb_ref.at[:QKV], w_all.at[QKV:])
        loads.start()
        for p in range(2):
            kb_all[p] = mm(e_ref[...], tbl_ref[p]).astype(bf16)
        loads.wait()

    if n1_ref is None:
        x = x_ref[...]
    else:
        hat, _ = ln_parts(x_ref[...].astype(f32))
        x = (hat * (1.0 + mode_ref[1:2]) + mode_ref[0:1]).astype(bf16)
        n1_ref[...] = x
    pk = mm(x, w_all[...], NT).astype(bf16)
    packed_ref[...] = pk
    lane = lax.broadcasted_iota(jnp.int32, (WIN, 128), 1)
    low = lane < 64
    frame = lax.broadcasted_iota(jnp.int32, (WIN, 128), 0) // (WH * WW)
    mask_lane = (lane & 63) == 2 * NOFF
    hide = jnp.where(frame < len_ref[w], 0.0, -1e30).astype(bf16)
    for p in range(2):
        q = pk[:, p * QKV : p * QKV + 128]
        k = pk[:, p * QKV + 128 : p * QKV + 256]
        v = pk[:, p * QKV + 256 : p * QKV + 384]
        kb = jnp.where(mask_lane, hide, kb_all[p])
        v_rows = v.T
        outs = []
        for i in range(2):
            mine = low if i == 0 else ~low
            s = mm(jnp.where(mine, k, kb), jnp.where(mine, q, e_ref[...]), NT)
            ex = jnp.exp(s - jnp.max(s, axis=0, keepdims=True))
            pr = (ex * (1.0 / jnp.sum(ex, axis=0, keepdims=True))).astype(bf16)
            probs_ref[2 * p + i] = pr
            outs.append(mm(v_rows[i * HD : (i + 1) * HD], pr))
        heads_ref[:, p * 128 : (p + 1) * 128] = jnp.concatenate(outs, axis=0).T.astype(bf16)


def attend(lengths, source, modes, weight, table, query_hot, after=()):
    count = lengths.shape[0]
    rows = count * WIN
    first = source.ndim == 3
    outs = [
        (shape((rows, 2 * QKV), bf16), rows_of(2 * QKV)),
        (shape((rows, 256), bf16), rows_of(256)),
        (shape((count * 4, WIN, WIN), bf16), pl.BlockSpec((4, WIN, WIN), lambda i, l: (i, 0, 0))),
    ]
    if first:
        outs = [(near((rows, D), bf16), rows_of(D))] + outs
    return run(
        attend_kernel,
        "attend",
        count,
        [
            (source, window_of(WIN, D) if first else rows_of(D)),
            (modes, window_of(6, D)),
            (weight[0], HBM),
            (weight[1], HBM),
            (table, whole(2, 128, 128)),
            (query_hot, whole(WIN, 128)),
        ],
        outs,
        [pltpu.VMEM((2 * QKV, D), bf16), pltpu.VMEM((2, WIN, 128), bf16), pltpu.SemaphoreType.DMA((2,))],
        after,
        [lengths],
        9e9,
        12e6,
    )


def middle_kernel(h0, h1, h2, h3, w0, w1, w2, w3, w4, w5, w6, w7, tok, cot, mode, attn_ref, mid_ref, n2_ref, di_ref, w_all, sems):
    @pl.when(pl.program_id(0) == 0)
    def _():
        loads = Loads(sems)
        for i, ref in enumerate((w0, w1, w2, w3, w4, w5, w6, w7)):
            loads.add(ref.at[QKV:], w_all.at[pl.ds(i * 128, 128)])
        loads.start()
        loads.wait()

    heads = jnp.concatenate([h0[...], h1[...], h2[...], h3[...]], axis=1)
    attn = mm(heads, w_all[...])
    attn_ref[...] = attn.astype(bf16)
    middle = tok[...].astype(f32) + mode[2:3] * attn
    mid_ref[...] = middle
    hat, _ = ln_parts(middle)
    n2_ref[...] = (hat * (1.0 + mode[4:5]) + mode[3:4]).astype(bf16)
    di_ref[...] = (mode[5:6] * cot[...].astype(f32)).astype(bf16)


def middle_step(heads, weights, tokens, cotangent, modes, after=()):
    count = tokens.shape[0]
    rows = count * WIN
    return run(
        middle_kernel,
        "middle",
        count,
        [(h, rows_of(256)) for h in heads]
        + [(half, HBM) for pair in weights for half in pair]
        + [(tokens, window_of(WIN, D)), (cotangent, window_of(WIN, D)), (modes, window_of(6, D))],
        [(shape((rows, D), kind), rows_of(D)) for kind in (bf16, f32)] + [(near((rows, D), bf16), rows_of(D))] * 2,
        [pltpu.VMEM((D, D), bf16), pltpu.SemaphoreType.DMA((8,))],
        after,
        flops=2.7e9,
        moved=22e6,
    )


CHUNK = 256


def feed_kernel(places, n2, di, up0, dn0, up1, dn1, hid_hbm, pre_hbm, g0_hbm, g1_hbm, weight, hid, pre, grad, in_sems, out_sems):
    loads, stores = Loads(in_sems), Loads(out_sems)
    for i, ref in enumerate((up0, dn0, up1, dn1)):
        loads.add(ref.at[places[i]], weight.at[i // 2, i % 2])
    for i in (2, 3, 0, 1):
        loads.copies[i].start()

    def store(from_ref, to_ref):
        stores.add(from_ref, to_ref).start()

    for h, g_hbm in ((1, g1_hbm), (0, g0_hbm)):
        units = pl.ds(h * HALF, HALF)
        loads.copies[2 * h].wait()
        loads.copies[2 * h + 1].wait()
        for i in range(n2.shape[0] // CHUNK):
            rows = pl.ds(i * CHUNK, CHUNK)
            v = mm(n2[rows], weight[h, 0], NT)
            hg = mm(di[rows], weight[h, 1], NT)
            v2 = v * v
            t = jnp.tanh(v * (C0 + (C0 * C1) * v2))
            share = 0.5 + 0.5 * t
            hid[h, rows] = (v * share).astype(bf16)
            slope = share + (0.5 * v) * (1.0 - t * t) * (C0 + (3.0 * C0 * C1) * v2)
            pre[h, rows] = (slope * hg).astype(bf16)
        store(hid.at[h], hid_hbm.at[:, units])
        store(pre.at[h], pre_hbm.at[:, units])
        grad[h, 1] = mm(hid[h], di[...], TN).astype(bf16)
        store(grad.at[h, 1], g_hbm.at[1])
        grad[h, 0] = mm(pre[h], n2[...], TN).astype(bf16)
        store(grad.at[h, 0], g_hbm.at[0])
    stores.wait()


def feed(normed, down_in, weight, after=()):
    rows = normed.shape[0]
    halves = [array for half in weight for array, _ in half]
    places = [place for half in weight for _, place in half]
    return run(
        partial(feed_kernel, places),
        "feed",
        1,
        [(normed, VMEM), (down_in, VMEM)] + [(array, HBM) for array in halves],
        [(shape((rows, 2 * HALF), bf16), HBM)] * 2 + [(shape((2, HALF, D), bf16), HBM)] * 2,
        [pltpu.VMEM((2, 2, HALF, D), bf16)]
        + [pltpu.VMEM((2, rows, HALF), bf16)] * 2
        + [pltpu.VMEM((2, 2, HALF, D), bf16), pltpu.SemaphoreType.DMA((4,)), pltpu.SemaphoreType.DMA((8,))],
        after,
        vmem=32,
    )


def unit_sums(sources, pieces, places, weight, acc, sems):
    w = pl.program_id(0)

    def span(i):
        return slice(i % 2 * HALF, (i % 2 + 1) * HALF)

    @pl.when(w == 0)
    def _():
        loads = Loads(sems)
        for i, piece in enumerate(pieces):
            loads.add(piece.at[places[i]], weight.at[pl.ds(i * HALF, HALF)])
        loads.start()
        for i, copy in enumerate(loads.copies):
            copy.wait()
            term = mm(sources[i // 2][:, span(i)], weight[i * HALF : (i + 1) * HALF])
            acc[...] = term if i == 0 else acc[...] + term

    @pl.when(w > 0)
    def _():
        source = jnp.concatenate([ref[...] for ref in sources], axis=1)
        acc[...] = mm(source, weight[...])


def turn_kernel(places, p0, p1, p2, p3, w0, w1, w2, w3, w4, w5, w6, w7, mid_ref, attn_ref, cot_ref, mode_ref, *rest):
    mg_ref, oi_ref, sum_ref, weight, acc, sems = rest
    unit_sums((p0, p1, p2, p3), (w0, w1, w2, w3, w4, w5, w6, w7), places, weight, acc, sems)
    ng = acc[...]
    hat, rstd = ln_parts(mid_ref[...])
    mg = cot_ref[...].astype(f32) + ln_back(ng, mode_ref[4:5], hat, rstd)
    mg_ref[...] = mg
    oi_ref[...] = (mode_ref[2:3] * mg).astype(bf16)
    sum_ref[0:1] = jnp.sum(mg * attn_ref[...].astype(f32), axis=0, keepdims=True)
    sum_ref[1:2] = jnp.sum(ng, axis=0, keepdims=True)
    sum_ref[2:3] = jnp.sum(ng * hat, axis=0, keepdims=True)


def out_kernel(places, p0, p1, p2, p3, w0, w1, w2, w3, w4, w5, w6, w7, mid_ref, cot_ref, mode_ref, *rest):
    out_ref, sum_ref, weight, acc, sems = rest
    unit_sums((p0, p1, p2, p3), (w0, w1, w2, w3, w4, w5, w6, w7), places, weight, acc, sems)
    mlp = acc[...]
    out_ref[...] = (mid_ref[...] + mode_ref[5:6] * mlp).astype(bf16)
    sum_ref[...] = jnp.sum(cot_ref[...].astype(f32) * mlp, axis=0, keepdims=True)


def of_units(arrays, weights, which):
    halves = [half[which] for pair in weights for half in pair]
    ins = [(array, rows_of(2 * HALF)) for array in arrays] + [(array, HBM) for array, _ in halves]
    scratch = [pltpu.VMEM((8 * HALF, D), bf16), pltpu.VMEM((WIN, D), f32), pltpu.SemaphoreType.DMA((8,))]
    return ins, scratch, [place for _, place in halves]


def turn_step(pre, weights, middle, attn_out, cotangent, modes, after=()):
    count = cotangent.shape[0]
    rows = count * WIN
    ins, scratch, places = of_units(pre, weights, 0)
    return run(
        partial(turn_kernel, places),
        "turn",
        count,
        ins
        + [(middle, rows_of(D)), (attn_out, rows_of(D)), (cotangent, window_of(WIN, D)), (modes, window_of(6, D))],
        [
            (shape((rows, D), f32), rows_of(D)),
            (near((rows, D), bf16), rows_of(D)),
            (shape((count, 3, D), f32), window_of(3, D)),
        ],
        scratch,
        after,
        vmem=36,
        flops=10.7e9,
        moved=35e6,
    )


def out_step(hid, weights, middle, cotangent, modes, after=()):
    count = cotangent.shape[0]
    ins, scratch, places = of_units(hid, weights, 1)
    return run(
        partial(out_kernel, places),
        "output",
        count,
        ins + [(middle, rows_of(D)), (cotangent, window_of(WIN, D)), (modes, window_of(6, D))],
        [(shape((count, WIN, D), bf16), window_of(WIN, D)), (shape((count, 1, D), f32), window_of(1, D))],
        scratch,
        after,
        vmem=36,
        flops=10.7e9,
        moved=30e6,
    )


def attend_back_kernel(
    oi_ref, o0, o1, pk_ref, pr_ref, e_ref, n1_ref, oi_all, ho_hbm, pg_ref, g0_ref, g1_ref, rel_ref, *scratch
):
    pg_all, t_all, ow, ho_ref, sems = scratch
    w = pl.program_id(0)
    loads = Loads(sems)
    weights = [loads.add(o.at[QKV:], ow.at[pl.ds(i * 128, 128)]) for i, o in enumerate((o0, o1))]
    heads = loads.add(ho_hbm, ho_ref)

    @pl.when(w == 0)
    def _():
        loads.start()
        t_all[...] = jnp.zeros_like(t_all)
        for copy in weights:
            copy.wait()

    hg = mm(oi_ref[...], ow[...], NT).astype(bf16)
    pk = pk_ref[...]
    low = lax.broadcasted_iota(jnp.int32, (WIN, 128), 1) < 64
    for p in range(2):
        q = pk[:, p * QKV : p * QKV + 128]
        k = pk[:, p * QKV + 128 : p * QKV + 256]
        v = pk[:, p * QKV + 256 : p * QKV + 384]
        do = hg[:, p * 128 : (p + 1) * 128]
        k_rows = k.T
        dv, dq, dk = [], [], []
        for i in range(2):
            mine = low if i == 0 else ~low
            qa = jnp.where(mine, q, e_ref[...])
            dp = mm(jnp.where(mine, v, jnp.zeros_like(v)), do, NT)
            prl = pr_ref[2 * p + i]
            pr = prl.astype(f32)
            t = pr * dp
            ds = (t - pr * jnp.sum(t, axis=0, keepdims=True)).astype(bf16)
            dv.append(mm(prl, do))
            dq.append(mm(k_rows[i * HD : (i + 1) * HD], ds))
            dk.append(mm(ds, qa))
        dq = jnp.concatenate(dq, axis=0).T
        block = jnp.concatenate(
            [dq, jnp.where(low, dk[0], dk[1]), jnp.where(low, dv[0], dv[1])], axis=1
        ).astype(bf16)
        pg_ref[:, p * QKV : (p + 1) * QKV] = block
        pg_all[pl.ds(pl.multiple_of(w * WIN, WIN), WIN), p * QKV : (p + 1) * QKV] = block
        t_all[p] += jnp.where(low, dk[1], dk[0])

    @pl.when(w == pl.num_programs(0) - 1)
    def _():
        heads.wait()
        go = mm(ho_ref[...], oi_all[...], TN).astype(bf16)
        gq = mm(pg_all[...], n1_ref[...], TN).astype(bf16)
        for p, g_ref in enumerate((g0_ref, g1_ref)):
            g_ref[:QKV] = gq[p * QKV : (p + 1) * QKV]
            g_ref[QKV:] = go[p * 128 : (p + 1) * 128]
        hot = e_ref[...].astype(f32)
        for p in range(2):
            sums = lax.dot_general(hot, t_all[p], TN, precision=precise, preferred_element_type=f32)
            rel_ref[p] = sums[:32]


def attend_back(out_in, weight, packed, probs, query_hot, normed, heads, after=()):
    rows = normed.shape[0]
    return run(
        attend_back_kernel,
        "attend_back",
        rows // WIN,
        [
            (out_in, rows_of(D)),
            (weight[0], HBM),
            (weight[1], HBM),
            (packed, rows_of(2 * QKV)),
            (probs, pl.BlockSpec((4, WIN, WIN), lambda i: (i, 0, 0))),
            (query_hot, whole(WIN, 128)),
            (normed, VMEM),
            (out_in, VMEM),
            (heads, HBM),
        ],
        [
            (shape((rows, 2 * QKV), bf16), rows_of(2 * QKV)),
            (shape((HALF, D), bf16), whole(HALF, D)),
            (shape((HALF, D), bf16), whole(HALF, D)),
            (shape((2, 32, 128), f32), whole(2, 32, 128)),
        ],
        [pltpu.VMEM((rows, 2 * QKV), bf16), pltpu.VMEM((2, WIN, 128), f32), pltpu.VMEM((256, D), bf16)]
        + [pltpu.VMEM((rows, 256), bf16), pltpu.SemaphoreType.DMA((3,))],
        after,
        flops=13e9,
        moved=20e6,
    )


def last_kernel(p0, p1, p2, p3, w0, w1, w2, w3, w4, w5, w6, w7, tok_ref, mode_ref, mg_ref, out_ref, sum_ref, w_all, acc, sems):
    @pl.when(pl.program_id(0) == 0)
    def _():
        loads = Loads(sems)
        for i, ref in enumerate((w0, w1, w2, w3, w4, w5, w6, w7)):
            loads.add(ref.at[:QKV], w_all.at[pl.ds(i * QKV, QKV)])
        loads.start()
        for i, src in enumerate((p0, p1, p2, p3)):
            loads.copies[2 * i].wait()
            loads.copies[2 * i + 1].wait()
            term = mm(src[...], w_all[i * 2 * QKV : (i + 1) * 2 * QKV])
            acc[...] = term if i == 0 else acc[...] + term

    @pl.when(pl.program_id(0) > 0)
    def _():
        acc[...] = mm(jnp.concatenate([p0[...], p1[...], p2[...], p3[...]], axis=1), w_all[...])

    ng = acc[...]
    hat, rstd = ln_parts(tok_ref[...].astype(f32))
    out_ref[...] = (mg_ref[...] + ln_back(ng, mode_ref[1:2], hat, rstd)).astype(bf16)
    sum_ref[0:1] = jnp.sum(ng, axis=0, keepdims=True)
    sum_ref[1:2] = jnp.sum(ng * hat, axis=0, keepdims=True)


def last_step(packed_grads, weights, tokens, modes, middle_grad, after=()):
    count = tokens.shape[0]
    return run(
        last_kernel,
        "last",
        count,
        [(array, rows_of(2 * QKV)) for array in packed_grads]
        + [(half, HBM) for pair in weights for half in pair]
        + [(tokens, window_of(WIN, D)), (modes, window_of(6, D)), (middle_grad, rows_of(D))],
        [(shape((count, WIN, D), bf16), window_of(WIN, D)), (shape((count, 2, D), f32), window_of(2, D))],
        [pltpu.VMEM((8 * QKV, D), bf16), pltpu.VMEM((WIN, D), f32), pltpu.SemaphoreType.DMA((8,))],
        after,
        flops=8e9,
        moved=24e6,
    )


def merge_kernel(sums, count, *refs):
    i = pl.program_id(0)
    refs = list(refs)
    outs = refs[len(refs) - len(sums) :]
    for spans, out in zip(sums, outs):
        value = None
        for first, last in spans:
            term = refs.pop(0)[...].astype(f32)
            if (first, last) != (0, count):
                term = jnp.where((i >= first) & (i < last), term, 0.0)
            value = term if value is None else value + term
        out[...] = value.astype(bf16)


def merge(*sums, rows=HALF, after=()):
    block = min(256, rows)
    ins, spans = [], []
    for terms in sums:
        spans.append([])
        for array, place, start, *limits in terms:
            first, last = [limit // block for limit in (limits or (0, rows))]
            start = start // block

            def at(i, start=start, first=first, last=last):
                return jnp.clip(i, first, last - 1) + start

            if place is None:
                spec = pl.BlockSpec((block, D), lambda i, at=at: (at(i), 0))
            else:
                spec = pl.BlockSpec((None, block, D), lambda i, p=place, at=at: (p, at(i), 0))
            ins.append((array, spec))
            spans[-1].append((first, last))
    out = (shape((rows, D), bf16), pl.BlockSpec((block, D), lambda i: (i, 0)))
    return run(partial(merge_kernel, spans, rows // block), "merge", rows // block, ins, [out] * len(sums), (), after)


def parts_kernel(count, only, z_ref, *refs):
    which_sum = pl.program_id(0) % (1 + max([0] + [w for w in only if w is not None]))
    terms = len(only)
    for k in range(count):
        value = None
        for ref, which in zip(refs[k * terms : (k + 1) * terms], only):
            term = ref[...].astype(f32)
            if which is not None:
                term = jnp.where(which_sum == which, term, 0.0)
            value = term if value is None else value + term
        refs[count * terms + k][...] = value.astype(bf16)


def merge_parts(terms, z, count, outputs):
    size = HALF // count
    sums = 2 if terms[0].ndim == 3 else 1
    ins, only = [], []
    for j in range(outputs):
        for term in terms:
            array, which = term if type(term) is tuple else (term, None)
            dims = array.array.ndim if isinstance(array, Moved) else array.ndim

            def at(i, zr, j=j):
                return zr[0] ^ (i // sums * outputs + j)

            if dims == 3:
                spec = pl.BlockSpec((None, size, D), lambda i, zr, at=at: (i % sums, at(i, zr), 0))
            else:
                spec = pl.BlockSpec((size, D), lambda i, zr, at=at: (at(i, zr), 0))
            ins.append((array, spec))
            only.append(which)
    grid = sums * count // outputs
    outs = [(shape((grid * size, D), bf16), pl.BlockSpec((size, D), lambda i, zr: (i, 0)))] * outputs
    return run(partial(parts_kernel, outputs, only[: len(terms)]), "merge_parts", grid, ins, outs, (), (), [z])


def attn_final_kernel(place_ref, a_ref, b_ref, qkv_ref, out_ref, rows, hot):
    core, z = place_ref[0], place_ref[1]
    size = HALF // 4

    @pl.when(pl.program_id(0) == 0)
    def _():
        match, row = hot_rows(2 * QKV, qkv_source(core))
        inner = jnp.where(row >= QKV, row - QKV, row)
        hot[...] = jnp.where(match, jnp.where(inner < 128, HD**-0.5, 1.0), 0.0).astype(bf16)

    for h, ref in enumerate((a_ref, b_ref)):
        for k in range(4):
            part_at = z ^ k
            block = ref[k * size : (k + 1) * size]

            @pl.when(part_at < 3)
            def _():
                rows[pl.ds(pl.multiple_of(h * QKV + part_at * size, size), size)] = block

            @pl.when(part_at == 3)
            def _():
                out_ref[pl.ds(pl.multiple_of((core ^ h) * size, size), size)] = block.astype(f32)

    qkv_ref[...] = mm(rows[...], hot[...], TN)


def columns_of(rows):
    return pl.BlockSpec((rows, 256), lambda i, *_: (0, i))


def attn_final(place, a, b):
    ins = [(a, columns_of(HALF)), (b, columns_of(HALF))]
    outs = [
        (shape((D, 2 * QKV), f32), pl.BlockSpec((256, 2 * QKV), lambda i, *_: (i, 0))),
        (shape((256, D), f32), columns_of(256)),
    ]
    scratch = [pltpu.VMEM((2 * QKV, 256), bf16), pltpu.VMEM((2 * QKV, 2 * QKV), bf16)]
    return run(attn_final_kernel, "attn_final", D // 256, ins, outs, scratch, (), [place])


def feed_final_kernel(place_ref, *refs):
    up_ref, down_ref, rows, hot = refs[4:]
    core, z = place_ref[0], place_ref[1]
    size = HALF // 4

    @pl.when(pl.program_id(0) == 0)
    def _():
        hot[...] = jnp.where(hot_rows(2 * HALF, lambda row: row ^ (core * HALF))[0], 1.0, 0.0).astype(bf16)

    for h in range(2):
        for k, (ref, first) in enumerate(((refs[2 * h], 0), (refs[2 * h + 1], 0), (refs[2 * h], 2), (refs[2 * h + 1], 2))):
            start = (z ^ k) * size
            rows[pl.ds(pl.multiple_of(h * HALF + start, size), size)] = ref[first * size : (first + 1) * size]
            block = ref[(first + 1) * size : (first + 2) * size].astype(f32)
            down_ref[pl.ds(pl.multiple_of((core ^ h) * HALF + start, size), size)] = block
    up_ref[...] = mm(rows[...], hot[...], TN)


def feed_final(place, even, odd, other_even, other_odd):
    ins = [(v, columns_of(HALF)) for v in (even, odd, other_even, other_odd)]
    outs = [
        (shape((D, 2 * HALF), f32), pl.BlockSpec((256, 2 * HALF), lambda i, *_: (i, 0))),
        (shape((2 * HALF, D), f32), columns_of(2 * HALF)),
    ]
    scratch = [pltpu.VMEM((2 * HALF, 256), bf16), pltpu.VMEM((2 * HALF, 2 * HALF), bf16)]
    return run(feed_final_kernel, "feed_final", D // 256, ins, outs, scratch, (), [place])


def mode_shares_kernel(m0, m1, m2, m3, rel_ref, ada_ref, low_ref, s0, s1, s2, s3, rows):
    count = m0.shape[0]
    for r, ref in enumerate((m0, m1, m2, m3)):
        rows[r * count : (r + 1) * count] = ref[...]
    low = rows[...].astype(bf16)
    low_ref[...] = low
    cond = mm(low, ada_ref[...], NT)
    for r, ref in enumerate((s0, s1, s2, s3)):
        ref[:, :D] = cond
        ref[:, D:] = rel_ref[r]


def mode_shares(messages, rel_part, ada_weight):
    count, columns = messages[0].shape
    rows = 4 * count
    ins = [(v, whole(count, columns)) for v in messages]
    ins += [(rel_part, whole(4, rows, 128)), (ada_weight, whole(D, columns))]
    outs = [(shape((rows, columns), bf16), whole(rows, columns))] + [(shape((rows, D + 128), f32), whole(rows, D + 128))] * 4
    return run(mode_shares_kernel, "mode_shares", 1, ins, outs, [pltpu.VMEM((rows, columns), f32)])


def mode_rows_kernel(mp_ref, low_ref, s0, s1, s2, s3, slope_ref, cond_ref, out_ref):
    rows, columns = low_ref.shape
    count = rows // 4
    mp = mp_ref[0]
    moved = [s0[:, :D]]
    for k, ref in ((1, s1), (2, s2), (3, s3)):
        blocks = [ref[(r ^ k) * count : ((r ^ k) + 1) * count, :D] for r in range(4)]
        moved.append(jnp.concatenate(blocks, axis=0))
    cond = (moved[0] + moved[1]) + (moved[2] + moved[3])
    value = (cond * slope_ref[...]).astype(bf16)
    row = lax.broadcasted_iota(jnp.int32, (rows, rows), 0)
    col = lax.broadcasted_iota(jnp.int32, (rows, rows), 1)
    hot = jnp.where(col == row ^ (mp * count), 1.0, 0.0).astype(bf16)
    out_ref[:, :columns] = low_ref[...]
    out_ref[:, columns : columns + D] = mm(hot, value).astype(bf16)
    out_ref[:, columns + D : columns + D + 128] = (s0[:, D:] + s1[:, D:] + s2[:, D:] + s3[:, D:]).astype(bf16)
    out_ref[:, columns + D + 128 :] = cond_ref[...]


def mode_rows(mp, low, shares, slope, cond):
    rows, columns = low.shape
    width = columns + 2 * (D + 128)
    ins = [(low, whole(rows, columns))] + [(v, whole(rows, D + 128)) for v in shares]
    ins += [(slope, whole(rows, D)), (cond, whole(rows, D + 128))]
    outs = [(shape((rows, width), bf16), whole(rows, width))]
    return run(mode_rows_kernel, "mode_rows", 1, ins, outs, (), (), [mp])[0]


def mode_final_kernel(dp_ref, *refs):
    *parts, ada_ref, bias_ref, class_ref, rel_ref, rows = refs
    size = parts[0].shape[0]
    columns = ada_ref.shape[1]
    marks = [0, columns, columns + D, columns + D + 128, columns + 2 * D + 128, columns + 2 * D + 256]
    for k, ref in enumerate(parts):
        rows[pl.ds(pl.multiple_of((dp_ref[0] ^ k) * size, size), size)] = ref[...]
    modes, classes, rel, cond, index = [rows[:, i:j] for i, j in zip(marks, marks[1:])]
    ada_ref[...] = mm(cond, modes, TN)
    bias_ref[...] = jnp.sum(modes.astype(f32), axis=0)
    lane = lax.broadcasted_iota(jnp.int32, index.shape, 1).astype(f32)
    hot = jnp.where(lane == index[:, :1].astype(f32), 1.0, 0.0).astype(bf16)
    class_ref[...] = mm(hot, classes, TN)[: class_ref.shape[0]]
    total = rel[:size].astype(f32)
    for i in range(1, len(parts)):
        total = total + rel[i * size : (i + 1) * size].astype(f32)
    rel_ref[...] = total[: rel_ref.shape[0], : rel_ref.shape[1]]


def mode_final(dp, parts, columns, class_count, rel_shape):
    size, width = parts[0].shape
    ins = [(v, whole(size, width)) for v in parts]
    outs = [(shape(dims, f32), whole(*dims)) for dims in ((D, columns), (columns,), (class_count, D), rel_shape)]
    scratch = [pltpu.VMEM((len(parts) * size, width), bf16)]
    return run(mode_final_kernel, "mode_final", 1, ins, outs, scratch, (), [dp], vmem=32)


def silu_plain(values):
    return values / (1.0 + jnp.exp(-values))


def condition(timesteps, classes, class_table):
    half_width = class_table.shape[1] // 2
    frequency = jnp.exp(
        -math.log(10000.0) * jnp.arange(half_width).astype(class_table.dtype) / half_width
    )
    phase_angle = timesteps.astype(class_table.dtype)[..., None] * frequency
    sinusoid = jnp.concatenate([jnp.cos(phase_angle), jnp.sin(phase_angle)], axis=-1)
    onehot = (classes[..., None] == jnp.arange(class_table.shape[0])).astype(class_table.dtype)
    lookup = jnp.einsum("mwc,cd->mwd", onehot, class_table, precision=precise)
    return sinusoid + lookup


SPANS = ((0, 0, WT), (WT, 2 * WT - 1, WH), (WT + WH, 2 * WT + 2 * WH - 2, WW))


def place_hot():
    spot = np.arange(WIN)
    hot = np.zeros((WIN, NOFF), np.float32)
    for (start, _, _), where in zip(SPANS, (spot // (WH * WW), (spot // WW) % WH, spot % WW)):
        hot[spot, start + where] = 1.0
    return hot


def query_side():
    half = np.zeros((WIN, 64), np.float32)
    half[:, :NOFF] = place_hot()
    half[:, NOFF : 2 * NOFF] = place_hot()
    half[:, 2 * NOFF] = 1.0
    return np.concatenate([half, half], axis=1)


def offset_hot(rows, copies):
    hot = np.zeros((2 * NOFF - 3, rows, 64), np.float32)
    for start, begin, length in SPANS:
        for key in range(length):
            for query in range(length):
                for copy in range(copies):
                    hot[begin + query - key + length - 1, start + key, copy * NOFF + start + query] = 1.0
    return hot


def key_tables(rel, core):
    value = jnp.einsum("hr,rkq->hkq", rel.reshape(16, -1), offset_hot(64, 2), precision=precise)
    top = lax.reduce_precision(value, 8, 7)
    value = jnp.where(jnp.arange(64) < NOFF, top, value - top).astype(bf16)
    value = value.reshape(4, 2, 2, 64, 64)
    value = jnp.where(core == 0, value, value[:, ::-1])
    value = jnp.concatenate([value[:, :, 1], value[:, :, 0]], axis=-1)
    return jnp.pad(value, ((0, 0), (0, 0), (0, 64), (0, 0)))


def rel_sums(grids, core):
    grids = jnp.where(core == 0, grids, grids[:, ::-1])
    grids = grids.reshape(4, 2, 32, 2, 64)
    grids = jnp.stack([grids[:, :, :, 1], grids[:, :, :, 0]], axis=2).reshape(16, 32, 64)
    return jnp.einsum("hkq,rkq->hr", grids, offset_hot(32, 1), precision=precise).reshape(4, 4, -1)


def local_windows(
    sizes,
    tokens,
    cotangent,
    qkv_weight,
    out_weight,
    up_weight,
    down_weight,
    ada_weight,
    ada_bias,
    rel_bias,
    class_table,
    lengths,
    timesteps,
    classes,
):
    n_z, n_mp = sizes
    n_dp = 2 * n_z
    micro = tokens.shape[0]
    mp = lax.axis_index("mp")
    z = lax.axis_index("z")
    core = lax.axis_index("core")

    def swap_mp(bit):
        return lambda v: lax.ppermute(v, "mp", [(i, i ^ bit) for i in range(n_mp)])

    def swap_dp(bit):
        return lambda v: lax.ppermute(v, ("z", "core"), [(i, i ^ bit) for i in range(n_dp)])

    px, py, pd = swap_mp(1), swap_mp(2), swap_mp(3)
    pc = swap_dp(1)
    by_rel = [lambda v: v, px, py, pd]

    def cat(a, b, axis=0):
        return jnp.concatenate([a, b], axis=axis)

    pre_cond = condition(timesteps, classes, class_table)
    cond_low = silu_plain(pre_cond).astype(bf16)
    mode_cols = jnp.einsum("mwd,de->mwe", cond_low, ada_weight, preferred_element_type=f32) + ada_bias.astype(f32)
    order = jnp.arange(4) ^ mp
    rel_row = jnp.pad(rel_bias, ((0, 0), (0, 128 - rel_bias.shape[1])))
    messages = [
        by_rel[r](cat(lax.dynamic_index_in_dim(mode_cols, mp ^ r, axis=1, keepdims=False), rel_row, 1))
        for r in range(4)
    ]
    messages = jnp.stack(messages)
    columns = mode_cols.shape[-1]
    modes = jnp.take(messages[:, :, :columns], order, axis=0)
    modes = modes.transpose(1, 0, 2).reshape(micro, 6, D)
    tables = key_tables(messages[:, :, columns : columns + rel_bias.shape[1]], core)
    own_lengths = lax.dynamic_index_in_dim(lengths, mp, axis=1, keepdims=False)

    core_row = core.reshape(1)
    query_hot = jnp.asarray(query_side(), bf16)
    packed, heads, probs = [None] * 4, [None] * 4, [None] * 4

    attn_own = list(attn_rows(core_row, qkv_weight, out_weight, [mode_cols]))
    (attn_own[0],) = hold(attn_own[:1], [messages])
    ax, ay = px(attn_own[0]), py(attn_own[0])
    normed_one, packed[0], heads[0], probs[0] = attend(own_lengths, tokens, modes, attn_own, tables[0], query_hot)
    up0, down0, up1, down1 = feed_rows(core_row, up_weight, down_weight, [heads[0]])
    ax, ay = hold([ax, ay], [down1])
    adx, ady = py(ax[: HALF // 2]), px(ay[HALF // 2 :])
    attn_w = [attn_own] + [[Moved(v), Moved(pc(v))] for v in (ax, ay)]
    packed[1], heads[1], probs[1] = attend(
        own_lengths, normed_one, modes, attn_w[1], tables[1], query_hot, [down1]
    )
    adx, ady = hold([adx, ady], [heads[1]])
    ad = cat(adx, ady)
    up0, down0 = hold([up0, down0], [ad])
    x_up, y_down = px(up0), py(down0)
    attn_w.append([ad, Moved(pc(ad))])
    packed[2], heads[2], probs[2] = attend(
        own_lengths, normed_one, modes, attn_w[2], tables[2], query_hot, [heads[1]]
    )
    packed[3], heads[3], probs[3] = attend(
        own_lengths, normed_one, modes, attn_w[3], tables[3], query_hot, [heads[2]]
    )
    x_up, y_down = hold([x_up, y_down], [heads[3]])
    d_up, d_down = py(x_up), px(y_down)
    attn_w = [[v.array if isinstance(v, Moved) else v for v in halves] for halves in attn_w]
    attn_out, middle, normed_two, down_in = middle_step(heads, attn_w, tokens, cotangent, modes)

    hid, pre, mine, other = [None] * 4, [None] * 4, [None] * 4, [None] * 4

    def feed_step(r, weight, after):
        hid[r], pre[r], mine[r], sent = feed(normed_two, down_in, weight, after)
        other[r] = pc(sent)

    def pair(r, which):
        return [(mine[r], which, 0), (Moved(other[r]), which, 0)]

    def weight_of(up, down):
        return [((Moved(u), 0), (Moved(v), 0)) for u, v in ((up, down), (pc(up), pc(down)))]

    feed_w = [[((up0, 0), (down0, 0)), ((up1, 0), (down1, 0))], None, None, None]
    feed_step(0, feed_w[0], [])
    d_up, d_down = hold([d_up, d_down], [hid[0]])
    feed_w[3] = weight_of(d_up, d_down)
    feed_step(3, feed_w[3], [hid[0]])
    x_down, y_up = arrive([px(down0), py(up0)], [hid[3]])
    feed_w[1], feed_w[2] = weight_of(x_up, x_down), weight_of(y_up, y_down)
    diag_x, diag_y = merge(pair(3, 0), pair(3, 1), after=[hid[3]])
    feed_step(1, feed_w[1], [hid[3], diag_x])
    feed_step(2, feed_w[2], [hid[1]])
    diag_x, diag_y = arrive([px(diag_x), py(diag_y)], [hid[2]])
    both = 2 * HALF
    flat = [v.reshape(both, D) for v in mine]
    flat_other = [v.reshape(both, D) for v in other]
    (last_x,) = merge(
        [(flat[1], None, 0), (Moved(flat_other[1]), None, 0), (Moved(diag_y), None, -HALF, HALF, both)], rows=both
    )
    (last_y,) = merge(
        [(flat[2], None, 0), (Moved(flat_other[2]), None, 0), (Moved(diag_x), None, 0, 0, HALF)], rows=both, after=[last_x]
    )
    middle_grad, out_in, turn_sums = turn_step(
        pre, feed_w, middle, attn_out, cotangent, modes, [last_x, last_y]
    )
    still = [[[(v.array if isinstance(v, Moved) else v, at) for v, at in half] for half in halves] for halves in feed_w]
    output, out_sums = out_step(hid, still, middle, cotangent, modes, [turn_sums])
    last_x, last_y = arrive([px(last_x), py(last_y)], [out_sums])
    z_row = z.reshape(1)
    terms = [mine[0], Moved(other[0]), *[Moved(v.reshape(2, HALF, D)) for v in (last_x, last_y)]]
    feed_keep, feed_sent = merge_parts(terms, z_row, n_z, 2)
    z_one, z_two = swap_dp(2), swap_dp(4)

    own_pre = jnp.take(pre_cond.transpose(1, 0, 2), order, axis=0).reshape(4 * micro, D)
    share = 1.0 / (1.0 + jnp.exp(-own_pre))
    class_col = jnp.pad(classes.T.reshape(-1, 1).astype(bf16), ((0, 0), (0, 127)))
    cond_rel = jnp.take(cond_low, order, axis=1).transpose(1, 0, 2).reshape(4 * micro, D)
    slope, cond_rel = hold([share * (1.0 + own_pre * (1.0 - share)), cat(cond_rel, class_col, 1)])

    packed_grad, rel_grid, a_mine, a_other = [None] * 4, [None] * 4, [None] * 4, [None] * 4

    def back_step(r, after):
        packed_grad[r], a_mine[r], sent, rel_grid[r] = attend_back(
            out_in, attn_w[r], packed[r], probs[r], query_hot, normed_one, heads[r], after
        )
        a_other[r] = pc(sent)

    cut = HALF // 2

    def a_pair(r, start):
        return [(a_mine[r], None, start), (Moved(a_other[r]), None, start)]

    back_step(3, [feed_keep])
    (feed_got,) = arrive([z_one(feed_sent)], [packed_grad[3]])
    (feed_sent,) = merge([(feed_keep, None, cut), (Moved(feed_got), None, cut)], rows=cut)
    back_step(1, [packed_grad[3], feed_sent])
    (feed_two,) = arrive([z_two(feed_sent)], [packed_grad[1]])
    (feed_one,) = merge([(feed_keep, None, 0), (Moved(feed_got), None, 0), (Moved(feed_two), None, 0)], rows=cut)
    a_diag_x, a_diag_y = merge(a_pair(3, 0), a_pair(3, cut), rows=cut, after=[feed_one])
    back_step(2, [a_diag_x, a_diag_y, slope, cond_rel])
    feed_two, a_diag_x, a_diag_y = arrive([z_two(feed_one), px(a_diag_x), py(a_diag_y)], [packed_grad[2]])
    feed_even = cat(feed_one, feed_two)
    (a_last_x,) = merge(a_pair(1, 0) + [(Moved(a_diag_y), None, -cut, cut, HALF)])
    (a_last_y,) = merge(a_pair(2, 0) + [(Moved(a_diag_x), None, 0, 0, cut)], after=[a_last_x])
    back_step(0, [packed_grad[2], a_last_y, feed_even])
    feed_odd, a_last_x, a_last_y = arrive([z_one(feed_even), px(a_last_x), py(a_last_y)], [packed_grad[0]])

    def exchange(parts):
        return [swap_dp(2 * k)(v) for k, v in enumerate(parts) if k]

    attn_parts = merge_parts([a_mine[0], *map(Moved, (a_other[0], a_last_x, a_last_y))], z_row, n_z, n_z)
    token_grads, last_sums = last_step(packed_grad, attn_w, tokens, modes, middle_grad, attn_parts)
    attn_got = exchange(attn_parts)
    feed_other = [pc(feed_even), pc(feed_odd)]
    *attn_got, feed_other[0], feed_other[1] = arrive(attn_got + feed_other, [last_sums])
    (attn_own,) = merge([(v, None, 0) for v in (attn_parts[0], *attn_got)], rows=HALF // n_z)

    place = jnp.stack([core, z])
    mode_grad = jnp.concatenate([last_sums, turn_sums, out_sums], axis=1).reshape(micro, 4, -1).transpose(1, 0, 2)
    messages = [lax.dynamic_index_in_dim(mode_grad, mp ^ r, axis=0, keepdims=False) for r in range(4)]
    rel_grid = hold(rel_grid, [attn_own])
    rel_part = jnp.pad(rel_sums(jnp.stack(rel_grid), core), ((0, 0), (0, 4 * (micro - 1)), (0, 128 - rel_bias.shape[1])))
    grad_up, grad_down = feed_final(place, feed_even, Moved(feed_odd), *map(Moved, feed_other))
    *messages[1:], attn_far = arrive(
        [by_rel[r](messages[r]) for r in (1, 2, 3)] + [swap_dp(6)(attn_own)], [attn_own, grad_up]
    )
    mode_low, *shares = mode_shares(messages, rel_part, ada_weight)
    *shares[1:], attn_two, attn_one = arrive(
        [by_rel[r](shares[r]) for r in (1, 2, 3)] + [swap_dp(4)(attn_own), swap_dp(2)(attn_own)], [attn_far]
    )
    grads = mode_rows(mp.reshape(1), mode_low, shares, slope, cond_rel)
    attn_own = jnp.concatenate([attn_own, attn_one, attn_two, attn_far])
    got = [swap_dp(k)(grads) for k in range(1, n_dp)]
    (attn_other,) = hold([pc(attn_own)], [grads])
    grad_qkv, grad_out = attn_final(place, attn_own, Moved(attn_other))
    got = arrive(got, [grad_qkv])
    grad_ada, grad_ada_bias, class_grad, grad_rel = mode_final(
        (2 * z + core).reshape(1), [grads, *got], columns, class_table.shape[0], rel_bias.shape
    )

    return (
        output,
        token_grads,
        grad_qkv,
        grad_out,
        grad_up,
        grad_down,
        grad_ada,
        grad_ada_bias,
        grad_rel,
        class_grad,
    )


def layer_norm(values):
    center = values - jnp.mean(values, axis=-1, keepdims=True)
    spread = jnp.mean(center * center, axis=-1, keepdims=True)
    return center * lax.rsqrt(spread + EPS)


def modulate(values, shift, scale):
    return layer_norm(values) * (1.0 + scale) + shift


def gelu_tanh(values):
    return (
        0.5
        * values
        * (
            1.0
            + jnp.tanh(math.sqrt(2.0 / math.pi) * (values + 0.044715 * values * values * values))
        )
    )


def condition_whole(timesteps, classes, class_table):
    half_width = class_table.shape[1] // 2
    frequency = jnp.exp(
        -math.log(10000.0) * jnp.arange(half_width).astype(class_table.dtype) / half_width
    )
    phase_angle = timesteps.astype(class_table.dtype)[..., None] * frequency
    sinusoid = jnp.concatenate([jnp.cos(phase_angle), jnp.sin(phase_angle)], axis=-1)
    onehot = (classes[..., None] == jnp.arange(class_table.shape[0])[None, None, :]).astype(
        class_table.dtype
    )
    lookup = jnp.einsum("mwc,cd->mwd", onehot, class_table, precision=precise)
    return silu_plain(sinusoid + lookup)


def axis_table(rel_part, window_span):
    places = jnp.arange(window_span)
    offsets = places[:, None] - places[None, :] + window_span - 1
    onehot = (offsets[:, :, None] == jnp.arange(2 * window_span - 1)[None, None, :]).astype(
        rel_part.dtype
    )
    return jnp.einsum("hr,abr->hab", rel_part, onehot, precision=precise)


def window_bias(rel_bias):
    frame_part = axis_table(rel_bias[:, : 2 * WT - 1], WT)
    row_part = axis_table(rel_bias[:, 2 * WT - 1 : 2 * WT + 2 * WH - 2], WH)
    column_part = axis_table(rel_bias[:, 2 * WT + 2 * WH - 2 :], WW)
    full_bias = (
        frame_part[:, :, None, None, :, None, None]
        + row_part[:, None, :, None, None, :, None]
        + column_part[:, None, None, :, None, None, :]
    )
    return full_bias.reshape(rel_bias.shape[0], WIN, WIN)


def attention_scores(query_part, key_part, bias_full, masks):
    scores = (
        jnp.einsum("wqhd,wkhd->whqk", query_part, key_part, preferred_element_type=jnp.float32)
        * HD ** (-0.5)
        + bias_full[None]
    )
    return jnp.where(masks[:, None, None, :], scores, -1e30)


def local_general(
    tokens,
    cotangent,
    qkv_weight,
    out_weight,
    up_weight,
    down_weight,
    ada_weight,
    ada_bias,
    rel_bias,
    class_table,
    lengths,
    timesteps,
    classes,
):
    micro_count = tokens.shape[0]
    row_count = tokens.shape[1]
    win_count = lengths.shape[1]
    heads_here = rel_bias.shape[0]
    head_scale = HD ** (-0.5)
    first_row = lax.axis_index("mp") * row_count
    row_window = (first_row + jnp.arange(row_count)) // WIN
    spread_rows = (row_window[:, None] == jnp.arange(win_count)[None, :]).astype(jnp.float32)
    cond_low = condition_whole(timesteps, classes, class_table).astype(jnp.bfloat16)
    mode_cols = jnp.einsum(
        "mwd,de->mwe", cond_low, ada_weight, preferred_element_type=jnp.float32
    ) + ada_bias.astype(jnp.float32)
    mode_all = lax.all_gather(mode_cols, "mp", axis=2, tiled=True)
    bias_full, bias_pull = jax.vjp(window_bias, rel_bias)
    frame_of = jnp.arange(WIN) // (WH * WW)
    grad_qkv = jnp.zeros(qkv_weight.shape, jnp.float32)
    grad_out = jnp.zeros(out_weight.shape, jnp.float32)
    grad_up = jnp.zeros(up_weight.shape, jnp.float32)
    grad_down = jnp.zeros(down_weight.shape, jnp.float32)
    grad_rel = jnp.zeros(rel_bias.shape, jnp.float32)
    mode_parts = []
    outputs = []
    token_grads = []
    for micro_step in range(micro_count):
        mode_rows = jnp.dot(spread_rows, mode_all[micro_step], precision=precise)
        shift_attn, scale_attn, gate_attn, shift_mlp, scale_mlp, gate_mlp = jnp.split(
            mode_rows, 6, axis=1
        )
        inputs = tokens[micro_step].astype(jnp.float32)
        normed_one, pull_one = jax.vjp(modulate, inputs, shift_attn, scale_attn)
        gathered_one = lax.all_gather(normed_one.astype(jnp.bfloat16), "mp", axis=0, tiled=True)
        packed = jnp.dot(gathered_one, qkv_weight, preferred_element_type=jnp.float32).astype(
            jnp.bfloat16
        )
        packed = packed.reshape(win_count, WIN, heads_here, 3, HD)
        query_part = packed[:, :, :, 0]
        key_part = packed[:, :, :, 1]
        value_part = packed[:, :, :, 2]
        masks = frame_of[None, :] < lengths[micro_step][:, None]
        scores = attention_scores(query_part, key_part, bias_full, masks)
        top_score = jnp.max(scores, axis=-1, keepdims=True)
        expo = jnp.exp(scores - top_score)
        total = jnp.sum(expo, axis=-1, keepdims=True)
        log_total = top_score + jnp.log(total)
        probs_low = (expo / total).astype(jnp.bfloat16)
        heads_out = jnp.einsum(
            "whqk,wkhd->wqhd", probs_low, value_part, preferred_element_type=jnp.float32
        ).astype(jnp.bfloat16)
        heads_out = heads_out.reshape(win_count * WIN, heads_here * HD)
        attn_out = lax.psum_scatter(
            jnp.dot(heads_out, out_weight, preferred_element_type=jnp.float32),
            "mp",
            scatter_dimension=0,
            tiled=True,
        )
        middle = inputs + gate_attn * attn_out
        normed_two, pull_two = jax.vjp(modulate, middle, shift_mlp, scale_mlp)
        grad_y = cotangent[micro_step].astype(jnp.float32)
        down_in = (gate_mlp * grad_y).astype(jnp.bfloat16)
        gathered_two = lax.all_gather(normed_two.astype(jnp.bfloat16), "mp", axis=0, tiled=True)
        hidden_pre = jnp.dot(gathered_two, up_weight, preferred_element_type=jnp.float32)
        hidden_low, gelu_pull = jax.vjp(gelu_tanh, hidden_pre)
        hidden_low = hidden_low.astype(jnp.bfloat16)
        mlp_out = lax.psum_scatter(
            jnp.dot(hidden_low, down_weight, preferred_element_type=jnp.float32),
            "mp",
            scatter_dimension=0,
            tiled=True,
        )
        down_all = lax.all_gather(down_in, "mp", axis=0, tiled=True)
        hidden_grad = jnp.einsum(
            "rd,fd->rf", down_all, down_weight, preferred_element_type=jnp.float32
        )
        micro_down = jnp.einsum(
            "rf,rd->fd", hidden_low, down_all, preferred_element_type=jnp.float32
        )
        pre_low = gelu_pull(hidden_grad)[0].astype(jnp.bfloat16)
        micro_up = jnp.einsum(
            "rd,rf->df", gathered_two, pre_low, preferred_element_type=jnp.float32
        )
        normed_two_grad = lax.psum_scatter(
            jnp.einsum("rf,df->rd", pre_low, up_weight, preferred_element_type=jnp.float32),
            "mp",
            scatter_dimension=0,
            tiled=True,
        )
        outputs.append(middle + gate_mlp * mlp_out)
        grad_gate_mlp = grad_y * mlp_out
        resid_grad, grad_shift_mlp, grad_scale_mlp = pull_two(normed_two_grad)
        middle_grad = grad_y + resid_grad
        grad_gate_attn = middle_grad * attn_out
        out_in = (gate_attn * middle_grad).astype(jnp.bfloat16)
        out_all = lax.all_gather(out_in, "mp", axis=0, tiled=True)
        micro_out = jnp.einsum("rc,rd->cd", heads_out, out_all, preferred_element_type=jnp.float32)
        heads_grad = jnp.einsum(
            "rd,cd->rc", out_all, out_weight, preferred_element_type=jnp.float32
        ).astype(jnp.bfloat16)
        heads_grad = heads_grad.reshape(win_count, WIN, heads_here, HD)
        probs = jnp.exp(attention_scores(query_part, key_part, bias_full, masks) - log_total)
        probs_low = probs.astype(jnp.bfloat16)
        value_grad = jnp.einsum(
            "whqk,wqhd->wkhd", probs_low, heads_grad, preferred_element_type=jnp.float32
        )
        probs_grad = jnp.einsum(
            "wqhd,wkhd->whqk", heads_grad, value_part, preferred_element_type=jnp.float32
        )
        score_grad = probs * (probs_grad - jnp.sum(probs * probs_grad, axis=-1, keepdims=True))
        micro_rel = bias_pull(jnp.sum(score_grad, axis=0))[0]
        score_low = (score_grad * head_scale).astype(jnp.bfloat16)
        query_grad = jnp.einsum(
            "whqk,wkhd->wqhd", score_low, key_part, preferred_element_type=jnp.float32
        )
        key_grad = jnp.einsum(
            "whqk,wqhd->wkhd", score_low, query_part, preferred_element_type=jnp.float32
        )
        packed_grad = jnp.stack([query_grad, key_grad, value_grad], axis=3).astype(jnp.bfloat16)
        packed_grad = packed_grad.reshape(win_count * WIN, heads_here * 3 * HD)
        micro_qkv = jnp.einsum(
            "rd,rc->dc", gathered_one, packed_grad, preferred_element_type=jnp.float32
        )
        normed_one_grad = lax.psum_scatter(
            jnp.einsum("rc,dc->rd", packed_grad, qkv_weight, preferred_element_type=jnp.float32),
            "mp",
            scatter_dimension=0,
            tiled=True,
        )
        input_grad, grad_shift_attn, grad_scale_attn = pull_one(normed_one_grad)
        token_grads.append(middle_grad + input_grad)
        row_modes = jnp.concatenate(
            [
                grad_shift_attn,
                grad_scale_attn,
                grad_gate_attn,
                grad_shift_mlp,
                grad_scale_mlp,
                grad_gate_mlp,
            ],
            axis=1,
        )
        mode_parts.append(jnp.einsum("rw,re->we", spread_rows, row_modes, precision=precise))
        local_grads = (micro_qkv, micro_out, micro_rel, micro_up, micro_down)
        grad_qkv = grad_qkv + local_grads[0]
        grad_out = grad_out + local_grads[1]
        grad_rel = grad_rel + local_grads[2]
        grad_up = grad_up + local_grads[3]
        grad_down = grad_down + local_grads[4]
    mode_grad_cols = lax.psum_scatter(jnp.stack(mode_parts), "mp", scatter_dimension=2, tiled=True)
    mode_low = mode_grad_cols.astype(jnp.bfloat16)
    grad_ada = jnp.einsum("mwd,mwe->de", cond_low, mode_low, preferred_element_type=jnp.float32)
    grad_ada_bias = jnp.sum(mode_grad_cols, axis=(0, 1))
    cond_grad = jnp.einsum("mwe,de->mwd", mode_low, ada_weight, preferred_element_type=jnp.float32)
    cond_value, cond_pull = jax.vjp(partial(condition_whole, timesteps, classes), class_table)
    class_total = lax.psum(cond_pull(cond_grad)[0], ("dp", "mp"))
    grad_qkv, grad_out, grad_up, grad_down, grad_rel, grad_ada, grad_ada_bias = lax.psum(
        (grad_qkv, grad_out, grad_up, grad_down, grad_rel, grad_ada, grad_ada_bias), "dp"
    )
    return (
        jnp.stack(outputs).astype(jnp.bfloat16),
        jnp.stack(token_grads).astype(jnp.bfloat16),
        grad_qkv,
        grad_out,
        grad_up,
        grad_down,
        grad_ada,
        grad_ada_bias,
        grad_rel,
        class_total,
    )


def solution(mesh):
    n_dp, n_mp = mesh.shape["dp"], mesh.shape["mp"]

    def specs(*dp):
        rows = P(None, (*dp, "mp"), None)
        weights = (P(None, "mp"), P("mp", None), P(None, "mp"), P("mp", None), P(None, "mp"), P("mp"), P("mp", None), P())
        return (rows, rows, *weights, *[P(None, dp)] * 3), (rows, rows, *weights)

    def program(tokens, *arrays):
        if n_mp == 4 and n_dp % 2 == 0 and tokens.shape[1] == n_dp * n_mp * WIN:
            devices = mesh.devices.reshape(n_dp // 2, 2, n_mp)
            split = jax.sharding.Mesh(devices, ("z", "core", "mp"))
            ins, outs = specs("z", "core")
            step = jax.shard_map(
                partial(local_windows, (n_dp // 2, n_mp)), mesh=split, in_specs=ins, out_specs=outs, check_vma=False
            )
        else:
            ins, outs = specs("dp")
            step = jax.shard_map(local_general, mesh=mesh, in_specs=ins, out_specs=outs, check_vma=False)
        return step(tokens, *arrays)

    return program
```

```python
from functools import partial
import math
from typing import NamedTuple

import jax
import jax.numpy as jnp
import numpy as np
from jax import lax
from jax.experimental import pallas as pl
from jax.experimental.pallas import tpu as pltpu
from jax.sharding import PartitionSpec as P

HD = 64
WT = 5
WH = 8
WW = 8
WIN = 320
D = 1024
EPS = 1e-06
NOFF = WT + WH + WW
C0 = math.sqrt(2.0 / math.pi)
C1 = 0.044715
precise = lax.Precision.HIGHEST
f32 = jnp.float32
bf16 = jnp.bfloat16
NN = (((1,), (0,)), ((), ()))
NT = (((1,), (1,)), ((), ()))
TN = (((0,), (0,)), ((), ()))
HALF = 512
QKV = 384


def mm(a, b, dims=NN):
    return lax.dot_general(a, b, dims, preferred_element_type=f32)


def whole(*dims):
    return pl.BlockSpec(dims, lambda i, *_: (0,) * len(dims))


def part(index, *dims):
    return pl.BlockSpec(dims, lambda i, *_: index)


def rows_of(width):
    return pl.BlockSpec((WIN, width), lambda i, *_: (i, 0))


def window_of(*dims):
    return pl.BlockSpec((None,) + dims, lambda i, *_: (i,) + (0,) * len(dims))


def shape(dims, dtype):
    return pltpu.HBM(dims, dtype)


def near(dims, dtype):
    return jax.ShapeDtypeStruct(dims, dtype)


HBM = pl.BlockSpec(memory_space=pltpu.HBM)
VMEM = pl.BlockSpec(memory_space=pltpu.VMEM)


class Loads:
    def __init__(self, sems):
        self.sems, self.copies = sems, []

    def add(self, source, target):
        self.copies.append(pltpu.make_async_copy(source, target, self.sems.at[len(self.copies)]))
        return self.copies[-1]

    def start(self):
        for copy in self.copies:
            copy.start()

    def wait(self):
        for copy in self.copies:
            copy.wait()


class Moved(NamedTuple):
    array: jax.Array


def in_hbm(array):
    return pltpu.with_memory_space_constraint(array, pltpu.HBM)


def operand(array, spec):
    if isinstance(array, Moved):
        return array.array, pl.BlockSpec(memory_space=pl.ANY) if spec is HBM else spec
    return array if spec is VMEM else in_hbm(array), spec


def run(kernel, name, grid, ins, outs, scratch=(), after=(), scalars=(), flops=0, moved=0, vmem=24):
    first = len(scalars) + len(ins)

    ins = [operand(array, spec) for array, spec in ins]

    def body(*refs):
        kernel(*refs[:first], *refs[first + len(after) :])

    return pl.pallas_call(
        body,
        grid_spec=pltpu.PrefetchScalarGridSpec(
            num_scalar_prefetch=len(scalars),
            grid=(grid,),
            in_specs=[spec for _, spec in ins] + [HBM] * len(after),
            out_specs=[spec for _, spec in outs],
            scratch_shapes=list(scratch),
        ),
        out_shape=[what for what, _ in outs],
        compiler_params=pltpu.CompilerParams(vmem_limit_bytes=vmem * 2**20),
        cost_estimate=pl.CostEstimate(flops=1000, bytes_accessed=1000, transcendentals=0),
        name=name,
    )(*scalars, *[array for array, _ in ins], *map(in_hbm, after))


def hold(values, after=(), flops=1000):
    anywhere = pl.BlockSpec(memory_space=pl.ANY)
    return pl.pallas_call(
        lambda *refs: None,
        in_specs=[anywhere] * len(values) + [HBM] * len(after),
        out_specs=[anywhere] * len(values),
        out_shape=[near(v.shape, v.dtype) for v in values],
        input_output_aliases={i: i for i in range(len(values))},
        cost_estimate=pl.CostEstimate(flops=flops, bytes_accessed=1000, transcendentals=0),
        name="hold",
    )(*values, *map(in_hbm, after))


def arrive(values, after):
    return hold(values, after, 30 * 10**9)


def ln_parts(values):
    center = values - jnp.mean(values, axis=-1, keepdims=True)
    rstd = lax.rsqrt(jnp.mean(center * center, axis=-1, keepdims=True) + EPS)
    return center * rstd, rstd


def ln_back(grad, scale, hat, rstd):
    inner = grad * (1.0 + scale)
    mean_one = jnp.mean(inner, axis=-1, keepdims=True)
    mean_two = jnp.mean(inner * hat, axis=-1, keepdims=True)
    return rstd * (inner - mean_one - hat * mean_two)


def hot_rows(count, source):
    row = lax.broadcasted_iota(jnp.int32, (count, count), 0)
    col = lax.broadcasted_iota(jnp.int32, (count, count), 1)
    return col == source(row), row


def qkv_source(core):
    def source(row):
        half = jnp.where(row >= QKV, 1, 0)
        inner = row - half * QKV
        head = 2 * (half ^ core) + ((inner & 127) >> 6)
        return head * 3 * HD + (inner >> 7) * HD + (inner & 63)

    return source


def attn_rows_kernel(core_ref, qkv_ref, out_ref, own0, own1):
    core = core_ref[0]
    hot, row = hot_rows(2 * QKV, qkv_source(core))
    inner = jnp.where(row >= QKV, row - QKV, row)
    hot = jnp.where(hot, jnp.where(inner < 128, HD**-0.5, 1.0), 0.0).astype(bf16)
    rows = mm(hot, qkv_ref[...], NT).astype(bf16)
    for h, own in enumerate((own0, own1)):
        own[:QKV] = rows[h * QKV : (h + 1) * QKV]
        own[QKV:] = out_ref[pl.ds(pl.multiple_of((core ^ h) * 128, 128), 128)]


def feed_rows_kernel(core_ref, up_ref, down_ref, up0, down0, up1, down1):
    core = core_ref[0]
    hot, _ = hot_rows(2 * HALF, lambda row: row ^ (core * HALF))
    rows = mm(jnp.where(hot, 1.0, 0.0).astype(bf16), up_ref[...], NT).astype(bf16)
    for h, (up, down) in enumerate(((up0, down0), (up1, down1))):
        up[0] = rows[h * HALF : (h + 1) * HALF]
        down[0] = down_ref[pl.ds(pl.multiple_of((core ^ h) * HALF, HALF), HALF)]


def attn_rows(core, qkv, out, after):
    half = (shape((HALF, D), bf16), whole(HALF, D))
    ins = [(qkv, whole(D, 2 * QKV)), (out, whole(256, D))]
    return run(attn_rows_kernel, "attn_rows", 1, ins, [half, half], (), after, [core], 1e9, 4e6)


def feed_rows(core, up, down, after):
    half = (shape((1, HALF, D), bf16), whole(1, HALF, D))
    ins = [(up, whole(D, 2 * HALF)), (down, whole(2 * HALF, D))]
    return run(feed_rows_kernel, "feed_rows", 1, ins, [half] * 4, (), after, [core], 2e9, 8e6)


def attend_kernel(len_ref, x_ref, mode_ref, wa_ref, wb_ref, tbl_ref, e_ref, *rest):
    n1_ref, packed_ref, heads_ref, probs_ref, w_all, kb_all, sems = rest if len(rest) == 7 else (None, *rest)
    w = pl.program_id(0)

    @pl.when(w == 0)
    def _():
        loads = Loads(sems)
        loads.add(wa_ref.at[:QKV], w_all.at[:QKV])
        loads.add(wb_ref.at[:QKV], w_all.at[QKV:])
        loads.start()
        for p in range(2):
            kb_all[p] = mm(e_ref[...], tbl_ref[p]).astype(bf16)
        loads.wait()

    if n1_ref is None:
        x = x_ref[...]
    else:
        hat, _ = ln_parts(x_ref[...].astype(f32))
        x = (hat * (1.0 + mode_ref[1:2]) + mode_ref[0:1]).astype(bf16)
        n1_ref[...] = x
    pk = mm(x, w_all[...], NT).astype(bf16)
    packed_ref[...] = pk
    lane = lax.broadcasted_iota(jnp.int32, (WIN, 128), 1)
    low = lane < 64
    frame = lax.broadcasted_iota(jnp.int32, (WIN, 128), 0) // (WH * WW)
    mask_lane = (lane & 63) == 2 * NOFF
    hide = jnp.where(frame < len_ref[w], 0.0, -1e30).astype(bf16)
    for p in range(2):
        q = pk[:, p * QKV : p * QKV + 128]
        k = pk[:, p * QKV + 128 : p * QKV + 256]
        v = pk[:, p * QKV + 256 : p * QKV + 384]
        kb = jnp.where(mask_lane, hide, kb_all[p])
        v_rows = v.T
        outs = []
        for i in range(2):
            mine = low if i == 0 else ~low
            s = mm(jnp.where(mine, k, kb), jnp.where(mine, q, e_ref[...]), NT)
            ex = jnp.exp(s - jnp.max(s, axis=0, keepdims=True))
            pr = (ex * (1.0 / jnp.sum(ex, axis=0, keepdims=True))).astype(bf16)
            probs_ref[2 * p + i] = pr
            outs.append(mm(v_rows[i * HD : (i + 1) * HD], pr))
        heads_ref[:, p * 128 : (p + 1) * 128] = jnp.concatenate(outs, axis=0).T.astype(bf16)


def attend(lengths, source, modes, weight, table, query_hot, after=()):
    count = lengths.shape[0]
    rows = count * WIN
    first = source.ndim == 3
    outs = [
        (shape((rows, 2 * QKV), bf16), rows_of(2 * QKV)),
        (shape((rows, 256), bf16), rows_of(256)),
        (shape((count * 4, WIN, WIN), bf16), pl.BlockSpec((4, WIN, WIN), lambda i, l: (i, 0, 0))),
    ]
    if first:
        outs = [(near((rows, D), bf16), rows_of(D))] + outs
    return run(
        attend_kernel,
        "attend",
        count,
        [
            (source, window_of(WIN, D) if first else rows_of(D)),
            (modes, window_of(6, D)),
            (weight[0], HBM),
            (weight[1], HBM),
            (table, whole(2, 128, 128)),
            (query_hot, whole(WIN, 128)),
        ],
        outs,
        [pltpu.VMEM((2 * QKV, D), bf16), pltpu.VMEM((2, WIN, 128), bf16), pltpu.SemaphoreType.DMA((2,))],
        after,
        [lengths],
        9e9,
        12e6,
    )


def middle_kernel(h0, h1, h2, h3, w0, w1, w2, w3, w4, w5, w6, w7, tok, cot, mode, attn_ref, mid_ref, n2_ref, di_ref, w_all, sems):
    @pl.when(pl.program_id(0) == 0)
    def _():
        loads = Loads(sems)
        for i, ref in enumerate((w0, w1, w2, w3, w4, w5, w6, w7)):
            loads.add(ref.at[QKV:], w_all.at[pl.ds(i * 128, 128)])
        loads.start()
        loads.wait()

    heads = jnp.concatenate([h0[...], h1[...], h2[...], h3[...]], axis=1)
    attn = mm(heads, w_all[...])
    attn_ref[...] = attn.astype(bf16)
    middle = tok[...].astype(f32) + mode[2:3] * attn
    mid_ref[...] = middle
    hat, _ = ln_parts(middle)
    n2_ref[...] = (hat * (1.0 + mode[4:5]) + mode[3:4]).astype(bf16)
    di_ref[...] = (mode[5:6] * cot[...].astype(f32)).astype(bf16)


def middle_step(heads, weights, tokens, cotangent, modes, after=()):
    count = tokens.shape[0]
    rows = count * WIN
    return run(
        middle_kernel,
        "middle",
        count,
        [(h, rows_of(256)) for h in heads]
        + [(half, HBM) for pair in weights for half in pair]
        + [(tokens, window_of(WIN, D)), (cotangent, window_of(WIN, D)), (modes, window_of(6, D))],
        [(shape((rows, D), kind), rows_of(D)) for kind in (bf16, f32)] + [(near((rows, D), bf16), rows_of(D))] * 2,
        [pltpu.VMEM((D, D), bf16), pltpu.SemaphoreType.DMA((8,))],
        after,
        flops=2.7e9,
        moved=22e6,
    )


CHUNK = 256


def feed_kernel(places, n2, di, up0, dn0, up1, dn1, hid_hbm, pre_hbm, g0_hbm, g1_hbm, weight, hid, pre, grad, in_sems, out_sems):
    loads, stores = Loads(in_sems), Loads(out_sems)
    for i, ref in enumerate((up0, dn0, up1, dn1)):
        loads.add(ref.at[places[i]], weight.at[i // 2, i % 2])
    for i in (2, 3, 0, 1):
        loads.copies[i].start()

    def store(from_ref, to_ref):
        stores.add(from_ref, to_ref).start()

    for h, g_hbm in ((1, g1_hbm), (0, g0_hbm)):
        units = pl.ds(h * HALF, HALF)
        loads.copies[2 * h].wait()
        loads.copies[2 * h + 1].wait()
        for i in range(n2.shape[0] // CHUNK):
            rows = pl.ds(i * CHUNK, CHUNK)
            v = mm(n2[rows], weight[h, 0], NT)
            hg = mm(di[rows], weight[h, 1], NT)
            v2 = v * v
            t = jnp.tanh(v * (C0 + (C0 * C1) * v2))
            share = 0.5 + 0.5 * t
            hid[h, rows] = (v * share).astype(bf16)
            slope = share + (0.5 * v) * (1.0 - t * t) * (C0 + (3.0 * C0 * C1) * v2)
            pre[h, rows] = (slope * hg).astype(bf16)
        store(hid.at[h], hid_hbm.at[:, units])
        store(pre.at[h], pre_hbm.at[:, units])
        grad[h, 1] = mm(hid[h], di[...], TN).astype(bf16)
        store(grad.at[h, 1], g_hbm.at[1])
        grad[h, 0] = mm(pre[h], n2[...], TN).astype(bf16)
        store(grad.at[h, 0], g_hbm.at[0])
    stores.wait()


def feed(normed, down_in, weight, after=()):
    rows = normed.shape[0]
    halves = [array for half in weight for array, _ in half]
    places = [place for half in weight for _, place in half]
    return run(
        partial(feed_kernel, places),
        "feed",
        1,
        [(normed, VMEM), (down_in, VMEM)] + [(array, HBM) for array in halves],
        [(shape((rows, 2 * HALF), bf16), HBM)] * 2 + [(shape((2, HALF, D), bf16), HBM)] * 2,
        [pltpu.VMEM((2, 2, HALF, D), bf16)]
        + [pltpu.VMEM((2, rows, HALF), bf16)] * 2
        + [pltpu.VMEM((2, 2, HALF, D), bf16), pltpu.SemaphoreType.DMA((4,)), pltpu.SemaphoreType.DMA((8,))],
        after,
        vmem=32,
    )


def unit_sums(sources, pieces, places, weight, acc, sems):
    w = pl.program_id(0)

    def span(i):
        return slice(i % 2 * HALF, (i % 2 + 1) * HALF)

    @pl.when(w == 0)
    def _():
        loads = Loads(sems)
        for i, piece in enumerate(pieces):
            loads.add(piece.at[places[i]], weight.at[pl.ds(i * HALF, HALF)])
        loads.start()
        for i, copy in enumerate(loads.copies):
            copy.wait()
            term = mm(sources[i // 2][:, span(i)], weight[i * HALF : (i + 1) * HALF])
            acc[...] = term if i == 0 else acc[...] + term

    @pl.when(w > 0)
    def _():
        source = jnp.concatenate([ref[...] for ref in sources], axis=1)
        acc[...] = mm(source, weight[...])


def turn_kernel(places, p0, p1, p2, p3, w0, w1, w2, w3, w4, w5, w6, w7, mid_ref, attn_ref, cot_ref, mode_ref, *rest):
    mg_ref, oi_ref, sum_ref, weight, acc, sems = rest
    unit_sums((p0, p1, p2, p3), (w0, w1, w2, w3, w4, w5, w6, w7), places, weight, acc, sems)
    ng = acc[...]
    hat, rstd = ln_parts(mid_ref[...])
    mg = cot_ref[...].astype(f32) + ln_back(ng, mode_ref[4:5], hat, rstd)
    mg_ref[...] = mg
    oi_ref[...] = (mode_ref[2:3] * mg).astype(bf16)
    sum_ref[0:1] = jnp.sum(mg * attn_ref[...].astype(f32), axis=0, keepdims=True)
    sum_ref[1:2] = jnp.sum(ng, axis=0, keepdims=True)
    sum_ref[2:3] = jnp.sum(ng * hat, axis=0, keepdims=True)


def out_kernel(places, p0, p1, p2, p3, w0, w1, w2, w3, w4, w5, w6, w7, mid_ref, cot_ref, mode_ref, *rest):
    out_ref, sum_ref, weight, acc, sems = rest
    unit_sums((p0, p1, p2, p3), (w0, w1, w2, w3, w4, w5, w6, w7), places, weight, acc, sems)
    mlp = acc[...]
    out_ref[...] = (mid_ref[...] + mode_ref[5:6] * mlp).astype(bf16)
    sum_ref[...] = jnp.sum(cot_ref[...].astype(f32) * mlp, axis=0, keepdims=True)


def of_units(arrays, weights, which):
    halves = [half[which] for pair in weights for half in pair]
    ins = [(array, rows_of(2 * HALF)) for array in arrays] + [(array, HBM) for array, _ in halves]
    scratch = [pltpu.VMEM((8 * HALF, D), bf16), pltpu.VMEM((WIN, D), f32), pltpu.SemaphoreType.DMA((8,))]
    return ins, scratch, [place for _, place in halves]


def turn_step(pre, weights, middle, attn_out, cotangent, modes, after=()):
    count = cotangent.shape[0]
    rows = count * WIN
    ins, scratch, places = of_units(pre, weights, 0)
    return run(
        partial(turn_kernel, places),
        "turn",
        count,
        ins
        + [(middle, rows_of(D)), (attn_out, rows_of(D)), (cotangent, window_of(WIN, D)), (modes, window_of(6, D))],
        [
            (shape((rows, D), f32), rows_of(D)),
            (near((rows, D), bf16), rows_of(D)),
            (shape((count, 3, D), f32), window_of(3, D)),
        ],
        scratch,
        after,
        vmem=36,
        flops=10.7e9,
        moved=35e6,
    )


def out_step(hid, weights, middle, cotangent, modes, after=()):
    count = cotangent.shape[0]
    ins, scratch, places = of_units(hid, weights, 1)
    return run(
        partial(out_kernel, places),
        "output",
        count,
        ins + [(middle, rows_of(D)), (cotangent, window_of(WIN, D)), (modes, window_of(6, D))],
        [(shape((count, WIN, D), bf16), window_of(WIN, D)), (shape((count, 1, D), f32), window_of(1, D))],
        scratch,
        after,
        vmem=36,
        flops=10.7e9,
        moved=30e6,
    )


def attend_back_kernel(
    oi_ref, o0, o1, pk_ref, pr_ref, e_ref, n1_ref, oi_all, ho_hbm, pg_ref, g0_ref, g1_ref, rel_ref, *scratch
):
    pg_all, t_all, ow, ho_ref, sems = scratch
    w = pl.program_id(0)
    loads = Loads(sems)
    weights = [loads.add(o.at[QKV:], ow.at[pl.ds(i * 128, 128)]) for i, o in enumerate((o0, o1))]
    heads = loads.add(ho_hbm, ho_ref)

    @pl.when(w == 0)
    def _():
        loads.start()
        t_all[...] = jnp.zeros_like(t_all)
        for copy in weights:
            copy.wait()

    hg = mm(oi_ref[...], ow[...], NT).astype(bf16)
    pk = pk_ref[...]
    low = lax.broadcasted_iota(jnp.int32, (WIN, 128), 1) < 64
    for p in range(2):
        q = pk[:, p * QKV : p * QKV + 128]
        k = pk[:, p * QKV + 128 : p * QKV + 256]
        v = pk[:, p * QKV + 256 : p * QKV + 384]
        do = hg[:, p * 128 : (p + 1) * 128]
        k_rows = k.T
        dv, dq, dk = [], [], []
        for i in range(2):
            mine = low if i == 0 else ~low
            qa = jnp.where(mine, q, e_ref[...])
            dp = mm(jnp.where(mine, v, jnp.zeros_like(v)), do, NT)
            prl = pr_ref[2 * p + i]
            pr = prl.astype(f32)
            t = pr * dp
            ds = (t - pr * jnp.sum(t, axis=0, keepdims=True)).astype(bf16)
            dv.append(mm(prl, do))
            dq.append(mm(k_rows[i * HD : (i + 1) * HD], ds))
            dk.append(mm(ds, qa))
        dq = jnp.concatenate(dq, axis=0).T
        block = jnp.concatenate(
            [dq, jnp.where(low, dk[0], dk[1]), jnp.where(low, dv[0], dv[1])], axis=1
        ).astype(bf16)
        pg_ref[:, p * QKV : (p + 1) * QKV] = block
        pg_all[pl.ds(pl.multiple_of(w * WIN, WIN), WIN), p * QKV : (p + 1) * QKV] = block
        t_all[p] += jnp.where(low, dk[1], dk[0])

    @pl.when(w == pl.num_programs(0) - 1)
    def _():
        heads.wait()
        go = mm(ho_ref[...], oi_all[...], TN).astype(bf16)
        gq = mm(pg_all[...], n1_ref[...], TN).astype(bf16)
        for p, g_ref in enumerate((g0_ref, g1_ref)):
            g_ref[:QKV] = gq[p * QKV : (p + 1) * QKV]
            g_ref[QKV:] = go[p * 128 : (p + 1) * 128]
        hot = e_ref[...].astype(f32)
        for p in range(2):
            sums = lax.dot_general(hot, t_all[p], TN, precision=precise, preferred_element_type=f32)
            rel_ref[p] = sums[:32]


def attend_back(out_in, weight, packed, probs, query_hot, normed, heads, after=()):
    rows = normed.shape[0]
    return run(
        attend_back_kernel,
        "attend_back",
        rows // WIN,
        [
            (out_in, rows_of(D)),
            (weight[0], HBM),
            (weight[1], HBM),
            (packed, rows_of(2 * QKV)),
            (probs, pl.BlockSpec((4, WIN, WIN), lambda i: (i, 0, 0))),
            (query_hot, whole(WIN, 128)),
            (normed, VMEM),
            (out_in, VMEM),
            (heads, HBM),
        ],
        [
            (shape((rows, 2 * QKV), bf16), rows_of(2 * QKV)),
            (shape((HALF, D), bf16), whole(HALF, D)),
            (shape((HALF, D), bf16), whole(HALF, D)),
            (shape((2, 32, 128), f32), whole(2, 32, 128)),
        ],
        [pltpu.VMEM((rows, 2 * QKV), bf16), pltpu.VMEM((2, WIN, 128), f32), pltpu.VMEM((256, D), bf16)]
        + [pltpu.VMEM((rows, 256), bf16), pltpu.SemaphoreType.DMA((3,))],
        after,
        flops=13e9,
        moved=20e6,
    )


def last_kernel(p0, p1, p2, p3, w0, w1, w2, w3, w4, w5, w6, w7, tok_ref, mode_ref, mg_ref, out_ref, sum_ref, w_all, acc, sems):
    @pl.when(pl.program_id(0) == 0)
    def _():
        loads = Loads(sems)
        for i, ref in enumerate((w0, w1, w2, w3, w4, w5, w6, w7)):
            loads.add(ref.at[:QKV], w_all.at[pl.ds(i * QKV, QKV)])
        loads.start()
        for i, src in enumerate((p0, p1, p2, p3)):
            loads.copies[2 * i].wait()
            loads.copies[2 * i + 1].wait()
            term = mm(src[...], w_all[i * 2 * QKV : (i + 1) * 2 * QKV])
            acc[...] = term if i == 0 else acc[...] + term

    @pl.when(pl.program_id(0) > 0)
    def _():
        acc[...] = mm(jnp.concatenate([p0[...], p1[...], p2[...], p3[...]], axis=1), w_all[...])

    ng = acc[...]
    hat, rstd = ln_parts(tok_ref[...].astype(f32))
    out_ref[...] = (mg_ref[...] + ln_back(ng, mode_ref[1:2], hat, rstd)).astype(bf16)
    sum_ref[0:1] = jnp.sum(ng, axis=0, keepdims=True)
    sum_ref[1:2] = jnp.sum(ng * hat, axis=0, keepdims=True)


def last_step(packed_grads, weights, tokens, modes, middle_grad, after=()):
    count = tokens.shape[0]
    return run(
        last_kernel,
        "last",
        count,
        [(array, rows_of(2 * QKV)) for array in packed_grads]
        + [(half, HBM) for pair in weights for half in pair]
        + [(tokens, window_of(WIN, D)), (modes, window_of(6, D)), (middle_grad, rows_of(D))],
        [(shape((count, WIN, D), bf16), window_of(WIN, D)), (shape((count, 2, D), f32), window_of(2, D))],
        [pltpu.VMEM((8 * QKV, D), bf16), pltpu.VMEM((WIN, D), f32), pltpu.SemaphoreType.DMA((8,))],
        after,
        flops=8e9,
        moved=24e6,
    )


def merge_kernel(sums, count, *refs):
    i = pl.program_id(0)
    refs = list(refs)
    outs = refs[len(refs) - len(sums) :]
    for spans, out in zip(sums, outs):
        value = None
        for first, last in spans:
            term = refs.pop(0)[...].astype(f32)
            if (first, last) != (0, count):
                term = jnp.where((i >= first) & (i < last), term, 0.0)
            value = term if value is None else value + term
        out[...] = value.astype(bf16)


def merge(*sums, rows=HALF, after=()):
    block = min(256, rows)
    ins, spans = [], []
    for terms in sums:
        spans.append([])
        for array, place, start, *limits in terms:
            first, last = [limit // block for limit in (limits or (0, rows))]
            start = start // block

            def at(i, start=start, first=first, last=last):
                return jnp.clip(i, first, last - 1) + start

            if place is None:
                spec = pl.BlockSpec((block, D), lambda i, at=at: (at(i), 0))
            else:
                spec = pl.BlockSpec((None, block, D), lambda i, p=place, at=at: (p, at(i), 0))
            ins.append((array, spec))
            spans[-1].append((first, last))
    out = (shape((rows, D), bf16), pl.BlockSpec((block, D), lambda i: (i, 0)))
    return run(partial(merge_kernel, spans, rows // block), "merge", rows // block, ins, [out] * len(sums), (), after)


def parts_kernel(count, only, z_ref, *refs):
    which_sum = pl.program_id(0) % (1 + max([0] + [w for w in only if w is not None]))
    terms = len(only)
    for k in range(count):
        value = None
        for ref, which in zip(refs[k * terms : (k + 1) * terms], only):
            term = ref[...].astype(f32)
            if which is not None:
                term = jnp.where(which_sum == which, term, 0.0)
            value = term if value is None else value + term
        refs[count * terms + k][...] = value.astype(bf16)


def merge_parts(terms, z, count, outputs):
    size = HALF // count
    sums = 2 if terms[0].ndim == 3 else 1
    ins, only = [], []
    for j in range(outputs):
        for term in terms:
            array, which = term if type(term) is tuple else (term, None)
            dims = array.array.ndim if isinstance(array, Moved) else array.ndim

            def at(i, zr, j=j):
                return zr[0] ^ (i // sums * outputs + j)

            if dims == 3:
                spec = pl.BlockSpec((None, size, D), lambda i, zr, at=at: (i % sums, at(i, zr), 0))
            else:
                spec = pl.BlockSpec((size, D), lambda i, zr, at=at: (at(i, zr), 0))
            ins.append((array, spec))
            only.append(which)
    grid = sums * count // outputs
    outs = [(shape((grid * size, D), bf16), pl.BlockSpec((size, D), lambda i, zr: (i, 0)))] * outputs
    return run(partial(parts_kernel, outputs, only[: len(terms)]), "merge_parts", grid, ins, outs, (), (), [z])


def attn_final_kernel(place_ref, a_ref, b_ref, qkv_ref, out_ref, rows, hot):
    core, z = place_ref[0], place_ref[1]
    size = HALF // 4

    @pl.when(pl.program_id(0) == 0)
    def _():
        match, row = hot_rows(2 * QKV, qkv_source(core))
        inner = jnp.where(row >= QKV, row - QKV, row)
        hot[...] = jnp.where(match, jnp.where(inner < 128, HD**-0.5, 1.0), 0.0).astype(bf16)

    for h, ref in enumerate((a_ref, b_ref)):
        for k in range(4):
            part_at = z ^ k
            block = ref[k * size : (k + 1) * size]

            @pl.when(part_at < 3)
            def _():
                rows[pl.ds(pl.multiple_of(h * QKV + part_at * size, size), size)] = block

            @pl.when(part_at == 3)
            def _():
                out_ref[pl.ds(pl.multiple_of((core ^ h) * size, size), size)] = block.astype(f32)

    qkv_ref[...] = mm(rows[...], hot[...], TN)


def columns_of(rows):
    return pl.BlockSpec((rows, 256), lambda i, *_: (0, i))


def attn_final(place, a, b):
    ins = [(a, columns_of(HALF)), (b, columns_of(HALF))]
    outs = [
        (shape((D, 2 * QKV), f32), pl.BlockSpec((256, 2 * QKV), lambda i, *_: (i, 0))),
        (shape((256, D), f32), columns_of(256)),
    ]
    scratch = [pltpu.VMEM((2 * QKV, 256), bf16), pltpu.VMEM((2 * QKV, 2 * QKV), bf16)]
    return run(attn_final_kernel, "attn_final", D // 256, ins, outs, scratch, (), [place])


def feed_final_kernel(place_ref, *refs):
    up_ref, down_ref, rows, hot = refs[4:]
    core, z = place_ref[0], place_ref[1]
    size = HALF // 4

    @pl.when(pl.program_id(0) == 0)
    def _():
        hot[...] = jnp.where(hot_rows(2 * HALF, lambda row: row ^ (core * HALF))[0], 1.0, 0.0).astype(bf16)

    for h in range(2):
        for k, (ref, first) in enumerate(((refs[2 * h], 0), (refs[2 * h + 1], 0), (refs[2 * h], 2), (refs[2 * h + 1], 2))):
            start = (z ^ k) * size
            rows[pl.ds(pl.multiple_of(h * HALF + start, size), size)] = ref[first * size : (first + 1) * size]
            block = ref[(first + 1) * size : (first + 2) * size].astype(f32)
            down_ref[pl.ds(pl.multiple_of((core ^ h) * HALF + start, size), size)] = block
    up_ref[...] = mm(rows[...], hot[...], TN)


def feed_final(place, even, odd, other_even, other_odd):
    ins = [(v, columns_of(HALF)) for v in (even, odd, other_even, other_odd)]
    outs = [
        (shape((D, 2 * HALF), f32), pl.BlockSpec((256, 2 * HALF), lambda i, *_: (i, 0))),
        (shape((2 * HALF, D), f32), columns_of(2 * HALF)),
    ]
    scratch = [pltpu.VMEM((2 * HALF, 256), bf16), pltpu.VMEM((2 * HALF, 2 * HALF), bf16)]
    return run(feed_final_kernel, "feed_final", D // 256, ins, outs, scratch, (), [place])


def mode_shares_kernel(m0, m1, m2, m3, rel_ref, ada_ref, low_ref, s0, s1, s2, s3, rows):
    count = m0.shape[0]
    for r, ref in enumerate((m0, m1, m2, m3)):
        rows[r * count : (r + 1) * count] = ref[...]
    low = rows[...].astype(bf16)
    low_ref[...] = low
    cond = mm(low, ada_ref[...], NT)
    for r, ref in enumerate((s0, s1, s2, s3)):
        ref[:, :D] = cond
        ref[:, D:] = rel_ref[r]


def mode_shares(messages, rel_part, ada_weight):
    count, columns = messages[0].shape
    rows = 4 * count
    ins = [(v, whole(count, columns)) for v in messages]
    ins += [(rel_part, whole(4, rows, 128)), (ada_weight, whole(D, columns))]
    outs = [(shape((rows, columns), bf16), whole(rows, columns))] + [(shape((rows, D + 128), f32), whole(rows, D + 128))] * 4
    return run(mode_shares_kernel, "mode_shares", 1, ins, outs, [pltpu.VMEM((rows, columns), f32)])


def mode_rows_kernel(mp_ref, low_ref, s0, s1, s2, s3, slope_ref, cond_ref, out_ref):
    rows, columns = low_ref.shape
    count = rows // 4
    mp = mp_ref[0]
    moved = [s0[:, :D]]
    for k, ref in ((1, s1), (2, s2), (3, s3)):
        blocks = [ref[(r ^ k) * count : ((r ^ k) + 1) * count, :D] for r in range(4)]
        moved.append(jnp.concatenate(blocks, axis=0))
    cond = (moved[0] + moved[1]) + (moved[2] + moved[3])
    value = (cond * slope_ref[...]).astype(bf16)
    row = lax.broadcasted_iota(jnp.int32, (rows, rows), 0)
    col = lax.broadcasted_iota(jnp.int32, (rows, rows), 1)
    hot = jnp.where(col == row ^ (mp * count), 1.0, 0.0).astype(bf16)
    out_ref[:, :columns] = low_ref[...]
    out_ref[:, columns : columns + D] = mm(hot, value).astype(bf16)
    out_ref[:, columns + D : columns + D + 128] = (s0[:, D:] + s1[:, D:] + s2[:, D:] + s3[:, D:]).astype(bf16)
    out_ref[:, columns + D + 128 :] = cond_ref[...]


def mode_rows(mp, low, shares, slope, cond):
    rows, columns = low.shape
    width = columns + 2 * (D + 128)
    ins = [(low, whole(rows, columns))] + [(v, whole(rows, D + 128)) for v in shares]
    ins += [(slope, whole(rows, D)), (cond, whole(rows, D + 128))]
    outs = [(shape((rows, width), bf16), whole(rows, width))]
    return run(mode_rows_kernel, "mode_rows", 1, ins, outs, (), (), [mp])[0]


def mode_final_kernel(dp_ref, own_ref, other_ref, ada_ref, bias_ref, class_ref, rel_ref, rows, *, count):
    size = own_ref.shape[0] // count
    columns = ada_ref.shape[1]
    marks = [0, columns, columns + D, columns + D + 128, columns + 2 * D + 128, columns + 2 * D + 256]
    for core, ref in enumerate((own_ref, other_ref)):
        for k in range(count):
            at = (dp_ref[0] ^ (2 * k + core)) * size
            rows[pl.ds(pl.multiple_of(at, size), size)] = ref[k * size : (k + 1) * size]
    modes, classes, rel, cond, index = [rows[:, i:j] for i, j in zip(marks, marks[1:])]
    ada_ref[...] = mm(cond, modes, TN)
    bias_ref[...] = jnp.sum(modes.astype(f32), axis=0)
    lane = lax.broadcasted_iota(jnp.int32, index.shape, 1).astype(f32)
    hot = jnp.where(lane == index[:, :1].astype(f32), 1.0, 0.0).astype(bf16)
    class_ref[...] = mm(hot, classes, TN)[: class_ref.shape[0]]
    total = rel[:size].astype(f32)
    for i in range(1, 2 * count):
        total = total + rel[i * size : (i + 1) * size].astype(f32)
    rel_ref[...] = total[: rel_ref.shape[0], : rel_ref.shape[1]]


def mode_final(dp, own, other, count, columns, class_count, rel_shape):
    size, width = own.shape
    outs = [(shape(dims, f32), whole(*dims)) for dims in ((D, columns), (columns,), (class_count, D), rel_shape)]
    kernel = partial(mode_final_kernel, count=count)
    ins = [(own, whole(size, width)), (other, whole(size, width))]
    return run(kernel, "mode_final", 1, ins, outs, [pltpu.VMEM((2 * size, width), bf16)], (), [dp], vmem=32)


def silu_plain(values):
    return values / (1.0 + jnp.exp(-values))


def condition(timesteps, classes, class_table):
    half_width = class_table.shape[1] // 2
    frequency = jnp.exp(
        -math.log(10000.0) * jnp.arange(half_width).astype(class_table.dtype) / half_width
    )
    phase_angle = timesteps.astype(class_table.dtype)[..., None] * frequency
    sinusoid = jnp.concatenate([jnp.cos(phase_angle), jnp.sin(phase_angle)], axis=-1)
    onehot = (classes[..., None] == jnp.arange(class_table.shape[0])).astype(class_table.dtype)
    lookup = jnp.einsum("mwc,cd->mwd", onehot, class_table, precision=precise)
    return sinusoid + lookup


SPANS = ((0, 0, WT), (WT, 2 * WT - 1, WH), (WT + WH, 2 * WT + 2 * WH - 2, WW))


def place_hot():
    spot = np.arange(WIN)
    hot = np.zeros((WIN, NOFF), np.float32)
    for (start, _, _), where in zip(SPANS, (spot // (WH * WW), (spot // WW) % WH, spot % WW)):
        hot[spot, start + where] = 1.0
    return hot


def query_side():
    half = np.zeros((WIN, 64), np.float32)
    half[:, :NOFF] = place_hot()
    half[:, NOFF : 2 * NOFF] = place_hot()
    half[:, 2 * NOFF] = 1.0
    return np.concatenate([half, half], axis=1)


def offset_hot(rows, copies):
    hot = np.zeros((2 * NOFF - 3, rows, 64), np.float32)
    for start, begin, length in SPANS:
        for key in range(length):
            for query in range(length):
                for copy in range(copies):
                    hot[begin + query - key + length - 1, start + key, copy * NOFF + start + query] = 1.0
    return hot


def key_tables(rel, core):
    value = jnp.einsum("hr,rkq->hkq", rel.reshape(16, -1), offset_hot(64, 2), precision=precise)
    top = lax.reduce_precision(value, 8, 7)
    value = jnp.where(jnp.arange(64) < NOFF, top, value - top).astype(bf16)
    value = value.reshape(4, 2, 2, 64, 64)
    value = jnp.where(core == 0, value, value[:, ::-1])
    value = jnp.concatenate([value[:, :, 1], value[:, :, 0]], axis=-1)
    return jnp.pad(value, ((0, 0), (0, 0), (0, 64), (0, 0)))


def rel_sums(grids, core):
    grids = jnp.where(core == 0, grids, grids[:, ::-1])
    grids = grids.reshape(4, 2, 32, 2, 64)
    grids = jnp.stack([grids[:, :, :, 1], grids[:, :, :, 0]], axis=2).reshape(16, 32, 64)
    return jnp.einsum("hkq,rkq->hr", grids, offset_hot(32, 1), precision=precise).reshape(4, 4, -1)


def local_windows(
    sizes,
    tokens,
    cotangent,
    qkv_weight,
    out_weight,
    up_weight,
    down_weight,
    ada_weight,
    ada_bias,
    rel_bias,
    class_table,
    lengths,
    timesteps,
    classes,
):
    n_z, n_mp = sizes
    n_dp = 2 * n_z
    micro = tokens.shape[0]
    mp = lax.axis_index("mp")
    z = lax.axis_index("z")
    core = lax.axis_index("core")

    def swap_mp(bit):
        return lambda v: lax.ppermute(v, "mp", [(i, i ^ bit) for i in range(n_mp)])

    def swap_dp(bit):
        return lambda v: lax.ppermute(v, ("z", "core"), [(i, i ^ bit) for i in range(n_dp)])

    px, py, pd = swap_mp(1), swap_mp(2), swap_mp(3)
    pc = swap_dp(1)
    by_rel = [lambda v: v, px, py, pd]

    def cat(a, b, axis=0):
        return jnp.concatenate([a, b], axis=axis)

    pre_cond = condition(timesteps, classes, class_table)
    cond_low = silu_plain(pre_cond).astype(bf16)
    mode_cols = jnp.einsum("mwd,de->mwe", cond_low, ada_weight, preferred_element_type=f32) + ada_bias.astype(f32)
    order = jnp.arange(4) ^ mp
    rel_row = jnp.pad(rel_bias, ((0, 0), (0, 128 - rel_bias.shape[1])))
    messages = [
        by_rel[r](cat(lax.dynamic_index_in_dim(mode_cols, mp ^ r, axis=1, keepdims=False), rel_row, 1))
        for r in range(4)
    ]
    messages = jnp.stack(messages)
    columns = mode_cols.shape[-1]
    modes = jnp.take(messages[:, :, :columns], order, axis=0)
    modes = modes.transpose(1, 0, 2).reshape(micro, 6, D)
    tables = key_tables(messages[:, :, columns : columns + rel_bias.shape[1]], core)
    own_lengths = lax.dynamic_index_in_dim(lengths, mp, axis=1, keepdims=False)

    core_row = core.reshape(1)
    query_hot = jnp.asarray(query_side(), bf16)
    packed, heads, probs = [None] * 4, [None] * 4, [None] * 4

    attn_own = list(attn_rows(core_row, qkv_weight, out_weight, [mode_cols]))
    (attn_own[0],) = hold(attn_own[:1], [messages])
    ax, ay = px(attn_own[0]), py(attn_own[0])
    normed_one, packed[0], heads[0], probs[0] = attend(own_lengths, tokens, modes, attn_own, tables[0], query_hot)
    up0, down0, up1, down1 = feed_rows(core_row, up_weight, down_weight, [heads[0]])
    ax, ay = hold([ax, ay], [down1])
    adx, ady = py(ax[: HALF // 2]), px(ay[HALF // 2 :])
    attn_w = [attn_own] + [[Moved(v), Moved(pc(v))] for v in (ax, ay)]
    packed[1], heads[1], probs[1] = attend(
        own_lengths, normed_one, modes, attn_w[1], tables[1], query_hot, [down1]
    )
    adx, ady = hold([adx, ady], [heads[1]])
    ad = cat(adx, ady)
    up0, down0 = hold([up0, down0], [ad])
    x_up, y_down = px(up0), py(down0)
    attn_w.append([ad, Moved(pc(ad))])
    packed[2], heads[2], probs[2] = attend(
        own_lengths, normed_one, modes, attn_w[2], tables[2], query_hot, [heads[1]]
    )
    packed[3], heads[3], probs[3] = attend(
        own_lengths, normed_one, modes, attn_w[3], tables[3], query_hot, [heads[2]]
    )
    x_up, y_down = hold([x_up, y_down], [heads[3]])
    d_up, d_down = py(x_up), px(y_down)
    attn_w = [[v.array if isinstance(v, Moved) else v for v in halves] for halves in attn_w]
    attn_out, middle, normed_two, down_in = middle_step(heads, attn_w, tokens, cotangent, modes)

    hid, pre, mine, other = [None] * 4, [None] * 4, [None] * 4, [None] * 4

    def feed_step(r, weight, after):
        hid[r], pre[r], mine[r], sent = feed(normed_two, down_in, weight, after)
        other[r] = pc(sent)

    def pair(r, which):
        return [(mine[r], which, 0), (Moved(other[r]), which, 0)]

    def weight_of(up, down):
        return [((Moved(u), 0), (Moved(v), 0)) for u, v in ((up, down), (pc(up), pc(down)))]

    feed_w = [[((up0, 0), (down0, 0)), ((up1, 0), (down1, 0))], None, None, None]
    feed_step(0, feed_w[0], [])
    d_up, d_down = hold([d_up, d_down], [hid[0]])
    feed_w[3] = weight_of(d_up, d_down)
    feed_step(3, feed_w[3], [hid[0]])
    x_down, y_up = arrive([px(down0), py(up0)], [hid[3]])
    feed_w[1], feed_w[2] = weight_of(x_up, x_down), weight_of(y_up, y_down)
    diag_x, diag_y = merge(pair(3, 0), pair(3, 1), after=[hid[3]])
    feed_step(1, feed_w[1], [hid[3], diag_x])
    feed_step(2, feed_w[2], [hid[1]])
    diag_x, diag_y = arrive([px(diag_x), py(diag_y)], [hid[2]])
    both = 2 * HALF
    flat = [v.reshape(both, D) for v in mine]
    flat_other = [v.reshape(both, D) for v in other]
    (last_x,) = merge(
        [(flat[1], None, 0), (Moved(flat_other[1]), None, 0), (Moved(diag_y), None, -HALF, HALF, both)], rows=both
    )
    (last_y,) = merge(
        [(flat[2], None, 0), (Moved(flat_other[2]), None, 0), (Moved(diag_x), None, 0, 0, HALF)], rows=both, after=[last_x]
    )
    middle_grad, out_in, turn_sums = turn_step(
        pre, feed_w, middle, attn_out, cotangent, modes, [last_x, last_y]
    )
    still = [[[(v.array if isinstance(v, Moved) else v, at) for v, at in half] for half in halves] for halves in feed_w]
    output, out_sums = out_step(hid, still, middle, cotangent, modes, [turn_sums])
    last_x, last_y = arrive([px(last_x), py(last_y)], [out_sums])
    z_row = z.reshape(1)
    terms = [mine[0], Moved(other[0]), *[Moved(v.reshape(2, HALF, D)) for v in (last_x, last_y)]]
    feed_keep, feed_sent = merge_parts(terms, z_row, n_z, 2)
    z_one, z_two = swap_dp(2), swap_dp(4)

    own_pre = jnp.take(pre_cond.transpose(1, 0, 2), order, axis=0).reshape(4 * micro, D)
    share = 1.0 / (1.0 + jnp.exp(-own_pre))
    class_col = jnp.pad(classes.T.reshape(-1, 1).astype(bf16), ((0, 0), (0, 127)))
    cond_rel = jnp.take(cond_low, order, axis=1).transpose(1, 0, 2).reshape(4 * micro, D)
    slope, cond_rel = hold([share * (1.0 + own_pre * (1.0 - share)), cat(cond_rel, class_col, 1)])

    packed_grad, rel_grid, a_mine, a_other = [None] * 4, [None] * 4, [None] * 4, [None] * 4

    def back_step(r, after):
        packed_grad[r], a_mine[r], sent, rel_grid[r] = attend_back(
            out_in, attn_w[r], packed[r], probs[r], query_hot, normed_one, heads[r], after
        )
        a_other[r] = pc(sent)

    cut = HALF // 2

    def a_pair(r, start):
        return [(a_mine[r], None, start), (Moved(a_other[r]), None, start)]

    back_step(3, [feed_keep])
    (feed_got,) = arrive([z_one(feed_sent)], [packed_grad[3]])
    (feed_sent,) = merge([(feed_keep, None, cut), (Moved(feed_got), None, cut)], rows=cut)
    back_step(1, [packed_grad[3], feed_sent])
    (feed_two,) = arrive([z_two(feed_sent)], [packed_grad[1]])
    (feed_one,) = merge([(feed_keep, None, 0), (Moved(feed_got), None, 0), (Moved(feed_two), None, 0)], rows=cut)
    a_diag_x, a_diag_y = merge(a_pair(3, 0), a_pair(3, cut), rows=cut, after=[feed_one])
    back_step(2, [a_diag_x, a_diag_y, slope, cond_rel])
    feed_two, a_diag_x, a_diag_y = arrive([z_two(feed_one), px(a_diag_x), py(a_diag_y)], [packed_grad[2]])
    feed_even = cat(feed_one, feed_two)
    (a_last_x,) = merge(a_pair(1, 0) + [(Moved(a_diag_y), None, -cut, cut, HALF)])
    (a_last_y,) = merge(a_pair(2, 0) + [(Moved(a_diag_x), None, 0, 0, cut)], after=[a_last_x])
    back_step(0, [packed_grad[2], a_last_y, feed_even])
    feed_odd, a_last_x, a_last_y = arrive([z_one(feed_even), px(a_last_x), py(a_last_y)], [packed_grad[0]])

    def exchange(parts):
        return [swap_dp(2 * k)(v) for k, v in enumerate(parts) if k]

    attn_parts = merge_parts([a_mine[0], *map(Moved, (a_other[0], a_last_x, a_last_y))], z_row, n_z, n_z)
    token_grads, last_sums = last_step(packed_grad, attn_w, tokens, modes, middle_grad, attn_parts)
    attn_got = exchange(attn_parts)
    feed_other = [pc(feed_even), pc(feed_odd)]
    *attn_got, feed_other[0], feed_other[1] = arrive(attn_got + feed_other, [last_sums])
    (attn_own,) = merge([(v, None, 0) for v in (attn_parts[0], *attn_got)], rows=HALF // n_z)

    place = jnp.stack([core, z])
    mode_grad = jnp.concatenate([last_sums, turn_sums, out_sums], axis=1).reshape(micro, 4, -1).transpose(1, 0, 2)
    messages = [lax.dynamic_index_in_dim(mode_grad, mp ^ r, axis=0, keepdims=False) for r in range(4)]
    rel_grid = hold(rel_grid, [attn_own])
    rel_part = jnp.pad(rel_sums(jnp.stack(rel_grid), core), ((0, 0), (0, 4 * (micro - 1)), (0, 128 - rel_bias.shape[1])))
    grad_up, grad_down = feed_final(place, feed_even, Moved(feed_odd), *map(Moved, feed_other))
    *messages[1:], attn_far = arrive(
        [by_rel[r](messages[r]) for r in (1, 2, 3)] + [swap_dp(6)(attn_own)], [attn_own, grad_up]
    )
    mode_low, *shares = mode_shares(messages, rel_part, ada_weight)
    *shares[1:], attn_two, attn_one = arrive(
        [by_rel[r](shares[r]) for r in (1, 2, 3)] + [swap_dp(4)(attn_own), swap_dp(2)(attn_own)], [attn_far]
    )
    grads = mode_rows(mp.reshape(1), mode_low, shares, slope, cond_rel)
    attn_own = jnp.concatenate([attn_own, attn_one, attn_two, attn_far])
    got = exchange([grads] * n_z)
    (attn_other,) = hold([pc(attn_own)], [grads])
    grad_qkv, grad_out = attn_final(place, attn_own, Moved(attn_other))
    got = arrive(got, [grad_qkv])
    grads = jnp.concatenate([grads, *got])
    grad_ada, grad_ada_bias, class_grad, grad_rel = mode_final(
        (2 * z + core).reshape(1), grads, pc(grads), n_z, columns, class_table.shape[0], rel_bias.shape
    )

    return (
        output,
        token_grads,
        grad_qkv,
        grad_out,
        grad_up,
        grad_down,
        grad_ada,
        grad_ada_bias,
        grad_rel,
        class_grad,
    )


def layer_norm(values):
    center = values - jnp.mean(values, axis=-1, keepdims=True)
    spread = jnp.mean(center * center, axis=-1, keepdims=True)
    return center * lax.rsqrt(spread + EPS)


def modulate(values, shift, scale):
    return layer_norm(values) * (1.0 + scale) + shift


def gelu_tanh(values):
    return (
        0.5
        * values
        * (
            1.0
            + jnp.tanh(math.sqrt(2.0 / math.pi) * (values + 0.044715 * values * values * values))
        )
    )


def condition_whole(timesteps, classes, class_table):
    half_width = class_table.shape[1] // 2
    frequency = jnp.exp(
        -math.log(10000.0) * jnp.arange(half_width).astype(class_table.dtype) / half_width
    )
    phase_angle = timesteps.astype(class_table.dtype)[..., None] * frequency
    sinusoid = jnp.concatenate([jnp.cos(phase_angle), jnp.sin(phase_angle)], axis=-1)
    onehot = (classes[..., None] == jnp.arange(class_table.shape[0])[None, None, :]).astype(
        class_table.dtype
    )
    lookup = jnp.einsum("mwc,cd->mwd", onehot, class_table, precision=precise)
    return silu_plain(sinusoid + lookup)


def axis_table(rel_part, window_span):
    places = jnp.arange(window_span)
    offsets = places[:, None] - places[None, :] + window_span - 1
    onehot = (offsets[:, :, None] == jnp.arange(2 * window_span - 1)[None, None, :]).astype(
        rel_part.dtype
    )
    return jnp.einsum("hr,abr->hab", rel_part, onehot, precision=precise)


def window_bias(rel_bias):
    frame_part = axis_table(rel_bias[:, : 2 * WT - 1], WT)
    row_part = axis_table(rel_bias[:, 2 * WT - 1 : 2 * WT + 2 * WH - 2], WH)
    column_part = axis_table(rel_bias[:, 2 * WT + 2 * WH - 2 :], WW)
    full_bias = (
        frame_part[:, :, None, None, :, None, None]
        + row_part[:, None, :, None, None, :, None]
        + column_part[:, None, None, :, None, None, :]
    )
    return full_bias.reshape(rel_bias.shape[0], WIN, WIN)


def attention_scores(query_part, key_part, bias_full, masks):
    scores = (
        jnp.einsum("wqhd,wkhd->whqk", query_part, key_part, preferred_element_type=jnp.float32)
        * HD ** (-0.5)
        + bias_full[None]
    )
    return jnp.where(masks[:, None, None, :], scores, -1e30)


def local_general(
    tokens,
    cotangent,
    qkv_weight,
    out_weight,
    up_weight,
    down_weight,
    ada_weight,
    ada_bias,
    rel_bias,
    class_table,
    lengths,
    timesteps,
    classes,
):
    micro_count = tokens.shape[0]
    row_count = tokens.shape[1]
    win_count = lengths.shape[1]
    heads_here = rel_bias.shape[0]
    head_scale = HD ** (-0.5)
    first_row = lax.axis_index("mp") * row_count
    row_window = (first_row + jnp.arange(row_count)) // WIN
    spread_rows = (row_window[:, None] == jnp.arange(win_count)[None, :]).astype(jnp.float32)
    cond_low = condition_whole(timesteps, classes, class_table).astype(jnp.bfloat16)
    mode_cols = jnp.einsum(
        "mwd,de->mwe", cond_low, ada_weight, preferred_element_type=jnp.float32
    ) + ada_bias.astype(jnp.float32)
    mode_all = lax.all_gather(mode_cols, "mp", axis=2, tiled=True)
    bias_full, bias_pull = jax.vjp(window_bias, rel_bias)
    frame_of = jnp.arange(WIN) // (WH * WW)
    grad_qkv = jnp.zeros(qkv_weight.shape, jnp.float32)
    grad_out = jnp.zeros(out_weight.shape, jnp.float32)
    grad_up = jnp.zeros(up_weight.shape, jnp.float32)
    grad_down = jnp.zeros(down_weight.shape, jnp.float32)
    grad_rel = jnp.zeros(rel_bias.shape, jnp.float32)
    mode_parts = []
    outputs = []
    token_grads = []
    for micro_step in range(micro_count):
        mode_rows = jnp.dot(spread_rows, mode_all[micro_step], precision=precise)
        shift_attn, scale_attn, gate_attn, shift_mlp, scale_mlp, gate_mlp = jnp.split(
            mode_rows, 6, axis=1
        )
        inputs = tokens[micro_step].astype(jnp.float32)
        normed_one, pull_one = jax.vjp(modulate, inputs, shift_attn, scale_attn)
        gathered_one = lax.all_gather(normed_one.astype(jnp.bfloat16), "mp", axis=0, tiled=True)
        packed = jnp.dot(gathered_one, qkv_weight, preferred_element_type=jnp.float32).astype(
            jnp.bfloat16
        )
        packed = packed.reshape(win_count, WIN, heads_here, 3, HD)
        query_part = packed[:, :, :, 0]
        key_part = packed[:, :, :, 1]
        value_part = packed[:, :, :, 2]
        masks = frame_of[None, :] < lengths[micro_step][:, None]
        scores = attention_scores(query_part, key_part, bias_full, masks)
        top_score = jnp.max(scores, axis=-1, keepdims=True)
        expo = jnp.exp(scores - top_score)
        total = jnp.sum(expo, axis=-1, keepdims=True)
        log_total = top_score + jnp.log(total)
        probs_low = (expo / total).astype(jnp.bfloat16)
        heads_out = jnp.einsum(
            "whqk,wkhd->wqhd", probs_low, value_part, preferred_element_type=jnp.float32
        ).astype(jnp.bfloat16)
        heads_out = heads_out.reshape(win_count * WIN, heads_here * HD)
        attn_out = lax.psum_scatter(
            jnp.dot(heads_out, out_weight, preferred_element_type=jnp.float32),
            "mp",
            scatter_dimension=0,
            tiled=True,
        )
        middle = inputs + gate_attn * attn_out
        normed_two, pull_two = jax.vjp(modulate, middle, shift_mlp, scale_mlp)
        grad_y = cotangent[micro_step].astype(jnp.float32)
        down_in = (gate_mlp * grad_y).astype(jnp.bfloat16)
        gathered_two = lax.all_gather(normed_two.astype(jnp.bfloat16), "mp", axis=0, tiled=True)
        hidden_pre = jnp.dot(gathered_two, up_weight, preferred_element_type=jnp.float32)
        hidden_low, gelu_pull = jax.vjp(gelu_tanh, hidden_pre)
        hidden_low = hidden_low.astype(jnp.bfloat16)
        mlp_out = lax.psum_scatter(
            jnp.dot(hidden_low, down_weight, preferred_element_type=jnp.float32),
            "mp",
            scatter_dimension=0,
            tiled=True,
        )
        down_all = lax.all_gather(down_in, "mp", axis=0, tiled=True)
        hidden_grad = jnp.einsum(
            "rd,fd->rf", down_all, down_weight, preferred_element_type=jnp.float32
        )
        micro_down = jnp.einsum(
            "rf,rd->fd", hidden_low, down_all, preferred_element_type=jnp.float32
        )
        pre_low = gelu_pull(hidden_grad)[0].astype(jnp.bfloat16)
        micro_up = jnp.einsum(
            "rd,rf->df", gathered_two, pre_low, preferred_element_type=jnp.float32
        )
        normed_two_grad = lax.psum_scatter(
            jnp.einsum("rf,df->rd", pre_low, up_weight, preferred_element_type=jnp.float32),
            "mp",
            scatter_dimension=0,
            tiled=True,
        )
        outputs.append(middle + gate_mlp * mlp_out)
        grad_gate_mlp = grad_y * mlp_out
        resid_grad, grad_shift_mlp, grad_scale_mlp = pull_two(normed_two_grad)
        middle_grad = grad_y + resid_grad
        grad_gate_attn = middle_grad * attn_out
        out_in = (gate_attn * middle_grad).astype(jnp.bfloat16)
        out_all = lax.all_gather(out_in, "mp", axis=0, tiled=True)
        micro_out = jnp.einsum("rc,rd->cd", heads_out, out_all, preferred_element_type=jnp.float32)
        heads_grad = jnp.einsum(
            "rd,cd->rc", out_all, out_weight, preferred_element_type=jnp.float32
        ).astype(jnp.bfloat16)
        heads_grad = heads_grad.reshape(win_count, WIN, heads_here, HD)
        probs = jnp.exp(attention_scores(query_part, key_part, bias_full, masks) - log_total)
        probs_low = probs.astype(jnp.bfloat16)
        value_grad = jnp.einsum(
            "whqk,wqhd->wkhd", probs_low, heads_grad, preferred_element_type=jnp.float32
        )
        probs_grad = jnp.einsum(
            "wqhd,wkhd->whqk", heads_grad, value_part, preferred_element_type=jnp.float32
        )
        score_grad = probs * (probs_grad - jnp.sum(probs * probs_grad, axis=-1, keepdims=True))
        micro_rel = bias_pull(jnp.sum(score_grad, axis=0))[0]
        score_low = (score_grad * head_scale).astype(jnp.bfloat16)
        query_grad = jnp.einsum(
            "whqk,wkhd->wqhd", score_low, key_part, preferred_element_type=jnp.float32
        )
        key_grad = jnp.einsum(
            "whqk,wqhd->wkhd", score_low, query_part, preferred_element_type=jnp.float32
        )
        packed_grad = jnp.stack([query_grad, key_grad, value_grad], axis=3).astype(jnp.bfloat16)
        packed_grad = packed_grad.reshape(win_count * WIN, heads_here * 3 * HD)
        micro_qkv = jnp.einsum(
            "rd,rc->dc", gathered_one, packed_grad, preferred_element_type=jnp.float32
        )
        normed_one_grad = lax.psum_scatter(
            jnp.einsum("rc,dc->rd", packed_grad, qkv_weight, preferred_element_type=jnp.float32),
            "mp",
            scatter_dimension=0,
            tiled=True,
        )
        input_grad, grad_shift_attn, grad_scale_attn = pull_one(normed_one_grad)
        token_grads.append(middle_grad + input_grad)
        row_modes = jnp.concatenate(
            [
                grad_shift_attn,
                grad_scale_attn,
                grad_gate_attn,
                grad_shift_mlp,
                grad_scale_mlp,
                grad_gate_mlp,
            ],
            axis=1,
        )
        mode_parts.append(jnp.einsum("rw,re->we", spread_rows, row_modes, precision=precise))
        local_grads = (micro_qkv, micro_out, micro_rel, micro_up, micro_down)
        grad_qkv = grad_qkv + local_grads[0]
        grad_out = grad_out + local_grads[1]
        grad_rel = grad_rel + local_grads[2]
        grad_up = grad_up + local_grads[3]
        grad_down = grad_down + local_grads[4]
    mode_grad_cols = lax.psum_scatter(jnp.stack(mode_parts), "mp", scatter_dimension=2, tiled=True)
    mode_low = mode_grad_cols.astype(jnp.bfloat16)
    grad_ada = jnp.einsum("mwd,mwe->de", cond_low, mode_low, preferred_element_type=jnp.float32)
    grad_ada_bias = jnp.sum(mode_grad_cols, axis=(0, 1))
    cond_grad = jnp.einsum("mwe,de->mwd", mode_low, ada_weight, preferred_element_type=jnp.float32)
    cond_value, cond_pull = jax.vjp(partial(condition_whole, timesteps, classes), class_table)
    class_total = lax.psum(cond_pull(cond_grad)[0], ("dp", "mp"))
    grad_qkv, grad_out, grad_up, grad_down, grad_rel, grad_ada, grad_ada_bias = lax.psum(
        (grad_qkv, grad_out, grad_up, grad_down, grad_rel, grad_ada, grad_ada_bias), "dp"
    )
    return (
        jnp.stack(outputs).astype(jnp.bfloat16),
        jnp.stack(token_grads).astype(jnp.bfloat16),
        grad_qkv,
        grad_out,
        grad_up,
        grad_down,
        grad_ada,
        grad_ada_bias,
        grad_rel,
        class_total,
    )


def solution(mesh):
    n_dp, n_mp = mesh.shape["dp"], mesh.shape["mp"]

    def specs(*dp):
        rows = P(None, (*dp, "mp"), None)
        weights = (P(None, "mp"), P("mp", None), P(None, "mp"), P("mp", None), P(None, "mp"), P("mp"), P("mp", None), P())
        return (rows, rows, *weights, *[P(None, dp)] * 3), (rows, rows, *weights)

    def program(tokens, *arrays):
        if n_mp == 4 and n_dp % 2 == 0 and tokens.shape[1] == n_dp * n_mp * WIN:
            devices = mesh.devices.reshape(n_dp // 2, 2, n_mp)
            split = jax.sharding.Mesh(devices, ("z", "core", "mp"))
            ins, outs = specs("z", "core")
            step = jax.shard_map(
                partial(local_windows, (n_dp // 2, n_mp)), mesh=split, in_specs=ins, out_specs=outs, check_vma=False
            )
        else:
            ins, outs = specs("dp")
            step = jax.shard_map(local_general, mesh=mesh, in_specs=ins, out_specs=outs, check_vma=False)
        return step(tokens, *arrays)

    return program
```

```python
from functools import partial
import math
from typing import NamedTuple

import jax
import jax.numpy as jnp
import numpy as np
from jax import lax
from jax.experimental import pallas as pl
from jax.experimental.pallas import tpu as pltpu
from jax.sharding import PartitionSpec as P

HD = 64
WT = 5
WH = 8
WW = 8
WIN = 320
D = 1024
EPS = 1e-06
NOFF = WT + WH + WW
C0 = math.sqrt(2.0 / math.pi)
C1 = 0.044715
precise = lax.Precision.HIGHEST
f32 = jnp.float32
bf16 = jnp.bfloat16
NN = (((1,), (0,)), ((), ()))
NT = (((1,), (1,)), ((), ()))
TN = (((0,), (0,)), ((), ()))
HALF = 512
QKV = 384


def mm(a, b, dims=NN):
    return lax.dot_general(a, b, dims, preferred_element_type=f32)


def whole(*dims):
    return pl.BlockSpec(dims, lambda i, *_: (0,) * len(dims))


def part(index, *dims):
    return pl.BlockSpec(dims, lambda i, *_: index)


def rows_of(width):
    return pl.BlockSpec((WIN, width), lambda i, *_: (i, 0))


def window_of(*dims):
    return pl.BlockSpec((None,) + dims, lambda i, *_: (i,) + (0,) * len(dims))


def shape(dims, dtype):
    return pltpu.HBM(dims, dtype)


def near(dims, dtype):
    return jax.ShapeDtypeStruct(dims, dtype)


HBM = pl.BlockSpec(memory_space=pltpu.HBM)
VMEM = pl.BlockSpec(memory_space=pltpu.VMEM)


class Loads:
    def __init__(self, sems):
        self.sems, self.copies = sems, []

    def add(self, source, target):
        self.copies.append(pltpu.make_async_copy(source, target, self.sems.at[len(self.copies)]))
        return self.copies[-1]

    def start(self):
        for copy in self.copies:
            copy.start()

    def wait(self):
        for copy in self.copies:
            copy.wait()


class Moved(NamedTuple):
    array: jax.Array


def in_hbm(array):
    return pltpu.with_memory_space_constraint(array, pltpu.HBM)


def operand(array, spec):
    if isinstance(array, Moved):
        return array.array, pl.BlockSpec(memory_space=pl.ANY) if spec is HBM else spec
    return array if spec is VMEM else in_hbm(array), spec


def run(kernel, name, grid, ins, outs, scratch=(), after=(), scalars=(), flops=0, moved=0, vmem=24):
    first = len(scalars) + len(ins)

    ins = [operand(array, spec) for array, spec in ins]

    def body(*refs):
        kernel(*refs[:first], *refs[first + len(after) :])

    return pl.pallas_call(
        body,
        grid_spec=pltpu.PrefetchScalarGridSpec(
            num_scalar_prefetch=len(scalars),
            grid=(grid,),
            in_specs=[spec for _, spec in ins] + [HBM] * len(after),
            out_specs=[spec for _, spec in outs],
            scratch_shapes=list(scratch),
        ),
        out_shape=[what for what, _ in outs],
        compiler_params=pltpu.CompilerParams(vmem_limit_bytes=vmem * 2**20),
        cost_estimate=pl.CostEstimate(flops=1000, bytes_accessed=1000, transcendentals=0),
        name=name,
    )(*scalars, *[array for array, _ in ins], *map(in_hbm, after))


def hold(values, after=(), flops=1000):
    anywhere = pl.BlockSpec(memory_space=pl.ANY)
    return pl.pallas_call(
        lambda *refs: None,
        in_specs=[anywhere] * len(values) + [HBM] * len(after),
        out_specs=[anywhere] * len(values),
        out_shape=[near(v.shape, v.dtype) for v in values],
        input_output_aliases={i: i for i in range(len(values))},
        cost_estimate=pl.CostEstimate(flops=flops, bytes_accessed=1000, transcendentals=0),
        name="hold",
    )(*values, *map(in_hbm, after))


def arrive(values, after):
    return hold(values, after, 30 * 10**9)


def ln_parts(values):
    center = values - jnp.mean(values, axis=-1, keepdims=True)
    rstd = lax.rsqrt(jnp.mean(center * center, axis=-1, keepdims=True) + EPS)
    return center * rstd, rstd


def ln_back(grad, scale, hat, rstd):
    inner = grad * (1.0 + scale)
    mean_one = jnp.mean(inner, axis=-1, keepdims=True)
    mean_two = jnp.mean(inner * hat, axis=-1, keepdims=True)
    return rstd * (inner - mean_one - hat * mean_two)


def hot_rows(count, source):
    row = lax.broadcasted_iota(jnp.int32, (count, count), 0)
    col = lax.broadcasted_iota(jnp.int32, (count, count), 1)
    return col == source(row), row


def qkv_source(core):
    def source(row):
        half = jnp.where(row >= QKV, 1, 0)
        inner = row - half * QKV
        head = 2 * (half ^ core) + ((inner & 127) >> 6)
        return head * 3 * HD + (inner >> 7) * HD + (inner & 63)

    return source


def attn_rows_kernel(core_ref, qkv_ref, out_ref, own0, own1):
    core = core_ref[0]
    hot, row = hot_rows(2 * QKV, qkv_source(core))
    inner = jnp.where(row >= QKV, row - QKV, row)
    hot = jnp.where(hot, jnp.where(inner < 128, HD**-0.5, 1.0), 0.0).astype(bf16)
    rows = mm(hot, qkv_ref[...], NT).astype(bf16)
    for h, own in enumerate((own0, own1)):
        own[:QKV] = rows[h * QKV : (h + 1) * QKV]
        own[QKV:] = out_ref[pl.ds(pl.multiple_of((core ^ h) * 128, 128), 128)]


def feed_rows_kernel(core_ref, up_ref, down_ref, up0, down0, up1, down1):
    core = core_ref[0]
    hot, _ = hot_rows(2 * HALF, lambda row: row ^ (core * HALF))
    rows = mm(jnp.where(hot, 1.0, 0.0).astype(bf16), up_ref[...], NT).astype(bf16)
    for h, (up, down) in enumerate(((up0, down0), (up1, down1))):
        up[0] = rows[h * HALF : (h + 1) * HALF]
        down[0] = down_ref[pl.ds(pl.multiple_of((core ^ h) * HALF, HALF), HALF)]


def attn_rows(core, qkv, out, after):
    half = (shape((HALF, D), bf16), whole(HALF, D))
    ins = [(qkv, whole(D, 2 * QKV)), (out, whole(256, D))]
    return run(attn_rows_kernel, "attn_rows", 1, ins, [half, half], (), after, [core], 1e9, 4e6)


def feed_rows(core, up, down, after):
    half = (shape((1, HALF, D), bf16), whole(1, HALF, D))
    ins = [(up, whole(D, 2 * HALF)), (down, whole(2 * HALF, D))]
    return run(feed_rows_kernel, "feed_rows", 1, ins, [half] * 4, (), after, [core], 2e9, 8e6)


def attend_kernel(len_ref, x_ref, mode_ref, wa_ref, wb_ref, tbl_ref, e_ref, *rest):
    n1_ref, packed_ref, heads_ref, probs_ref, w_all, kb_all, sems = rest if len(rest) == 7 else (None, *rest)
    w = pl.program_id(0)

    @pl.when(w == 0)
    def _():
        loads = Loads(sems)
        loads.add(wa_ref.at[:QKV], w_all.at[:QKV])
        loads.add(wb_ref.at[:QKV], w_all.at[QKV:])
        loads.start()
        for p in range(2):
            kb_all[p] = mm(e_ref[...], tbl_ref[p]).astype(bf16)
        loads.wait()

    if n1_ref is None:
        x = x_ref[...]
    else:
        hat, _ = ln_parts(x_ref[...].astype(f32))
        x = (hat * (1.0 + mode_ref[1:2]) + mode_ref[0:1]).astype(bf16)
        n1_ref[...] = x
    pk = mm(x, w_all[...], NT).astype(bf16)
    packed_ref[...] = pk
    lane = lax.broadcasted_iota(jnp.int32, (WIN, 128), 1)
    low = lane < 64
    frame = lax.broadcasted_iota(jnp.int32, (WIN, 128), 0) // (WH * WW)
    mask_lane = (lane & 63) == 2 * NOFF
    hide = jnp.where(frame < len_ref[w], 0.0, -1e30).astype(bf16)
    for p in range(2):
        q = pk[:, p * QKV : p * QKV + 128]
        k = pk[:, p * QKV + 128 : p * QKV + 256]
        v = pk[:, p * QKV + 256 : p * QKV + 384]
        kb = jnp.where(mask_lane, hide, kb_all[p])
        v_rows = v.T
        outs = []
        for i in range(2):
            mine = low if i == 0 else ~low
            s = mm(jnp.where(mine, k, kb), jnp.where(mine, q, e_ref[...]), NT)
            ex = jnp.exp(s - jnp.max(s, axis=0, keepdims=True))
            pr = (ex * (1.0 / jnp.sum(ex, axis=0, keepdims=True))).astype(bf16)
            probs_ref[2 * p + i] = pr
            outs.append(mm(v_rows[i * HD : (i + 1) * HD], pr))
        heads_ref[:, p * 128 : (p + 1) * 128] = jnp.concatenate(outs, axis=0).T.astype(bf16)


def attend(lengths, source, modes, weight, table, query_hot, after=()):
    count = lengths.shape[0]
    rows = count * WIN
    first = source.ndim == 3
    outs = [
        (shape((rows, 2 * QKV), bf16), rows_of(2 * QKV)),
        (shape((rows, 256), bf16), rows_of(256)),
        (shape((count * 4, WIN, WIN), bf16), pl.BlockSpec((4, WIN, WIN), lambda i, l: (i, 0, 0))),
    ]
    if first:
        outs = [(near((rows, D), bf16), rows_of(D))] + outs
    return run(
        attend_kernel,
        "attend",
        count,
        [
            (source, window_of(WIN, D) if first else rows_of(D)),
            (modes, window_of(6, D)),
            (weight[0], HBM),
            (weight[1], HBM),
            (table, whole(2, 128, 128)),
            (query_hot, whole(WIN, 128)),
        ],
        outs,
        [pltpu.VMEM((2 * QKV, D), bf16), pltpu.VMEM((2, WIN, 128), bf16), pltpu.SemaphoreType.DMA((2,))],
        after,
        [lengths],
        9e9,
        12e6,
    )


def middle_kernel(h0, h1, h2, h3, w0, w1, w2, w3, w4, w5, w6, w7, tok, cot, mode, attn_ref, mid_ref, n2_ref, di_ref, w_all, sems):
    @pl.when(pl.program_id(0) == 0)
    def _():
        loads = Loads(sems)
        for i, ref in enumerate((w0, w1, w2, w3, w4, w5, w6, w7)):
            loads.add(ref.at[QKV:], w_all.at[pl.ds(i * 128, 128)])
        loads.start()
        loads.wait()

    heads = jnp.concatenate([h0[...], h1[...], h2[...], h3[...]], axis=1)
    attn = mm(heads, w_all[...])
    attn_ref[...] = attn.astype(bf16)
    middle = tok[...].astype(f32) + mode[2:3] * attn
    mid_ref[...] = middle
    hat, _ = ln_parts(middle)
    n2_ref[...] = (hat * (1.0 + mode[4:5]) + mode[3:4]).astype(bf16)
    di_ref[...] = (mode[5:6] * cot[...].astype(f32)).astype(bf16)


def middle_step(heads, weights, tokens, cotangent, modes, after=()):
    count = tokens.shape[0]
    rows = count * WIN
    return run(
        middle_kernel,
        "middle",
        count,
        [(h, rows_of(256)) for h in heads]
        + [(half, HBM) for pair in weights for half in pair]
        + [(tokens, window_of(WIN, D)), (cotangent, window_of(WIN, D)), (modes, window_of(6, D))],
        [(shape((rows, D), kind), rows_of(D)) for kind in (bf16, f32)] + [(near((rows, D), bf16), rows_of(D))] * 2,
        [pltpu.VMEM((D, D), bf16), pltpu.SemaphoreType.DMA((8,))],
        after,
        flops=2.7e9,
        moved=22e6,
    )


CHUNK = 256


def feed_kernel(places, n2, di, up0, dn0, up1, dn1, hid_hbm, pre_hbm, g0_hbm, g1_hbm, weight, hid, pre, grad, in_sems, out_sems):
    loads, stores = Loads(in_sems), Loads(out_sems)
    for i, ref in enumerate((up0, dn0, up1, dn1)):
        loads.add(ref.at[places[i]], weight.at[i // 2, i % 2])
    for i in (2, 3, 0, 1):
        loads.copies[i].start()

    def store(from_ref, to_ref):
        stores.add(from_ref, to_ref).start()

    for h, g_hbm in ((1, g1_hbm), (0, g0_hbm)):
        units = pl.ds(h * HALF, HALF)
        loads.copies[2 * h].wait()
        loads.copies[2 * h + 1].wait()
        for i in range(n2.shape[0] // CHUNK):
            rows = pl.ds(i * CHUNK, CHUNK)
            v = mm(n2[rows], weight[h, 0], NT)
            hg = mm(di[rows], weight[h, 1], NT)
            v2 = v * v
            t = jnp.tanh(v * (C0 + (C0 * C1) * v2))
            share = 0.5 + 0.5 * t
            hid[h, rows] = (v * share).astype(bf16)
            slope = share + (0.5 * v) * (1.0 - t * t) * (C0 + (3.0 * C0 * C1) * v2)
            pre[h, rows] = (slope * hg).astype(bf16)
        store(hid.at[h], hid_hbm.at[:, units])
        store(pre.at[h], pre_hbm.at[:, units])
        grad[h, 1] = mm(hid[h], di[...], TN).astype(bf16)
        store(grad.at[h, 1], g_hbm.at[1])
        grad[h, 0] = mm(pre[h], n2[...], TN).astype(bf16)
        store(grad.at[h, 0], g_hbm.at[0])
    stores.wait()


def feed(normed, down_in, weight, after=()):
    rows = normed.shape[0]
    halves = [array for half in weight for array, _ in half]
    places = [place for half in weight for _, place in half]
    return run(
        partial(feed_kernel, places),
        "feed",
        1,
        [(normed, VMEM), (down_in, VMEM)] + [(array, HBM) for array in halves],
        [(shape((rows, 2 * HALF), bf16), HBM)] * 2 + [(shape((2, HALF, D), bf16), HBM)] * 2,
        [pltpu.VMEM((2, 2, HALF, D), bf16)]
        + [pltpu.VMEM((2, rows, HALF), bf16)] * 2
        + [pltpu.VMEM((2, 2, HALF, D), bf16), pltpu.SemaphoreType.DMA((4,)), pltpu.SemaphoreType.DMA((8,))],
        after,
        vmem=32,
    )


def unit_sums(sources, pieces, places, weight, acc, sems):
    w = pl.program_id(0)

    def span(i):
        return slice(i % 2 * HALF, (i % 2 + 1) * HALF)

    @pl.when(w == 0)
    def _():
        loads = Loads(sems)
        for i, piece in enumerate(pieces):
            loads.add(piece.at[places[i]], weight.at[pl.ds(i * HALF, HALF)])
        loads.start()
        for i, copy in enumerate(loads.copies):
            copy.wait()
            term = mm(sources[i // 2][:, span(i)], weight[i * HALF : (i + 1) * HALF])
            acc[...] = term if i == 0 else acc[...] + term

    @pl.when(w > 0)
    def _():
        source = jnp.concatenate([ref[...] for ref in sources], axis=1)
        acc[...] = mm(source, weight[...])


def turn_kernel(places, p0, p1, p2, p3, w0, w1, w2, w3, w4, w5, w6, w7, mid_ref, attn_ref, cot_ref, mode_ref, *rest):
    mg_ref, oi_ref, sum_ref, weight, acc, sems = rest
    unit_sums((p0, p1, p2, p3), (w0, w1, w2, w3, w4, w5, w6, w7), places, weight, acc, sems)
    ng = acc[...]
    hat, rstd = ln_parts(mid_ref[...])
    mg = cot_ref[...].astype(f32) + ln_back(ng, mode_ref[4:5], hat, rstd)
    mg_ref[...] = mg
    oi_ref[...] = (mode_ref[2:3] * mg).astype(bf16)
    sum_ref[0:1] = jnp.sum(mg * attn_ref[...].astype(f32), axis=0, keepdims=True)
    sum_ref[1:2] = jnp.sum(ng, axis=0, keepdims=True)
    sum_ref[2:3] = jnp.sum(ng * hat, axis=0, keepdims=True)


def out_kernel(places, p0, p1, p2, p3, w0, w1, w2, w3, w4, w5, w6, w7, mid_ref, cot_ref, mode_ref, *rest):
    out_ref, sum_ref, weight, acc, sems = rest
    unit_sums((p0, p1, p2, p3), (w0, w1, w2, w3, w4, w5, w6, w7), places, weight, acc, sems)
    mlp = acc[...]
    out_ref[...] = (mid_ref[...] + mode_ref[5:6] * mlp).astype(bf16)
    sum_ref[...] = jnp.sum(cot_ref[...].astype(f32) * mlp, axis=0, keepdims=True)


def of_units(arrays, weights, which):
    halves = [half[which] for pair in weights for half in pair]
    ins = [(array, rows_of(2 * HALF)) for array in arrays] + [(array, HBM) for array, _ in halves]
    scratch = [pltpu.VMEM((8 * HALF, D), bf16), pltpu.VMEM((WIN, D), f32), pltpu.SemaphoreType.DMA((8,))]
    return ins, scratch, [place for _, place in halves]


def turn_step(pre, weights, middle, attn_out, cotangent, modes, after=()):
    count = cotangent.shape[0]
    rows = count * WIN
    ins, scratch, places = of_units(pre, weights, 0)
    return run(
        partial(turn_kernel, places),
        "turn",
        count,
        ins
        + [(middle, rows_of(D)), (attn_out, rows_of(D)), (cotangent, window_of(WIN, D)), (modes, window_of(6, D))],
        [
            (shape((rows, D), f32), rows_of(D)),
            (near((rows, D), bf16), rows_of(D)),
            (shape((count, 3, D), f32), window_of(3, D)),
        ],
        scratch,
        after,
        vmem=36,
        flops=10.7e9,
        moved=35e6,
    )


def out_step(hid, weights, middle, cotangent, modes, after=()):
    count = cotangent.shape[0]
    ins, scratch, places = of_units(hid, weights, 1)
    return run(
        partial(out_kernel, places),
        "output",
        count,
        ins + [(middle, rows_of(D)), (cotangent, window_of(WIN, D)), (modes, window_of(6, D))],
        [(shape((count, WIN, D), bf16), window_of(WIN, D)), (shape((count, 1, D), f32), window_of(1, D))],
        scratch,
        after,
        vmem=36,
        flops=10.7e9,
        moved=30e6,
    )


def attend_back_kernel(
    o0, o1, pk_ref, pr_ref, e_ref, n1_ref, oi_all, ho_hbm, pg_ref, g0_ref, g1_ref, rel_ref, *scratch
):
    pg_all, t_all, ow, ho_ref, sems = scratch
    w = pl.program_id(0)
    loads = Loads(sems)
    weights = [loads.add(o.at[QKV:], ow.at[pl.ds(i * 128, 128)]) for i, o in enumerate((o0, o1))]
    heads = loads.add(ho_hbm, ho_ref)

    @pl.when(w == 0)
    def _():
        loads.start()
        t_all[...] = jnp.zeros_like(t_all)
        for copy in weights:
            copy.wait()

    hg = mm(oi_all[pl.ds(pl.multiple_of(w * WIN, WIN), WIN)], ow[...], NT).astype(bf16)
    pk = pk_ref[...]
    low = lax.broadcasted_iota(jnp.int32, (WIN, 128), 1) < 64
    for p in range(2):
        q = pk[:, p * QKV : p * QKV + 128]
        k = pk[:, p * QKV + 128 : p * QKV + 256]
        v = pk[:, p * QKV + 256 : p * QKV + 384]
        do = hg[:, p * 128 : (p + 1) * 128]
        k_rows = k.T
        dv, dq, dk = [], [], []
        for i in range(2):
            mine = low if i == 0 else ~low
            qa = jnp.where(mine, q, e_ref[...])
            dp = mm(jnp.where(mine, v, jnp.zeros_like(v)), do, NT)
            prl = pr_ref[2 * p + i]
            pr = prl.astype(f32)
            t = pr * dp
            ds = (t - pr * jnp.sum(t, axis=0, keepdims=True)).astype(bf16)
            dv.append(mm(prl, do))
            dq.append(mm(k_rows[i * HD : (i + 1) * HD], ds))
            dk.append(mm(ds, qa))
        dq = jnp.concatenate(dq, axis=0).T
        block = jnp.concatenate(
            [dq, jnp.where(low, dk[0], dk[1]), jnp.where(low, dv[0], dv[1])], axis=1
        ).astype(bf16)
        pg_ref[:, p * QKV : (p + 1) * QKV] = block
        pg_all[pl.ds(pl.multiple_of(w * WIN, WIN), WIN), p * QKV : (p + 1) * QKV] = block
        t_all[p] += jnp.where(low, dk[1], dk[0])

    @pl.when(w == pl.num_programs(0) - 1)
    def _():
        heads.wait()
        go = mm(ho_ref[...], oi_all[...], TN).astype(bf16)
        gq = mm(pg_all[...], n1_ref[...], TN).astype(bf16)
        for p, g_ref in enumerate((g0_ref, g1_ref)):
            g_ref[:QKV] = gq[p * QKV : (p + 1) * QKV]
            g_ref[QKV:] = go[p * 128 : (p + 1) * 128]
        hot = e_ref[...].astype(f32)
        for p in range(2):
            sums = lax.dot_general(hot, t_all[p], TN, precision=precise, preferred_element_type=f32)
            rel_ref[p] = sums[:32]


def attend_back(out_in, weight, packed, probs, query_hot, normed, heads, after=()):
    rows = normed.shape[0]
    return run(
        attend_back_kernel,
        "attend_back",
        rows // WIN,
        [
            (weight[0], HBM),
            (weight[1], HBM),
            (packed, rows_of(2 * QKV)),
            (probs, pl.BlockSpec((4, WIN, WIN), lambda i: (i, 0, 0))),
            (query_hot, whole(WIN, 128)),
            (normed, VMEM),
            (out_in, VMEM),
            (heads, HBM),
        ],
        [
            (shape((rows, 2 * QKV), bf16), rows_of(2 * QKV)),
            (shape((HALF, D), bf16), whole(HALF, D)),
            (shape((HALF, D), bf16), whole(HALF, D)),
            (shape((2, 32, 128), f32), whole(2, 32, 128)),
        ],
        [pltpu.VMEM((rows, 2 * QKV), bf16), pltpu.VMEM((2, WIN, 128), f32), pltpu.VMEM((256, D), bf16)]
        + [pltpu.VMEM((rows, 256), bf16), pltpu.SemaphoreType.DMA((3,))],
        after,
        flops=13e9,
        moved=20e6,
        vmem=18,
    )


def last_kernel(p0, p1, p2, p3, w0, w1, w2, w3, w4, w5, w6, w7, tok_ref, mode_ref, mg_ref, out_ref, sum_ref, w_all, acc, sems):
    @pl.when(pl.program_id(0) == 0)
    def _():
        loads = Loads(sems)
        for i, ref in enumerate((w0, w1, w2, w3, w4, w5, w6, w7)):
            loads.add(ref.at[:QKV], w_all.at[pl.ds(i * QKV, QKV)])
        loads.start()
        for i, src in enumerate((p0, p1, p2, p3)):
            loads.copies[2 * i].wait()
            loads.copies[2 * i + 1].wait()
            term = mm(src[...], w_all[i * 2 * QKV : (i + 1) * 2 * QKV])
            acc[...] = term if i == 0 else acc[...] + term

    @pl.when(pl.program_id(0) > 0)
    def _():
        acc[...] = mm(jnp.concatenate([p0[...], p1[...], p2[...], p3[...]], axis=1), w_all[...])

    ng = acc[...]
    hat, rstd = ln_parts(tok_ref[...].astype(f32))
    out_ref[...] = (mg_ref[...] + ln_back(ng, mode_ref[1:2], hat, rstd)).astype(bf16)
    sum_ref[0:1] = jnp.sum(ng, axis=0, keepdims=True)
    sum_ref[1:2] = jnp.sum(ng * hat, axis=0, keepdims=True)


def last_step(packed_grads, weights, tokens, modes, middle_grad, after=()):
    count = tokens.shape[0]
    return run(
        last_kernel,
        "last",
        count,
        [(array, rows_of(2 * QKV)) for array in packed_grads]
        + [(half, HBM) for pair in weights for half in pair]
        + [(tokens, window_of(WIN, D)), (modes, window_of(6, D)), (middle_grad, rows_of(D))],
        [(shape((count, WIN, D), bf16), window_of(WIN, D)), (shape((count, 2, D), f32), window_of(2, D))],
        [pltpu.VMEM((8 * QKV, D), bf16), pltpu.VMEM((WIN, D), f32), pltpu.SemaphoreType.DMA((8,))],
        after,
        flops=8e9,
        moved=24e6,
    )


def merge_kernel(sums, count, *refs):
    i = pl.program_id(0)
    refs = list(refs)
    outs = refs[len(refs) - len(sums) :]
    for spans, out in zip(sums, outs):
        value = None
        for first, last in spans:
            term = refs.pop(0)[...].astype(f32)
            if (first, last) != (0, count):
                term = jnp.where((i >= first) & (i < last), term, 0.0)
            value = term if value is None else value + term
        out[...] = value.astype(bf16)


def merge(*sums, rows=HALF, after=()):
    block = min(256, rows)
    ins, spans = [], []
    for terms in sums:
        spans.append([])
        for array, place, start, *limits in terms:
            first, last = [limit // block for limit in (limits or (0, rows))]
            start = start // block

            def at(i, start=start, first=first, last=last):
                return jnp.clip(i, first, last - 1) + start

            if place is None:
                spec = pl.BlockSpec((block, D), lambda i, at=at: (at(i), 0))
            else:
                spec = pl.BlockSpec((None, block, D), lambda i, p=place, at=at: (p, at(i), 0))
            ins.append((array, spec))
            spans[-1].append((first, last))
    out = (shape((rows, D), bf16), pl.BlockSpec((block, D), lambda i: (i, 0)))
    return run(partial(merge_kernel, spans, rows // block), "merge", rows // block, ins, [out] * len(sums), (), after)


def parts_kernel(count, only, z_ref, *refs):
    which_sum = pl.program_id(0) % (1 + max([0] + [w for w in only if w is not None]))
    terms = len(only)
    for k in range(count):
        value = None
        for ref, which in zip(refs[k * terms : (k + 1) * terms], only):
            term = ref[...].astype(f32)
            if which is not None:
                term = jnp.where(which_sum == which, term, 0.0)
            value = term if value is None else value + term
        refs[count * terms + k][...] = value.astype(bf16)


def merge_parts(terms, z, count, outputs):
    size = HALF // count
    sums = 2 if terms[0].ndim == 3 else 1
    ins, only = [], []
    for j in range(outputs):
        for term in terms:
            array, which = term if type(term) is tuple else (term, None)
            dims = array.array.ndim if isinstance(array, Moved) else array.ndim

            def at(i, zr, j=j):
                return zr[0] ^ (i // sums * outputs + j)

            if dims == 3:
                spec = pl.BlockSpec((None, size, D), lambda i, zr, at=at: (i % sums, at(i, zr), 0))
            else:
                spec = pl.BlockSpec((size, D), lambda i, zr, at=at: (at(i, zr), 0))
            ins.append((array, spec))
            only.append(which)
    grid = sums * count // outputs
    outs = [(shape((grid * size, D), bf16), pl.BlockSpec((size, D), lambda i, zr: (i, 0)))] * outputs
    return run(partial(parts_kernel, outputs, only[: len(terms)]), "merge_parts", grid, ins, outs, (), (), [z])


def attn_final_kernel(place_ref, a_ref, b_ref, qkv_ref, out_ref, rows, hot):
    core, z = place_ref[0], place_ref[1]
    size = HALF // 4

    @pl.when(pl.program_id(0) == 0)
    def _():
        match, row = hot_rows(2 * QKV, qkv_source(core))
        inner = jnp.where(row >= QKV, row - QKV, row)
        hot[...] = jnp.where(match, jnp.where(inner < 128, HD**-0.5, 1.0), 0.0).astype(bf16)

    for h, ref in enumerate((a_ref, b_ref)):
        for k in range(4):
            part_at = z ^ k
            block = ref[k * size : (k + 1) * size]

            @pl.when(part_at < 3)
            def _():
                rows[pl.ds(pl.multiple_of(h * QKV + part_at * size, size), size)] = block

            @pl.when(part_at == 3)
            def _():
                out_ref[pl.ds(pl.multiple_of((core ^ h) * size, size), size)] = block.astype(f32)

    qkv_ref[...] = mm(rows[...], hot[...], TN)


def columns_of(rows):
    return pl.BlockSpec((rows, 256), lambda i, *_: (0, i))


def attn_final(place, a, b):
    ins = [(a, columns_of(HALF)), (b, columns_of(HALF))]
    outs = [
        (shape((D, 2 * QKV), f32), pl.BlockSpec((256, 2 * QKV), lambda i, *_: (i, 0))),
        (shape((256, D), f32), columns_of(256)),
    ]
    scratch = [pltpu.VMEM((2 * QKV, 256), bf16), pltpu.VMEM((2 * QKV, 2 * QKV), bf16)]
    return run(attn_final_kernel, "attn_final", D // 256, ins, outs, scratch, (), [place])


def feed_final_kernel(place_ref, *refs):
    up_ref, down_ref, rows, hot = refs[4:]
    core, z = place_ref[0], place_ref[1]
    size = HALF // 4

    @pl.when(pl.program_id(0) == 0)
    def _():
        hot[...] = jnp.where(hot_rows(2 * HALF, lambda row: row ^ (core * HALF))[0], 1.0, 0.0).astype(bf16)

    for h in range(2):
        for k, (ref, first) in enumerate(((refs[2 * h], 0), (refs[2 * h + 1], 0), (refs[2 * h], 2), (refs[2 * h + 1], 2))):
            start = (z ^ k) * size
            rows[pl.ds(pl.multiple_of(h * HALF + start, size), size)] = ref[first * size : (first + 1) * size]
            block = ref[(first + 1) * size : (first + 2) * size].astype(f32)
            down_ref[pl.ds(pl.multiple_of((core ^ h) * HALF + start, size), size)] = block
    up_ref[...] = mm(rows[...], hot[...], TN)


def feed_final(place, even, odd, other_even, other_odd):
    ins = [(v, columns_of(HALF)) for v in (even, odd, other_even, other_odd)]
    outs = [
        (shape((D, 2 * HALF), f32), pl.BlockSpec((256, 2 * HALF), lambda i, *_: (i, 0))),
        (shape((2 * HALF, D), f32), columns_of(2 * HALF)),
    ]
    scratch = [pltpu.VMEM((2 * HALF, 256), bf16), pltpu.VMEM((2 * HALF, 2 * HALF), bf16)]
    return run(feed_final_kernel, "feed_final", D // 256, ins, outs, scratch, (), [place])


def mode_shares_kernel(m0, m1, m2, m3, rel_ref, ada_ref, low_ref, s0, s1, s2, s3, rows):
    count = m0.shape[0]
    for r, ref in enumerate((m0, m1, m2, m3)):
        rows[r * count : (r + 1) * count] = ref[...]
    low = rows[...].astype(bf16)
    low_ref[...] = low
    cond = mm(low, ada_ref[...], NT)
    for r, ref in enumerate((s0, s1, s2, s3)):
        ref[:, :D] = cond
        ref[:, D:] = rel_ref[r]


def mode_shares(messages, rel_part, ada_weight):
    count, columns = messages[0].shape
    rows = 4 * count
    ins = [(v, whole(count, columns)) for v in messages]
    ins += [(rel_part, whole(4, rows, 128)), (ada_weight, whole(D, columns))]
    outs = [(shape((rows, columns), bf16), whole(rows, columns))] + [(shape((rows, D + 128), f32), whole(rows, D + 128))] * 4
    return run(mode_shares_kernel, "mode_shares", 1, ins, outs, [pltpu.VMEM((rows, columns), f32)])


def mode_rows_kernel(mp_ref, low_ref, s0, s1, s2, s3, slope_ref, cond_ref, out_ref):
    rows, columns = low_ref.shape
    count = rows // 4
    mp = mp_ref[0]
    moved = [s0[:, :D]]
    for k, ref in ((1, s1), (2, s2), (3, s3)):
        blocks = [ref[(r ^ k) * count : ((r ^ k) + 1) * count, :D] for r in range(4)]
        moved.append(jnp.concatenate(blocks, axis=0))
    cond = (moved[0] + moved[1]) + (moved[2] + moved[3])
    value = (cond * slope_ref[...]).astype(bf16)
    row = lax.broadcasted_iota(jnp.int32, (rows, rows), 0)
    col = lax.broadcasted_iota(jnp.int32, (rows, rows), 1)
    hot = jnp.where(col == row ^ (mp * count), 1.0, 0.0).astype(bf16)
    out_ref[:, :columns] = low_ref[...]
    out_ref[:, columns : columns + D] = mm(hot, value).astype(bf16)
    out_ref[:, columns + D : columns + D + 128] = (s0[:, D:] + s1[:, D:] + s2[:, D:] + s3[:, D:]).astype(bf16)
    out_ref[:, columns + D + 128 :] = cond_ref[...]


def mode_rows(mp, low, shares, slope, cond):
    rows, columns = low.shape
    width = columns + 2 * (D + 128)
    ins = [(low, whole(rows, columns))] + [(v, whole(rows, D + 128)) for v in shares]
    ins += [(slope, whole(rows, D)), (cond, whole(rows, D + 128))]
    outs = [(shape((rows, width), bf16), whole(rows, width))]
    return run(mode_rows_kernel, "mode_rows", 1, ins, outs, (), (), [mp])[0]


def mode_final_kernel(dp_ref, own_ref, other_ref, ada_ref, bias_ref, class_ref, rel_ref, rows, *, count, columns):
    size = own_ref.shape[0] // count
    i, width = pl.program_id(0), ada_ref.shape[1]
    marks = [columns, columns + D, columns + D + 128, columns + 2 * D + 128, columns + 2 * D + 256]

    @pl.when(i == 0)
    def _():
        for core, ref in enumerate((own_ref, other_ref)):
            for k in range(count):
                at = (dp_ref[0] ^ (2 * k + core)) * size
                rows[pl.ds(pl.multiple_of(at, size), size)] = ref[k * size : (k + 1) * size]
        classes, rel, _, index = [rows[:, i:j] for i, j in zip(marks, marks[1:])]
        lane = lax.broadcasted_iota(jnp.int32, index.shape, 1).astype(f32)
        hot = jnp.where(lane == index[:, :1].astype(f32), 1.0, 0.0).astype(bf16)
        class_ref[...] = mm(hot, classes, TN)[: class_ref.shape[0]]
        total = rel[:size].astype(f32)
        for k in range(1, 2 * count):
            total = total + rel[k * size : (k + 1) * size].astype(f32)
        rel_ref[...] = total[: rel_ref.shape[0], : rel_ref.shape[1]]
        bias_ref[...] = jnp.sum(rows[:, :columns].astype(f32), axis=0)

    modes = rows[:, pl.ds(pl.multiple_of(i * width, width), width)]
    ada_ref[...] = mm(rows[:, marks[2] : marks[3]], modes, TN)


def mode_final(dp, own, other, count, columns, class_count, rel_shape):
    size, width = own.shape
    outs = [(shape((D, columns), f32), pl.BlockSpec((D, columns // 3), lambda i, *_: (0, i)))]
    outs += [(shape(dims, f32), whole(*dims)) for dims in ((columns,), (class_count, D), rel_shape)]
    kernel = partial(mode_final_kernel, count=count, columns=columns)
    ins = [(own, whole(size, width)), (other, whole(size, width))]
    return run(kernel, "mode_final", 3, ins, outs, [pltpu.VMEM((2 * size, width), bf16)], (), [dp], vmem=32)


def silu_plain(values):
    return values / (1.0 + jnp.exp(-values))


def condition(timesteps, classes, class_table):
    half_width = class_table.shape[1] // 2
    frequency = jnp.exp(
        -math.log(10000.0) * jnp.arange(half_width).astype(class_table.dtype) / half_width
    )
    phase_angle = timesteps.astype(class_table.dtype)[..., None] * frequency
    sinusoid = jnp.concatenate([jnp.cos(phase_angle), jnp.sin(phase_angle)], axis=-1)
    onehot = (classes[..., None] == jnp.arange(class_table.shape[0])).astype(class_table.dtype)
    lookup = jnp.einsum("mwc,cd->mwd", onehot, class_table, precision=precise)
    return sinusoid + lookup


SPANS = ((0, 0, WT), (WT, 2 * WT - 1, WH), (WT + WH, 2 * WT + 2 * WH - 2, WW))


def place_hot():
    spot = np.arange(WIN)
    hot = np.zeros((WIN, NOFF), np.float32)
    for (start, _, _), where in zip(SPANS, (spot // (WH * WW), (spot // WW) % WH, spot % WW)):
        hot[spot, start + where] = 1.0
    return hot


def query_side():
    half = np.zeros((WIN, 64), np.float32)
    half[:, :NOFF] = place_hot()
    half[:, NOFF : 2 * NOFF] = place_hot()
    half[:, 2 * NOFF] = 1.0
    return np.concatenate([half, half], axis=1)


def offset_hot(rows, copies):
    hot = np.zeros((2 * NOFF - 3, rows, 64), np.float32)
    for start, begin, length in SPANS:
        for key in range(length):
            for query in range(length):
                for copy in range(copies):
                    hot[begin + query - key + length - 1, start + key, copy * NOFF + start + query] = 1.0
    return hot


def key_tables(rel, core):
    value = jnp.einsum("hr,rkq->hkq", rel.reshape(16, -1), offset_hot(64, 2), precision=precise)
    top = lax.reduce_precision(value, 8, 7)
    value = jnp.where(jnp.arange(64) < NOFF, top, value - top).astype(bf16)
    value = value.reshape(4, 2, 2, 64, 64)
    value = jnp.where(core == 0, value, value[:, ::-1])
    value = jnp.concatenate([value[:, :, 1], value[:, :, 0]], axis=-1)
    return jnp.pad(value, ((0, 0), (0, 0), (0, 64), (0, 0)))


def rel_sums(grids, core):
    grids = jnp.where(core == 0, grids, grids[:, ::-1])
    grids = grids.reshape(4, 2, 32, 2, 64)
    grids = jnp.stack([grids[:, :, :, 1], grids[:, :, :, 0]], axis=2).reshape(16, 32, 64)
    return jnp.einsum("hkq,rkq->hr", grids, offset_hot(32, 1), precision=precise).reshape(4, 4, -1)


def local_windows(
    sizes,
    tokens,
    cotangent,
    qkv_weight,
    out_weight,
    up_weight,
    down_weight,
    ada_weight,
    ada_bias,
    rel_bias,
    class_table,
    lengths,
    timesteps,
    classes,
):
    n_z, n_mp = sizes
    n_dp = 2 * n_z
    micro = tokens.shape[0]
    mp = lax.axis_index("mp")
    z = lax.axis_index("z")
    core = lax.axis_index("core")

    def swap_mp(bit):
        return lambda v: lax.ppermute(v, "mp", [(i, i ^ bit) for i in range(n_mp)])

    def swap_dp(bit):
        return lambda v: lax.ppermute(v, ("z", "core"), [(i, i ^ bit) for i in range(n_dp)])

    px, py, pd = swap_mp(1), swap_mp(2), swap_mp(3)
    pc = swap_dp(1)
    by_rel = [lambda v: v, px, py, pd]

    def cat(a, b, axis=0):
        return jnp.concatenate([a, b], axis=axis)

    cut = HALF // 2

    pre_cond = condition(timesteps, classes, class_table)
    cond_low = silu_plain(pre_cond).astype(bf16)
    mode_cols = jnp.einsum("mwd,de->mwe", cond_low, ada_weight, preferred_element_type=f32) + ada_bias.astype(f32)
    order = jnp.arange(4) ^ mp
    rel_row = jnp.pad(rel_bias, ((0, 0), (0, 128 - rel_bias.shape[1])))
    messages = [
        by_rel[r](cat(lax.dynamic_index_in_dim(mode_cols, mp ^ r, axis=1, keepdims=False), rel_row, 1))
        for r in range(4)
    ]
    messages = jnp.stack(messages)
    columns = mode_cols.shape[-1]
    modes = jnp.take(messages[:, :, :columns], order, axis=0)
    modes = modes.transpose(1, 0, 2).reshape(micro, 6, D)
    tables = key_tables(messages[:, :, columns : columns + rel_bias.shape[1]], core)
    own_lengths = lax.dynamic_index_in_dim(lengths, mp, axis=1, keepdims=False)

    core_row = core.reshape(1)
    query_hot = jnp.asarray(query_side(), bf16)
    packed, heads, probs = [None] * 4, [None] * 4, [None] * 4

    attn_own = list(attn_rows(core_row, qkv_weight, out_weight, [mode_cols]))
    (attn_own[0],) = hold(attn_own[:1], [messages])
    ax, ay = px(attn_own[0]), py(attn_own[0])
    normed_one, packed[0], heads[0], probs[0] = attend(own_lengths, tokens, modes, attn_own, tables[0], query_hot)
    up0, down0, up1, down1 = feed_rows(core_row, up_weight, down_weight, [heads[0]])
    ax, ay = hold([ax, ay], [down1])
    adx, ady = py(ax[: HALF // 2]), px(ay[HALF // 2 :])
    attn_w = [attn_own] + [[Moved(v), Moved(pc(v))] for v in (ax, ay)]
    packed[1], heads[1], probs[1] = attend(
        own_lengths, normed_one, modes, attn_w[1], tables[1], query_hot, [down1]
    )
    adx, ady = hold([adx, ady], [heads[1]])
    (ad,) = merge([(Moved(adx), None, 0, 0, cut), (Moved(ady), None, -cut, cut, HALF)])
    up0, down0 = hold([up0, down0], [ad])
    x_up, y_down = px(up0), py(down0)
    attn_w.append([ad, Moved(pc(ad))])
    packed[2], heads[2], probs[2] = attend(
        own_lengths, normed_one, modes, attn_w[2], tables[2], query_hot, [heads[1]]
    )
    packed[3], heads[3], probs[3] = attend(
        own_lengths, normed_one, modes, attn_w[3], tables[3], query_hot, [heads[2]]
    )
    x_up, y_down = hold([x_up, y_down], [heads[3]])
    d_up, d_down = py(x_up), px(y_down)
    attn_w = [[v.array if isinstance(v, Moved) else v for v in halves] for halves in attn_w]
    attn_out, middle, normed_two, down_in = middle_step(heads, attn_w, tokens, cotangent, modes)

    hid, pre, mine, other = [None] * 4, [None] * 4, [None] * 4, [None] * 4

    def feed_step(r, weight, after):
        hid[r], pre[r], mine[r], sent = feed(normed_two, down_in, weight, after)
        other[r] = pc(sent)

    def pair(r, which):
        return [(mine[r], which, 0), (Moved(other[r]), which, 0)]

    def weight_of(up, down):
        return [((Moved(u), 0), (Moved(v), 0)) for u, v in ((up, down), (pc(up), pc(down)))]

    feed_w = [[((up0, 0), (down0, 0)), ((up1, 0), (down1, 0))], None, None, None]
    feed_step(0, feed_w[0], [])
    d_up, d_down = hold([d_up, d_down], [hid[0]])
    feed_w[3] = weight_of(d_up, d_down)
    feed_step(3, feed_w[3], [hid[0]])
    x_down, y_up = arrive([px(down0), py(up0)], [hid[3]])
    feed_w[1], feed_w[2] = weight_of(x_up, x_down), weight_of(y_up, y_down)
    diag_x, diag_y = merge(pair(3, 0), pair(3, 1), after=[hid[3]])
    feed_step(1, feed_w[1], [hid[3], diag_x])
    feed_step(2, feed_w[2], [hid[1]])
    diag_x, diag_y = arrive([px(diag_x), py(diag_y)], [hid[2]])
    both = 2 * HALF
    flat = [v.reshape(both, D) for v in mine]
    flat_other = [v.reshape(both, D) for v in other]
    (last_x,) = merge(
        [(flat[1], None, 0), (Moved(flat_other[1]), None, 0), (Moved(diag_y), None, -HALF, HALF, both)], rows=both
    )
    (last_y,) = merge(
        [(flat[2], None, 0), (Moved(flat_other[2]), None, 0), (Moved(diag_x), None, 0, 0, HALF)], rows=both, after=[last_x]
    )
    middle_grad, out_in, turn_sums = turn_step(
        pre, feed_w, middle, attn_out, cotangent, modes, [last_x, last_y]
    )
    own_pre = jnp.take(pre_cond.transpose(1, 0, 2), order, axis=0).reshape(4 * micro, D)
    share = 1.0 / (1.0 + jnp.exp(-own_pre))
    class_col = jnp.pad(classes.T.reshape(-1, 1).astype(bf16), ((0, 0), (0, 127)))
    cond_rel = jnp.take(cond_low, order, axis=1).transpose(1, 0, 2).reshape(4 * micro, D)
    slope, cond_rel = hold([share * (1.0 + own_pre * (1.0 - share)), cat(cond_rel, class_col, 1)])

    packed_grad, rel_grid, a_mine, a_other = [None] * 4, [None] * 4, [None] * 4, [None] * 4

    def back_step(r, after):
        packed_grad[r], a_mine[r], sent, rel_grid[r] = attend_back(
            out_in, attn_w[r], packed[r], probs[r], query_hot, normed_one, heads[r], after
        )
        a_other[r] = pc(sent)

    def a_pair(r, start):
        return [(a_mine[r], None, start), (Moved(a_other[r]), None, start)]

    back_step(3, [turn_sums])
    last_x, last_y = arrive([px(last_x), py(last_y)], [packed_grad[3]])
    z_row = z.reshape(1)
    terms = [mine[0], Moved(other[0]), *[Moved(v.reshape(2, HALF, D)) for v in (last_x, last_y)]]
    feed_keep, feed_sent = merge_parts(terms, z_row, n_z, 2)
    z_one, z_two = swap_dp(2), swap_dp(4)

    back_step(1, [feed_keep])
    (feed_got,) = arrive([z_one(feed_sent)], [packed_grad[1]])
    (feed_sent,) = merge([(feed_keep, None, cut), (Moved(feed_got), None, cut)], rows=cut)
    a_diag_x, a_diag_y = merge(a_pair(3, 0), a_pair(3, cut), rows=cut, after=[feed_sent])
    back_step(2, [feed_sent, a_diag_x, a_diag_y, slope, cond_rel])
    feed_two, a_diag_x, a_diag_y = arrive([z_two(feed_sent), px(a_diag_x), py(a_diag_y)], [packed_grad[2]])
    (feed_one,) = merge([(feed_keep, None, 0), (Moved(feed_got), None, 0), (Moved(feed_two), None, 0)], rows=cut)
    (a_last_x,) = merge(a_pair(1, 0) + [(Moved(a_diag_y), None, -cut, cut, HALF)], after=[feed_one])
    (a_last_y,) = merge(a_pair(2, 0) + [(Moved(a_diag_x), None, 0, 0, cut)], after=[a_last_x])
    back_step(0, [feed_one, a_last_y])
    feed_two, a_last_x, a_last_y = arrive([z_two(feed_one), px(a_last_x), py(a_last_y)], [packed_grad[0]])
    feed_even = cat(feed_one, feed_two)

    def exchange(parts):
        return [swap_dp(2 * k)(v) for k, v in enumerate(parts) if k]

    attn_parts = merge_parts([a_mine[0], *map(Moved, (a_other[0], a_last_x, a_last_y))], z_row, n_z, n_z)
    still = [[[(v.array if isinstance(v, Moved) else v, at) for v, at in half] for half in halves] for halves in feed_w]
    output, out_sums = out_step(hid, still, middle, cotangent, modes, [*attn_parts, feed_even])
    token_grads, last_sums = last_step(packed_grad, attn_w, tokens, modes, middle_grad, [out_sums])
    feed_odd, *attn_got = arrive([z_one(feed_even), *exchange(attn_parts)], [last_sums])
    (attn_own,) = merge([(v, None, 0) for v in (attn_parts[0], *attn_got)], rows=HALF // n_z)

    place = jnp.stack([core, z])
    mode_grad = jnp.concatenate([last_sums, turn_sums, out_sums], axis=1).reshape(micro, 4, -1).transpose(1, 0, 2)
    messages = [lax.dynamic_index_in_dim(mode_grad, mp ^ r, axis=0, keepdims=False) for r in range(4)]
    rel_grid = hold(rel_grid, [attn_own])
    rel_part = jnp.pad(rel_sums(jnp.stack(rel_grid), core), ((0, 0), (0, 4 * (micro - 1)), (0, 128 - rel_bias.shape[1])))
    *messages[1:], attn_far, feed_even_other, feed_odd_other = arrive(
        [by_rel[r](messages[r]) for r in (1, 2, 3)] + [swap_dp(6)(attn_own), pc(feed_even), pc(feed_odd)], [attn_own]
    )
    mode_low, *shares = mode_shares(messages, rel_part, ada_weight)
    grad_up, grad_down = feed_final(place, feed_even, Moved(feed_odd), Moved(feed_even_other), Moved(feed_odd_other))
    *shares[1:], attn_two, attn_one = arrive(
        [by_rel[r](shares[r]) for r in (1, 2, 3)] + [swap_dp(4)(attn_own), swap_dp(2)(attn_own)], [attn_far, grad_up]
    )
    grads = mode_rows(mp.reshape(1), mode_low, shares, slope, cond_rel)
    attn_own = jnp.concatenate([attn_own, attn_one, attn_two, attn_far])
    got = exchange([grads] * n_z)
    (attn_other,) = hold([pc(attn_own)], [grads])
    grad_qkv, grad_out = attn_final(place, attn_own, Moved(attn_other))
    got = arrive(got, [grad_qkv])
    grads = jnp.concatenate([grads, *got])
    grad_ada, grad_ada_bias, class_grad, grad_rel = mode_final(
        (2 * z + core).reshape(1), grads, pc(grads), n_z, columns, class_table.shape[0], rel_bias.shape
    )

    return (
        output,
        token_grads,
        grad_qkv,
        grad_out,
        grad_up,
        grad_down,
        grad_ada,
        grad_ada_bias,
        grad_rel,
        class_grad,
    )


def layer_norm(values):
    center = values - jnp.mean(values, axis=-1, keepdims=True)
    spread = jnp.mean(center * center, axis=-1, keepdims=True)
    return center * lax.rsqrt(spread + EPS)


def modulate(values, shift, scale):
    return layer_norm(values) * (1.0 + scale) + shift


def gelu_tanh(values):
    return (
        0.5
        * values
        * (
            1.0
            + jnp.tanh(math.sqrt(2.0 / math.pi) * (values + 0.044715 * values * values * values))
        )
    )


def condition_whole(timesteps, classes, class_table):
    half_width = class_table.shape[1] // 2
    frequency = jnp.exp(
        -math.log(10000.0) * jnp.arange(half_width).astype(class_table.dtype) / half_width
    )
    phase_angle = timesteps.astype(class_table.dtype)[..., None] * frequency
    sinusoid = jnp.concatenate([jnp.cos(phase_angle), jnp.sin(phase_angle)], axis=-1)
    onehot = (classes[..., None] == jnp.arange(class_table.shape[0])[None, None, :]).astype(
        class_table.dtype
    )
    lookup = jnp.einsum("mwc,cd->mwd", onehot, class_table, precision=precise)
    return silu_plain(sinusoid + lookup)


def axis_table(rel_part, window_span):
    places = jnp.arange(window_span)
    offsets = places[:, None] - places[None, :] + window_span - 1
    onehot = (offsets[:, :, None] == jnp.arange(2 * window_span - 1)[None, None, :]).astype(
        rel_part.dtype
    )
    return jnp.einsum("hr,abr->hab", rel_part, onehot, precision=precise)


def window_bias(rel_bias):
    frame_part = axis_table(rel_bias[:, : 2 * WT - 1], WT)
    row_part = axis_table(rel_bias[:, 2 * WT - 1 : 2 * WT + 2 * WH - 2], WH)
    column_part = axis_table(rel_bias[:, 2 * WT + 2 * WH - 2 :], WW)
    full_bias = (
        frame_part[:, :, None, None, :, None, None]
        + row_part[:, None, :, None, None, :, None]
        + column_part[:, None, None, :, None, None, :]
    )
    return full_bias.reshape(rel_bias.shape[0], WIN, WIN)


def attention_scores(query_part, key_part, bias_full, masks):
    scores = (
        jnp.einsum("wqhd,wkhd->whqk", query_part, key_part, preferred_element_type=jnp.float32)
        * HD ** (-0.5)
        + bias_full[None]
    )
    return jnp.where(masks[:, None, None, :], scores, -1e30)


def local_general(
    tokens,
    cotangent,
    qkv_weight,
    out_weight,
    up_weight,
    down_weight,
    ada_weight,
    ada_bias,
    rel_bias,
    class_table,
    lengths,
    timesteps,
    classes,
):
    micro_count = tokens.shape[0]
    row_count = tokens.shape[1]
    win_count = lengths.shape[1]
    heads_here = rel_bias.shape[0]
    head_scale = HD ** (-0.5)
    first_row = lax.axis_index("mp") * row_count
    row_window = (first_row + jnp.arange(row_count)) // WIN
    spread_rows = (row_window[:, None] == jnp.arange(win_count)[None, :]).astype(jnp.float32)
    cond_low = condition_whole(timesteps, classes, class_table).astype(jnp.bfloat16)
    mode_cols = jnp.einsum(
        "mwd,de->mwe", cond_low, ada_weight, preferred_element_type=jnp.float32
    ) + ada_bias.astype(jnp.float32)
    mode_all = lax.all_gather(mode_cols, "mp", axis=2, tiled=True)
    bias_full, bias_pull = jax.vjp(window_bias, rel_bias)
    frame_of = jnp.arange(WIN) // (WH * WW)
    grad_qkv = jnp.zeros(qkv_weight.shape, jnp.float32)
    grad_out = jnp.zeros(out_weight.shape, jnp.float32)
    grad_up = jnp.zeros(up_weight.shape, jnp.float32)
    grad_down = jnp.zeros(down_weight.shape, jnp.float32)
    grad_rel = jnp.zeros(rel_bias.shape, jnp.float32)
    mode_parts = []
    outputs = []
    token_grads = []
    for micro_step in range(micro_count):
        mode_rows = jnp.dot(spread_rows, mode_all[micro_step], precision=precise)
        shift_attn, scale_attn, gate_attn, shift_mlp, scale_mlp, gate_mlp = jnp.split(
            mode_rows, 6, axis=1
        )
        inputs = tokens[micro_step].astype(jnp.float32)
        normed_one, pull_one = jax.vjp(modulate, inputs, shift_attn, scale_attn)
        gathered_one = lax.all_gather(normed_one.astype(jnp.bfloat16), "mp", axis=0, tiled=True)
        packed = jnp.dot(gathered_one, qkv_weight, preferred_element_type=jnp.float32).astype(
            jnp.bfloat16
        )
        packed = packed.reshape(win_count, WIN, heads_here, 3, HD)
        query_part = packed[:, :, :, 0]
        key_part = packed[:, :, :, 1]
        value_part = packed[:, :, :, 2]
        masks = frame_of[None, :] < lengths[micro_step][:, None]
        scores = attention_scores(query_part, key_part, bias_full, masks)
        top_score = jnp.max(scores, axis=-1, keepdims=True)
        expo = jnp.exp(scores - top_score)
        total = jnp.sum(expo, axis=-1, keepdims=True)
        log_total = top_score + jnp.log(total)
        probs_low = (expo / total).astype(jnp.bfloat16)
        heads_out = jnp.einsum(
            "whqk,wkhd->wqhd", probs_low, value_part, preferred_element_type=jnp.float32
        ).astype(jnp.bfloat16)
        heads_out = heads_out.reshape(win_count * WIN, heads_here * HD)
        attn_out = lax.psum_scatter(
            jnp.dot(heads_out, out_weight, preferred_element_type=jnp.float32),
            "mp",
            scatter_dimension=0,
            tiled=True,
        )
        middle = inputs + gate_attn * attn_out
        normed_two, pull_two = jax.vjp(modulate, middle, shift_mlp, scale_mlp)
        grad_y = cotangent[micro_step].astype(jnp.float32)
        down_in = (gate_mlp * grad_y).astype(jnp.bfloat16)
        gathered_two = lax.all_gather(normed_two.astype(jnp.bfloat16), "mp", axis=0, tiled=True)
        hidden_pre = jnp.dot(gathered_two, up_weight, preferred_element_type=jnp.float32)
        hidden_low, gelu_pull = jax.vjp(gelu_tanh, hidden_pre)
        hidden_low = hidden_low.astype(jnp.bfloat16)
        mlp_out = lax.psum_scatter(
            jnp.dot(hidden_low, down_weight, preferred_element_type=jnp.float32),
            "mp",
            scatter_dimension=0,
            tiled=True,
        )
        down_all = lax.all_gather(down_in, "mp", axis=0, tiled=True)
        hidden_grad = jnp.einsum(
            "rd,fd->rf", down_all, down_weight, preferred_element_type=jnp.float32
        )
        micro_down = jnp.einsum(
            "rf,rd->fd", hidden_low, down_all, preferred_element_type=jnp.float32
        )
        pre_low = gelu_pull(hidden_grad)[0].astype(jnp.bfloat16)
        micro_up = jnp.einsum(
            "rd,rf->df", gathered_two, pre_low, preferred_element_type=jnp.float32
        )
        normed_two_grad = lax.psum_scatter(
            jnp.einsum("rf,df->rd", pre_low, up_weight, preferred_element_type=jnp.float32),
            "mp",
            scatter_dimension=0,
            tiled=True,
        )
        outputs.append(middle + gate_mlp * mlp_out)
        grad_gate_mlp = grad_y * mlp_out
        resid_grad, grad_shift_mlp, grad_scale_mlp = pull_two(normed_two_grad)
        middle_grad = grad_y + resid_grad
        grad_gate_attn = middle_grad * attn_out
        out_in = (gate_attn * middle_grad).astype(jnp.bfloat16)
        out_all = lax.all_gather(out_in, "mp", axis=0, tiled=True)
        micro_out = jnp.einsum("rc,rd->cd", heads_out, out_all, preferred_element_type=jnp.float32)
        heads_grad = jnp.einsum(
            "rd,cd->rc", out_all, out_weight, preferred_element_type=jnp.float32
        ).astype(jnp.bfloat16)
        heads_grad = heads_grad.reshape(win_count, WIN, heads_here, HD)
        probs = jnp.exp(attention_scores(query_part, key_part, bias_full, masks) - log_total)
        probs_low = probs.astype(jnp.bfloat16)
        value_grad = jnp.einsum(
            "whqk,wqhd->wkhd", probs_low, heads_grad, preferred_element_type=jnp.float32
        )
        probs_grad = jnp.einsum(
            "wqhd,wkhd->whqk", heads_grad, value_part, preferred_element_type=jnp.float32
        )
        score_grad = probs * (probs_grad - jnp.sum(probs * probs_grad, axis=-1, keepdims=True))
        micro_rel = bias_pull(jnp.sum(score_grad, axis=0))[0]
        score_low = (score_grad * head_scale).astype(jnp.bfloat16)
        query_grad = jnp.einsum(
            "whqk,wkhd->wqhd", score_low, key_part, preferred_element_type=jnp.float32
        )
        key_grad = jnp.einsum(
            "whqk,wqhd->wkhd", score_low, query_part, preferred_element_type=jnp.float32
        )
        packed_grad = jnp.stack([query_grad, key_grad, value_grad], axis=3).astype(jnp.bfloat16)
        packed_grad = packed_grad.reshape(win_count * WIN, heads_here * 3 * HD)
        micro_qkv = jnp.einsum(
            "rd,rc->dc", gathered_one, packed_grad, preferred_element_type=jnp.float32
        )
        normed_one_grad = lax.psum_scatter(
            jnp.einsum("rc,dc->rd", packed_grad, qkv_weight, preferred_element_type=jnp.float32),
            "mp",
            scatter_dimension=0,
            tiled=True,
        )
        input_grad, grad_shift_attn, grad_scale_attn = pull_one(normed_one_grad)
        token_grads.append(middle_grad + input_grad)
        row_modes = jnp.concatenate(
            [
                grad_shift_attn,
                grad_scale_attn,
                grad_gate_attn,
                grad_shift_mlp,
                grad_scale_mlp,
                grad_gate_mlp,
            ],
            axis=1,
        )
        mode_parts.append(jnp.einsum("rw,re->we", spread_rows, row_modes, precision=precise))
        local_grads = (micro_qkv, micro_out, micro_rel, micro_up, micro_down)
        grad_qkv = grad_qkv + local_grads[0]
        grad_out = grad_out + local_grads[1]
        grad_rel = grad_rel + local_grads[2]
        grad_up = grad_up + local_grads[3]
        grad_down = grad_down + local_grads[4]
    mode_grad_cols = lax.psum_scatter(jnp.stack(mode_parts), "mp", scatter_dimension=2, tiled=True)
    mode_low = mode_grad_cols.astype(jnp.bfloat16)
    grad_ada = jnp.einsum("mwd,mwe->de", cond_low, mode_low, preferred_element_type=jnp.float32)
    grad_ada_bias = jnp.sum(mode_grad_cols, axis=(0, 1))
    cond_grad = jnp.einsum("mwe,de->mwd", mode_low, ada_weight, preferred_element_type=jnp.float32)
    cond_value, cond_pull = jax.vjp(partial(condition_whole, timesteps, classes), class_table)
    class_total = lax.psum(cond_pull(cond_grad)[0], ("dp", "mp"))
    grad_qkv, grad_out, grad_up, grad_down, grad_rel, grad_ada, grad_ada_bias = lax.psum(
        (grad_qkv, grad_out, grad_up, grad_down, grad_rel, grad_ada, grad_ada_bias), "dp"
    )
    return (
        jnp.stack(outputs).astype(jnp.bfloat16),
        jnp.stack(token_grads).astype(jnp.bfloat16),
        grad_qkv,
        grad_out,
        grad_up,
        grad_down,
        grad_ada,
        grad_ada_bias,
        grad_rel,
        class_total,
    )


def solution(mesh):
    n_dp, n_mp = mesh.shape["dp"], mesh.shape["mp"]

    def specs(*dp):
        rows = P(None, (*dp, "mp"), None)
        weights = (P(None, "mp"), P("mp", None), P(None, "mp"), P("mp", None), P(None, "mp"), P("mp"), P("mp", None), P())
        return (rows, rows, *weights, *[P(None, dp)] * 3), (rows, rows, *weights)

    def program(tokens, *arrays):
        if n_mp == 4 and n_dp % 2 == 0 and tokens.shape[1] == n_dp * n_mp * WIN:
            devices = mesh.devices.reshape(n_dp // 2, 2, n_mp)
            split = jax.sharding.Mesh(devices, ("z", "core", "mp"))
            ins, outs = specs("z", "core")
            step = jax.shard_map(
                partial(local_windows, (n_dp // 2, n_mp)), mesh=split, in_specs=ins, out_specs=outs, check_vma=False
            )
        else:
            ins, outs = specs("dp")
            step = jax.shard_map(local_general, mesh=mesh, in_specs=ins, out_specs=outs, check_vma=False)
        return step(tokens, *arrays)

    return program
```
